32 devices in a mesh: dp: 16 (over z, x, core), expert: 2 (over y).
Axes of the slice: x: 2, y: 2, z: 4, core: 2. Of those that a mesh axis runs over, the one named last changes fastest.
Arguments:
- tokens: bfloat16 [32, 1024, 384], P('dp', 'expert'), may hold values from -6 to 6
- lengths: int32 [32, 16], P('dp'), may hold values from 0 to 768, as said below
- routes: int32 [32, 1024, 2], P('dp', 'expert'), may hold values from 0 to 7, all different within a row; in each aligned block of 512 rows (0 to 511, 512 to 1023, ..., all dimensions but the last counted through in order) at most 192 rows name the same one
- cotangent: bfloat16 [32, 1024, 384], P('dp', 'expert'), may hold values from -6 to 6
- norm_one: float32 [384], replicated, may hold values from 0.5 to 1.5
- w_query: bfloat16 [384, 384], replicated, may hold values from -0.3125 to 0.3125
- w_key: bfloat16 [384, 384], replicated, may hold values from -0.3125 to 0.3125
- w_value: bfloat16 [384, 384], replicated, may hold values from -0.3125 to 0.3125
- w_out: bfloat16 [384, 384], replicated, may hold values from -1.25 to 1.25
- norm_two: float32 [384], replicated, may hold values from 0.5 to 1.5
- w_router: bfloat16 [384, 8], replicated, may hold values from -0.21875 to 0.21875
- w_gate: bfloat16 [8, 384, 512], P('expert'), may hold values from -0.3125 to 0.3125
- w_up: bfloat16 [8, 384, 512], P('expert'), may hold values from -0.3125 to 0.3125
- w_down: bfloat16 [8, 512, 384], P('expert'), may hold values from -0.5 to 0.5
Outputs:
- output: bfloat16 [32, 1024, 384], P('dp', 'expert')
- grad_tokens: float32 [32, 1024, 384], P('dp', 'expert')
- grad_norm_one: float32 [384], replicated
- grad_query: float32 [384, 384], replicated
- grad_key: float32 [384, 384], replicated
- grad_value: float32 [384, 384], replicated
- grad_out: float32 [384, 384], replicated
- grad_norm_two: float32 [384], replicated
- grad_router: float32 [384, 8], replicated
- grad_gate: float32 [8, 384, 512], P('expert')
- grad_up: float32 [8, 384, 512], P('expert')
- grad_down: float32 [8, 512, 384], P('expert')
The draws below stay inside these ranges and needn't reach their ends.
Inputs may be any that keep to these rules, and one draw needn't show every extreme that they name: Each row packs whole series in order from position 0; the first series of every row ends in the row's last 512 positions; a row's lengths sum to at most 1024, the rest being padding. `routes`: A token's two experts differ; within each aligned block of 512 positions of a row no expert is named more than 192 times.
All inputs are finite; a program needn't handle non-finite values.
Results may differ from the reference program's by a relative error of at most 0.023.
Values may be sent and summed in bfloat16 or wider, within the bound.
A program may use at most 192 MiB of HBM per device.

```python
import math
import jax
import jax.numpy as jnp
import numpy as np
from jax import lax

D = 384
HEADS = 6
HEAD_DIM = 64
HID = 512
EXPERTS = 8
ROW_LEN = 1024
NSER = 16
SEG = 512
ROWS = 32
CAP = 192
N_EXPERT = 2


def draw_lengths(key, part):
    key = jax.random.fold_in(key, 7)
    first_key, padding_key, short_key = jax.random.split(key, 3)
    longest = ROW_LEN - SEG // 2 - jax.random.randint(first_key, (ROWS,), 0, SEG // 2)
    longest = jnp.where(jnp.arange(ROWS) == 0, ROW_LEN - SEG // 2, longest)
    padding = jax.random.randint(padding_key, (ROWS,), 0, SEG // 4 + 1)
    remaining = ROW_LEN - longest - padding
    shorts = jax.random.randint(short_key, (ROWS, NSER - 1), 1, SEG)
    before = jnp.cumsum(shorts, axis=1) - shorts
    fitted = jnp.clip(remaining[:, None] - before, 0, shorts)
    return jnp.concatenate([longest[:, None], fitted], axis=1).astype(jnp.int32)


def shard_levels(key, dims, shards, smallest, largest):
    def one(axis_at, blocks):
        draws = jax.random.uniform(jax.random.fold_in(jax.random.fold_in(key, 6), axis_at), (blocks,), jnp.float32, smallest / len(shards), largest / len(shards))
        return jnp.repeat(jnp.exp(draws), dims[axis_at] // blocks).reshape((-1,) + (1,) * (len(dims) - axis_at - 1))

    factor_of = one(*shards[0])
    for cut in shards[1:]:
        factor_of = factor_of * one(*cut)
    return factor_of


def deal_out(rng, own, number, rows, amount, top, limit, skew):
    order = jax.random.permutation(rng, amount)
    crowded, ordinary = shares(amount, rows * top, limit, skew, True), shares(amount, rows * top, limit, skew, False)
    places = jnp.arange(amount)

    def named(sizes, turn):
        used = int((sizes > 0).sum())
        fixed = max(1, used // 4)
        passed = fixed + (places - fixed + turn * (used - fixed)) % max(1, amount - fixed)
        return jnp.zeros((amount,), jnp.int32).at[order[jnp.where(places < fixed, places, passed)]].set(jnp.asarray(sizes, jnp.int32))

    sizes = jnp.where(number % 4 == 0, named(crowded, number // 4), named(ordinary, number - number // 4 - 1))
    mixed = jax.random.permutation(jax.random.fold_in(own, 3), amount)
    donor, taker = mixed[0:amount // 2 * 2:2], mixed[1:amount // 2 * 2:2]
    room = jnp.minimum(sizes[donor] - 1, limit - sizes[taker]) // 2
    room = jnp.where((donor == order[0]) | (taker == order[0]) | (sizes[taker] == 0), 0, jnp.maximum(room, 0))
    passed = jax.random.randint(jax.random.fold_in(own, 4), (amount // 2,), 0, 1 << 20) % (room + 1)
    sizes = sizes.at[donor].add(-passed).at[taker].add(passed)
    items = jnp.searchsorted(jnp.cumsum(sizes), jnp.arange(rows * top), side="right").astype(jnp.int32)
    listing = items.reshape(top, rows).T
    listing = listing[jax.random.permutation(jax.random.fold_in(own, 1), rows)]
    turn = jax.random.randint(jax.random.fold_in(own, 2), (rows, 1), 0, top)
    return jnp.take_along_axis(listing, (jnp.arange(top)[None, :] + turn) % top, axis=1)


def shares(number_of, total, limit, slope, full):
    loads = [(1 << 20) // math.isqrt(rank ** slope) + 1 for rank in range(1, number_of + 1)]
    largest = limit if full else min(limit, max(-(-total // number_of), total * loads[0] // sum(loads)))
    least = 1 if total - largest >= number_of - 1 else 0
    given, rest = [largest] + [least] * (number_of - 1), total - largest - least * (number_of - 1)
    while rest > 0:
        candidates = [i for i in range(1, number_of) if given[i] < largest] or [i for i in range(1, number_of) if given[i] < limit]
        whole, left = sum([loads[i] for i in candidates]), rest
        for i in candidates:
            extra = min(limit - given[i], max(1, left * loads[i] // whole), rest)
            given[i] = given[i] + extra
            rest = rest - extra
    return np.array(given)


def noise(own_key, dims, width, bound, shards=(), held_as=jnp.bfloat16):
    drawn = width * jax.random.normal(own_key, dims, jnp.float32)
    if shards:
        drawn = drawn * shard_levels(own_key, dims, shards, -0.22, 0.18)
    return jnp.clip(drawn, -bound, bound).astype(held_as)


def setup_inputs(seed: int = 0) -> dict:
    keys = jax.random.split(jax.random.key(seed), 15)
    tokens = noise(keys[0], (ROWS, ROW_LEN, D), 1.0, 6.0, ((0, 16), (1, 2)))
    lengths = draw_lengths(jax.random.fold_in(keys[14], 71), 0)
    routes_keys = jax.random.split(jax.random.fold_in(keys[2], 1), ROWS * ROW_LEN // SEG)
    routes_turns = jax.random.permutation(jax.random.fold_in(keys[2], 3), ROWS * ROW_LEN // SEG)
    routes = jax.vmap(lambda own, number: deal_out(jax.random.fold_in(keys[2], 2), own, number, SEG, EXPERTS, 2, CAP, 2))(routes_keys, routes_turns).reshape((ROWS, ROW_LEN, 2))
    cotangent = noise(keys[3], (ROWS, ROW_LEN, D), 1.0, 6.0, ((0, 16), (1, 2)))
    norm_one = jnp.clip(1.0 + 0.1 * jax.random.normal(keys[4], (D,), jnp.float32), 0.5, 1.5)
    w_query = noise(keys[5], (D, D), D ** -0.5, 0.3125)
    w_key = noise(keys[6], (D, D), D ** -0.5, 0.3125)
    w_value = noise(keys[7], (D, D), D ** -0.5, 0.3125)
    w_out = noise(keys[8], (D, D), (D // 16) ** -0.5, 1.25)
    norm_two = jnp.clip(1.0 + 0.1 * jax.random.normal(keys[9], (D,), jnp.float32), 0.5, 1.5)
    w_router = noise(keys[10], (D, EXPERTS), (2 * D) ** -0.5, 0.21875)
    w_gate = noise(keys[11], (EXPERTS, D, HID), D ** -0.5, 0.3125, ((0, 2),))
    w_up = noise(keys[12], (EXPERTS, D, HID), D ** -0.5, 0.3125, ((0, 2),))
    w_down = noise(keys[13], (EXPERTS, HID, D), (HID // 4) ** -0.5, 0.5, ((0, 2),))
    return {"tokens": tokens, "lengths": lengths, "routes": routes, "cotangent": cotangent, "norm_one": norm_one, "w_query": w_query, "w_key": w_key, "w_value": w_value, "w_out": w_out, "norm_two": norm_two, "w_router": w_router, "w_gate": w_gate, "w_up": w_up, "w_down": w_down}


epsilon = 1e-06
masked_out = -1e+30
highest = lax.Precision.HIGHEST

@jax.custom_vjp
def low(v):
    return lax.optimization_barrier(v.astype(jnp.bfloat16)).astype(jnp.float32)

@jax.custom_vjp
def low_back(v):
    return v

def low_keep(v):
    return (low(v), None)

def low_pass(kept, grad):
    return (grad,)

def back_keep(v):
    return (v, None)

def back_low(kept, grad):
    return (low(grad),)
low.defvjp(low_keep, low_pass)
low_back.defvjp(back_keep, back_low)

def series_info(lengths, place):
    ends = jnp.cumsum(lengths, axis=-1).astype(jnp.int32)
    starts = jnp.concatenate([ends - lengths, ends[:, -1:]], axis=-1).astype(jnp.int32)
    series = lax.optimization_barrier(jnp.sum((ends[:, None, :] <= place[:, :, None]).astype(jnp.int32), axis=-1)).astype(jnp.int32)
    labels = jnp.arange(starts.shape[1], dtype=jnp.int32)
    opening = lax.optimization_barrier(jnp.sum(jnp.where(series[:, :, None] == labels, starts[:, None, :], 0), axis=-1)).astype(jnp.int32)
    return (series, place - opening)

def rotate(values, offset):
    half = values.shape[-1] // 2
    inverse = jnp.exp(jnp.arange(half, dtype=jnp.float32) * (-2.0 * math.log(10000.0) / values.shape[-1]))
    angle = offset.astype(jnp.float32)[..., None, None] * inverse
    cosine, sine = (jnp.cos(angle), jnp.sin(angle))
    former, latter = (values[..., :half], values[..., half:])
    return jnp.concatenate([former * cosine - latter * sine, latter * cosine + former * sine], axis=-1)

def rms_norm(values, gain):
    return values * lax.rsqrt(lax.optimization_barrier(jnp.mean(values * values, axis=-1, keepdims=True)) + epsilon) * gain

def attend_row(packed):
    query, key, value, series, place = packed
    score = jnp.einsum('qhd,khd->hqk', query, key, precision=highest) * HEAD_DIM ** (-0.5)
    score = low_back(score)
    allowed = (series[:, None] == series[None, :]) & (place[None, :] <= place[:, None])
    score = jnp.where(allowed[None], score, masked_out)
    peak = lax.optimization_barrier(jnp.max(score, axis=-1, keepdims=True))
    weight = jnp.exp(score - peak)
    weight = weight / lax.optimization_barrier(jnp.sum(weight, axis=-1, keepdims=True))
    weight = low(weight)
    return jnp.einsum('hqk,khd->qhd', weight, value, precision=highest)

def dispatch_table(route_row):
    pairs = route_row.reshape(N_EXPERT, SEG * 2)
    hits = (pairs[..., None] == jnp.arange(EXPERTS, dtype=jnp.int32)).astype(jnp.int32)
    rank = lax.optimization_barrier(jnp.sum(hits * (jnp.cumsum(hits, axis=1) - 1), axis=-1)).astype(jnp.int32)
    target = pairs * CAP + rank
    table = (target[..., None] == jnp.arange(EXPERTS * CAP, dtype=jnp.int32)) & (rank < CAP)[..., None]
    return table.reshape(N_EXPERT, SEG, 2, EXPERTS * CAP).astype(jnp.float32)

def dispatch_row(packed):
    route_row, second_row = packed
    table = dispatch_table(route_row)
    return jnp.einsum('jscx,jsd->jxd', table, second_row.reshape(N_EXPERT, SEG, D), precision=highest)

def combine_row(packed):
    route_row, made_row, gate_row = packed
    table = dispatch_table(route_row)
    picked = jnp.einsum('jscx,jxd->jscd', table, made_row, precision=highest)
    mixture = jnp.einsum('jsc,jscd->jsd', gate_row.reshape(N_EXPERT, SEG, 2), picked, precision=highest)
    return mixture.reshape(ROW_LEN, D)

def expert_apply(packed):
    routed, gate_weight, up_weight, down_weight = packed
    gate_pre = low_back(jnp.dot(routed, gate_weight, precision=highest))
    up_pre = low_back(jnp.dot(routed, up_weight, precision=highest))
    hidden = low(jax.nn.silu(gate_pre) * up_pre)
    return low(low_back(jnp.dot(hidden, down_weight, precision=highest)))

def forward(series, offset, place, routes, inputs, norm_one, w_query, w_key, w_value, w_out, norm_two, w_router, w_gate, w_up, w_down):
    first = low(rms_norm(inputs, norm_one))

    def project(weight):
        return jnp.einsum('rld,de->rle', first, weight, precision=highest).reshape(ROWS, ROW_LEN, HEADS, HEAD_DIM)
    query = low(rotate(low_back(project(w_query)), offset))
    key = low(rotate(low_back(project(w_key)), offset))
    value = low(low_back(project(w_value)))
    attended = lax.map(jax.checkpoint(attend_row), (query, key, value, series, place))
    mixed = low(low_back(attended.reshape(ROWS, ROW_LEN, D)))
    attention = low_back(jnp.einsum('rld,de->rle', mixed, w_out, precision=highest))
    residual = inputs + attention
    second = low(rms_norm(residual, norm_two))
    logits = low_back(jnp.einsum('rld,de->rle', second, w_router, precision=highest))
    chosen = jnp.take_along_axis(logits, routes, axis=-1)
    gates = jax.nn.softmax(chosen, axis=-1)
    sent = lax.map(jax.checkpoint(dispatch_row), (routes, second))
    sent = sent.reshape(ROWS, N_EXPERT, EXPERTS, CAP, D).transpose(2, 0, 1, 3, 4).reshape(EXPERTS, ROWS * N_EXPERT * CAP, D)
    sent = low_back(sent)
    made = lax.map(jax.checkpoint(expert_apply), (sent, w_gate, w_up, w_down))
    made = made.reshape(EXPERTS, ROWS, N_EXPERT, CAP, D).transpose(1, 2, 0, 3, 4).reshape(ROWS, N_EXPERT, EXPERTS * CAP, D)
    mixture = lax.map(jax.checkpoint(combine_row), (routes, made, gates))
    return residual + mixture

def reference(tokens, lengths, routes, cotangent, norm_one, w_query, w_key, w_value, w_out, norm_two, w_router, w_gate, w_up, w_down):
    place = jnp.broadcast_to(jnp.arange(ROW_LEN, dtype=jnp.int32), (ROWS, ROW_LEN))
    series, offset = series_info(lengths, place)
    floats = tuple((item.astype(jnp.float32) for item in (tokens, norm_one, w_query, w_key, w_value, w_out, norm_two, w_router, w_gate, w_up, w_down)))

    def wrapped(*items):
        return forward(series, offset, place, routes, *items)
    result, pullback = jax.vjp(wrapped, *floats)
    grads = pullback(cotangent.astype(jnp.float32))
    return (result.astype(jnp.bfloat16), grads[0], grads[1], grads[2], grads[3], grads[4], grads[5], grads[6], grads[7], grads[8], grads[9], grads[10])
```

```python
import functools
import math

import jax
import jax.numpy as jnp
from jax import lax
from jax.experimental import pallas as pl
from jax.experimental.pallas import tpu as pltpu
from jax.sharding import PartitionSpec as P

HEAD_DIM = 64
PAIR = 128
epsilon = 1e-06
masked_out = -1e30
f32 = jnp.float32
bf16 = jnp.bfloat16
LIMIT = 56 * 1024 * 1024


def nn(a, b):
    return lax.dot_general(a, b, (((1,), (0,)), ((), ())), preferred_element_type=f32)


def nt(a, b):
    return lax.dot_general(a, b, (((1,), (1,)), ((), ())), preferred_element_type=f32)


def tn(a, b):
    return lax.dot_general(a, b, (((0,), (0,)), ((), ())), preferred_element_type=f32)


def rms_factor(values):
    return lax.rsqrt(jnp.mean(values * values, axis=-1, keepdims=True) + epsilon)


def swap_halves(values):
    lane = lax.broadcasted_iota(jnp.int32, values.shape, 1) % HEAD_DIM
    return jnp.where(
        lane < HEAD_DIM // 2,
        pltpu.roll(values, PAIR - HEAD_DIM // 2, 1),
        pltpu.roll(values, HEAD_DIM // 2, 1),
    )


def rope(values, cosine, sine):
    return values * cosine + swap_halves(values) * sine


def rope_back(values, cosine, sine):
    return values * cosine - swap_halves(values) * sine


def one_head(values, which):
    lane = lax.broadcasted_iota(jnp.int32, values.shape, 1) // HEAD_DIM
    return jnp.where(lane == which, values, jnp.zeros_like(values))


def score_bias(keys, block, size, series_col, series_row):
    k_place = lax.broadcasted_iota(jnp.int32, (keys, size), 0)
    q_place = lax.broadcasted_iota(jnp.int32, (keys, size), 1) + block * size
    allowed = (series_col == series_row) & (k_place <= q_place)
    return jnp.where(allowed, 0.0, masked_out)


def project(rows, x_ref, cos_ref, sin_ref, norm_ref, w_ref, first_ref, q_ref, k_ref, v_ref):
    width = x_ref.shape[-1]
    x = x_ref[rows, :].astype(f32)
    first = (x * rms_factor(x) * norm_ref[...]).astype(bf16)
    first_ref[rows, :] = first
    cosine, sine = cos_ref[rows, :], sin_ref[rows, :]
    raw = nn(first, w_ref[...])
    for pair in range(width // PAIR):
        cut = pl.ds(pair * PAIR, PAIR)
        q = raw[:, pair * PAIR : (pair + 1) * PAIR]
        k = raw[:, width + pair * PAIR : width + (pair + 1) * PAIR]
        q_ref[rows, cut] = rope(q, cosine, sine).astype(bf16) * HEAD_DIM ** (-0.5)
        k_ref[rows, cut] = rope(k, cosine, sine).astype(bf16)
    v_ref[rows, :] = raw[:, 2 * width :].astype(bf16)


def attend(block, size, plain, series_col_ref, series_row_ref, q_ref, k_ref, vt_ref, mixed_ref, lse_ref, p_ref):
    width = q_ref.shape[-1]
    keys = (block + 1) * size
    rows = pl.ds(block * size, size)
    low = keys - size if plain else 0
    k_place = lax.broadcasted_iota(jnp.int32, (keys - low, size), 0) + low
    q_place = lax.broadcasted_iota(jnp.int32, (keys - low, size), 1) + block * size
    allowed = k_place <= q_place
    if not plain:
        allowed = allowed & (series_col_ref[:keys, :] == series_row_ref[:, block * size : keys])
    bias = jnp.where(allowed, 0.0, masked_out)
    for pair in range(width // PAIR):
        cut = pl.ds(pair * PAIR, PAIR)
        q = q_ref[rows, cut]
        outs = []
        for half in range(2):
            q_head = one_head(q, half)
            parts = []
            for at in range(0, keys, size):
                s = nt(k_ref[at : at + size, cut], q_head)
                if at >= low:
                    s = s + bias[at - low : at - low + size]
                parts.append(s)
            peak = functools.reduce(jnp.maximum, [jnp.max(s, axis=0, keepdims=True) for s in parts])
            total = jnp.zeros((1, size), f32)
            for n, s in enumerate(parts):
                e = jnp.exp(s - peak)
                total = total + jnp.sum(e, axis=0, keepdims=True)
                p_ref[half, n * size : (n + 1) * size, :] = e.astype(bf16)
            head = pair * 2 + half
            lse_ref[pl.ds(head, 1), rows] = peak + jnp.log(total)
            o = nn(vt_ref[pl.ds(head * HEAD_DIM, HEAD_DIM), :keys], p_ref[half, :keys, :])
            outs.append(o * (1.0 / total))
        mixed_ref[rows, cut] = jnp.concatenate(outs, axis=0).T.astype(bf16)


def forward_kernel(seg, size, x_ref, cos_ref, sin_ref, sc_ref, sr_ref, g1_ref, w_ref, wo_ref, g2_ref,
                   first_ref, q_ref, k_ref, v_ref, lse_ref, mixed_ref, res_ref, second_ref, vt_ref, p_ref):
    length = x_ref.shape[0]
    for block in range(length // size):
        rows = pl.ds(block * size, size)
        project(rows, x_ref, cos_ref, sin_ref, g1_ref, w_ref, first_ref, q_ref, k_ref, v_ref)
        vt_ref[:, rows] = v_ref[rows, :].T
    for block in range(length // size):
        rows = pl.ds(block * size, size)
        plain = (block + 1) * size <= length - seg
        attend(block, size, plain, sc_ref, sr_ref, q_ref, k_ref, vt_ref, mixed_ref, lse_ref, p_ref)
        residual = x_ref[rows, :].astype(f32) + nn(mixed_ref[rows, :], wo_ref[...])
        res_ref[rows, :] = residual
        second_ref[rows, :] = (residual * rms_factor(residual) * g2_ref[...]).astype(bf16)


def route_rows(routes, second, w_router_t, upper):
    logits = nt(w_router_t, second)
    expert = lax.broadcasted_iota(jnp.int32, logits.shape, 0)
    hit0, hit1 = expert == routes[0:1, :], expert == routes[1:2, :]
    l0 = jnp.sum(jnp.where(hit0, logits, 0.0), axis=0, keepdims=True)
    l1 = jnp.sum(jnp.where(hit1, logits, 0.0), axis=0, keepdims=True)
    peak = jnp.maximum(l0, l1)
    e0, e1 = jnp.exp(l0 - peak), jnp.exp(l1 - peak)
    scale = 1.0 / (e0 + e1)
    gates = jnp.where(hit0, e0 * scale, 0.0) + jnp.where(hit1, e1 * scale, 0.0)
    hit = hit0 | hit1
    rank = nn(hit.astype(bf16), upper)
    return jnp.where(hit, rank, -1.0).astype(jnp.int32), gates


def expert_kernel(ways, cap, routes_ref, second_ref, cot_ref, wrt_ref, upper_ref, wgu_ref, wd_ref,
                  mix_ref, gsec_ref, gg_ref, dgu_ref, dd_ref,
                  slot_ref, gate_ref, t_ref, both_ref, sent_ref, cots_ref, gslot_ref, y_ref, ggc_ref):
    step = pl.program_id(0)
    length, width = second_ref.shape[1], second_ref.shape[2]
    local, hid = wd_ref.shape[0], wd_ref.shape[1]
    seg = length // ways
    base = lax.axis_index("expert") * local

    @pl.when(step == 0)
    def _():
        dgu_ref[...] = jnp.zeros_like(dgu_ref)
        dd_ref[...] = jnp.zeros_like(dd_ref)

    for n in range(ways):
        rows = pl.ds(n * seg, seg)
        second = second_ref[0, rows, :]
        slots, gates = route_rows(routes_ref[0, :, rows], second, wrt_ref[...], upper_ref[...])
        slot_ref[...] = slots
        gate_ref[...] = gates
        both_ref[:, :width] = second
        both_ref[:, width:] = cot_ref[0, rows, :]
        for e in range(local):
            mine = lax.broadcasted_iota(jnp.int32, (cap, seg), 0) == slot_ref[pl.ds(base + e, 1), :]
            t_ref[n, e * cap : (e + 1) * cap, :] = jnp.where(mine, 1.0, 0.0).astype(bf16)
            gslot_ref[e, n * cap : (n + 1) * cap, :] = jnp.sum(
                jnp.where(mine, gate_ref[pl.ds(base + e, 1), :], 0.0), axis=1, keepdims=True
            )
        taken = nn(t_ref[n], both_ref[...]).astype(bf16)
        for e in range(local):
            sent_ref[e, n * cap : (n + 1) * cap, :] = taken[e * cap : (e + 1) * cap, :width]
            cots_ref[e, n * cap : (n + 1) * cap, :] = taken[e * cap : (e + 1) * cap, width:]

    for e in range(local):
        sent = sent_ref[e]
        cot = cots_ref[e].astype(f32)
        gate = gslot_ref[e]
        pre = nn(sent, wgu_ref[e])
        gate_pre, up_pre = pre[:, :hid], pre[:, hid:]
        sigma = jax.nn.sigmoid(gate_pre)
        active = gate_pre * sigma
        hidden = (active * up_pre).astype(bf16)
        made = nn(hidden, wd_ref[e]).astype(bf16).astype(f32)
        gmade = (gate * cot).astype(bf16)
        ghid = nt(gmade, wd_ref[e])
        slope = sigma * (1.0 + gate_pre * (1.0 - sigma))
        dgate = (ghid * up_pre * slope).astype(bf16)
        dup = (ghid * active).astype(bf16)
        gsent = (nt(dgate, wgu_ref[e, :, :hid]) + nt(dup, wgu_ref[e, :, hid:])).astype(bf16)
        dgu_ref[e, :, :hid] += tn(sent, dgate)
        dgu_ref[e, :, hid:] += tn(sent, dup)
        dd_ref[e] += tn(hidden, gmade)
        gg = jnp.sum(made * cot, axis=1, keepdims=True)
        weighted = (gate * made).astype(bf16)
        for n in range(ways):
            y_ref[n, e * cap : (e + 1) * cap, :width] = weighted[n * cap : (n + 1) * cap]
            y_ref[n, e * cap : (e + 1) * cap, width:] = gsent[n * cap : (n + 1) * cap]
            ggc_ref[n, e * cap : (e + 1) * cap, :] = gg[n * cap : (n + 1) * cap]

    for n in range(ways):
        rows = pl.ds(n * seg, seg)
        back = tn(t_ref[n], y_ref[n])
        mix_ref[0, rows, :] = back[:, :width].astype(bf16)
        gsec_ref[0, rows, :] = back[:, width:].astype(bf16)
        for e in range(local):
            cut = pl.ds(e * cap, cap)
            gg_ref[0, e : e + 1, rows] = jnp.sum(
                t_ref[n, cut, :].astype(f32) * ggc_ref[n, cut, :], axis=0, keepdims=True
            )


def through_router(rows, routes_ref, second_ref, gg_ref, gates_from, gsec_ref, wrt_ref):
    second = second_ref[rows, :]
    routes = routes_ref[:, rows]
    logits = nt(wrt_ref[...], second)
    expert = lax.broadcasted_iota(jnp.int32, logits.shape, 0)
    hit0, hit1 = expert == routes[0:1, :], expert == routes[1:2, :]
    l0 = jnp.sum(jnp.where(hit0, logits, 0.0), axis=0, keepdims=True)
    l1 = jnp.sum(jnp.where(hit1, logits, 0.0), axis=0, keepdims=True)
    peak = jnp.maximum(l0, l1)
    e0, e1 = jnp.exp(l0 - peak), jnp.exp(l1 - peak)
    scale = 1.0 / (e0 + e1)
    g0, g1 = e0 * scale, e1 * scale
    gg = gg_ref[:, rows]
    gg0 = jnp.sum(jnp.where(hit0, gg, 0.0), axis=0, keepdims=True)
    gg1 = jnp.sum(jnp.where(hit1, gg, 0.0), axis=0, keepdims=True)
    inner = g0 * gg0 + g1 * gg1
    glog = jnp.where(hit0, g0 * (gg0 - inner), 0.0) + jnp.where(hit1, g1 * (gg1 - inner), 0.0)
    glog = glog.astype(bf16)
    gsec = functools.reduce(lambda a, b: a + b, [gsec_ref[n, rows, :].astype(f32) for n in range(gsec_ref.shape[0])])
    return glog, gsec + tn(glog, wrt_ref[...])


def backward_kernel(seg, size, routes_ref, gg_ref, gsec_ref, cot_ref, x_ref, cos_ref, sin_ref, sc_ref, sr_ref,
                    g1_ref, w_ref, wo_ref, g2_ref, wrt_ref, first_ref, q_ref, k_ref, v_ref, lse_ref, mixed_ref,
                    res_ref, second_ref,
                    gtok_ref, gn1_ref, gw_ref, gout_ref, gn2_ref, grt_ref,
                    gres_ref, ga_ref, gm_ref, delta_ref, dk_ref, dv_ref, graw_ref, p_ref, ds_ref):
    length, width = x_ref.shape
    heads = width // HEAD_DIM
    blocks = length // size
    indicator = (
        lax.broadcasted_iota(jnp.int32, (8, width), 1) // HEAD_DIM
        == lax.broadcasted_iota(jnp.int32, (8, width), 0)
    ).astype(bf16)
    gn2 = jnp.zeros((1, width), f32)
    grt = jnp.zeros(grt_ref.shape, f32)
    for block in range(blocks):
        rows = pl.ds(block * size, size)
        glog, gsec = through_router(rows, routes_ref, second_ref, gg_ref, None, gsec_ref, wrt_ref)
        grt = grt + nn(glog, second_ref[rows, :])
        residual = res_ref[rows, :]
        factor = rms_factor(residual)
        unit = residual * factor
        weighted = gsec * g2_ref[...]
        inner = jnp.mean(weighted * unit, axis=-1, keepdims=True)
        gn2 = gn2 + jnp.sum(gsec * unit, axis=0, keepdims=True)
        gres = cot_ref[rows, :].astype(f32) + factor * (weighted - unit * inner)
        gres_ref[rows, :] = gres
        ga = gres.astype(bf16)
        ga_ref[rows, :] = ga
        gm = nt(ga, wo_ref[...]).astype(bf16)
        gm_ref[rows, :] = gm
        prod = gm.astype(f32) * mixed_ref[rows, :].astype(f32)
        high = prod.astype(bf16)
        rest = (prod - high.astype(f32)).astype(bf16)
        delta_ref[:, rows] = nt(indicator, high) + nt(indicator, rest)
    gn2_ref[...] = gn2
    grt_ref[...] = grt
    gout_ref[...] = tn(mixed_ref[...], ga_ref[...])
    dk_ref[...] = jnp.zeros_like(dk_ref)
    dv_ref[...] = jnp.zeros_like(dv_ref)
    for block in range(blocks):
        rows = pl.ds(block * size, size)
        keys = (block + 1) * size
        plain = keys <= length - seg
        low = keys - size if plain else 0
        k_place = lax.broadcasted_iota(jnp.int32, (keys - low, size), 0) + low
        q_place = lax.broadcasted_iota(jnp.int32, (keys - low, size), 1) + block * size
        allowed = k_place <= q_place
        if not plain:
            allowed = allowed & (sc_ref[:keys, :] == sr_ref[:, block * size : keys])
        bias = jnp.where(allowed, 0.0, masked_out)
        for pair in range(width // PAIR):
            cut = pl.ds(pair * PAIR, PAIR)
            q, gm = q_ref[rows, cut], gm_ref[rows, cut]
            dq = []
            for half in range(2):
                head = pair * 2 + half
                q_head, gm_head = one_head(q, half), one_head(gm, half)
                lse = lse_ref[pl.ds(head, 1), rows]
                delta = delta_ref[pl.ds(head, 1), rows]
                for at in range(0, keys, size):
                    cols = pl.ds(at, size)
                    s = nt(k_ref[cols, cut], q_head)
                    if at >= low:
                        s = s + bias[at - low : at - low + size]
                    p = jnp.exp(s - lse)
                    dp = nt(v_ref[cols, cut], gm_head)
                    p_ref[half, cols, :] = p.astype(bf16)
                    ds_ref[half, cols, :] = (p * (dp - delta)).astype(bf16)
                dq.append(tn(ds_ref[half, :keys, :], k_ref[:keys, cut]))
            both = jnp.concatenate([one_head(gm, 0), one_head(gm, 1)], axis=0)
            dv_ref[:keys, cut] += nn(p_ref[0, :keys, :], one_head(gm, 0)) + nn(p_ref[1, :keys, :], one_head(gm, 1))
            dk_ref[:keys, cut] += nn(ds_ref[0, :keys, :], one_head(q, 0)) + nn(ds_ref[1, :keys, :], one_head(q, 1))
            lane = lax.broadcasted_iota(jnp.int32, (size, PAIR), 1)
            dq = jnp.where(lane < HEAD_DIM, dq[0], dq[1]) * HEAD_DIM ** (-0.5)
            graw_ref[rows, cut] = rope_back(dq, cos_ref[rows, :], sin_ref[rows, :]).astype(bf16)
    for block in range(blocks):
        rows = pl.ds(block * size, size)
        cosine, sine = cos_ref[rows, :], sin_ref[rows, :]
        for pair in range(width // PAIR):
            dk = dk_ref[rows, pl.ds(pair * PAIR, PAIR)]
            graw_ref[rows, pl.ds(width + pair * PAIR, PAIR)] = rope_back(dk, cosine, sine).astype(bf16)
        graw_ref[rows, pl.ds(2 * width, width)] = dv_ref[rows, :].astype(bf16)
    gn1 = jnp.zeros((1, width), f32)
    for block in range(blocks):
        rows = pl.ds(block * size, size)
        gfirst = nt(graw_ref[rows, :], w_ref[...])
        x = x_ref[rows, :].astype(f32)
        factor = rms_factor(x)
        unit = x * factor
        weighted = gfirst * g1_ref[...]
        inner = jnp.mean(weighted * unit, axis=-1, keepdims=True)
        gn1 = gn1 + jnp.sum(gfirst * unit, axis=0, keepdims=True)
        gtok_ref[rows, :] = (gres_ref[rows, :] + factor * (weighted - unit * inner)).astype(bf16)
    gn1_ref[...] = gn1
    gw_ref[...] = tn(first_ref[...], graw_ref[...])


def vmem(count):
    return [pl.BlockSpec(memory_space=pltpu.VMEM)] * count


def series_info(lengths, row_len):
    place = jnp.arange(row_len, dtype=jnp.int32)
    ends = jnp.cumsum(lengths, axis=-1)
    starts = jnp.concatenate([ends - lengths, ends[:, -1:]], axis=-1)
    series = jnp.sum((ends[:, None, :] <= place[None, :, None]).astype(jnp.int32), axis=-1)
    labels = jnp.arange(starts.shape[1], dtype=jnp.int32)
    opening = jnp.sum(jnp.where(series[:, :, None] == labels, starts[:, None, :], 0), axis=-1)
    return series, place[None, :] - opening


def body(tokens, lengths, routes, cotangent, norm_one, w_query, w_key, w_value, w_out, norm_two, w_router, w_gate, w_up, w_down):
    rows, seg, width = tokens.shape
    ways = lax.axis_size("expert")
    mine = lax.axis_index("expert")
    row_len = seg * ways
    local, hid = w_gate.shape[0], w_gate.shape[2]
    experts = local * ways
    cap = -(-max(2, 3 * seg // experts) // 16) * 16
    size = 256
    own = rows // ways

    x_rows = lax.all_to_all(tokens, "expert", split_axis=0, concat_axis=1, tiled=True)
    cot_all = lax.all_gather(cotangent, "expert", axis=1, tiled=True)
    routes_t = lax.all_gather(routes, "expert", axis=1, tiled=True).transpose(0, 2, 1)
    own_lengths = lax.dynamic_slice_in_dim(lengths, mine * own, own, 0)
    series, offset = series_info(own_lengths, row_len)
    half = HEAD_DIM // 2
    inverse = jnp.exp(jnp.arange(half, dtype=f32) * (-2.0 * math.log(10000.0) / HEAD_DIM))
    angle = offset.astype(f32)[..., None] * inverse
    cosine, sine = jnp.cos(angle), jnp.sin(angle)
    cosine = jnp.concatenate([cosine] * 4, axis=-1)
    sine = jnp.concatenate([-sine, sine, -sine, sine], axis=-1)
    w_all = jnp.concatenate([w_query, w_key, w_value], axis=1)
    wgu = jnp.concatenate([w_gate, w_up], axis=2)
    w_router_t = w_router.T
    g1, g2 = norm_one[None, :], norm_two[None, :]
    params = pltpu.CompilerParams(vmem_limit_bytes=LIMIT)

    def shape(*dims, dtype=bf16):
        return jax.ShapeDtypeStruct(dims, dtype)

    def forward(x, cosine, sine, series):
        return pl.pallas_call(
            functools.partial(forward_kernel, seg, size),
            out_shape=[shape(row_len, width)] * 4 + [shape(8, row_len, dtype=f32), shape(row_len, width), shape(row_len, width, dtype=f32), shape(row_len, width)],
            in_specs=vmem(9), out_specs=vmem(8),
            scratch_shapes=[pltpu.VMEM((width, row_len), bf16), pltpu.VMEM((2, row_len, size), bf16)],
            compiler_params=params, name="attend_forward",
        )(x, cosine, sine, series[:, None], series[None, :], g1, w_all, w_out, g2)

    saved = [forward(x_rows[r], cosine[r], sine[r], series[r]) for r in range(own)]
    second = jnp.stack([s[7] for s in saved])
    second_all = lax.all_gather(second, "expert", axis=0, tiled=True)
    upper = (jnp.arange(seg)[:, None] < jnp.arange(seg)[None, :]).astype(bf16)

    slots = local * cap
    per = ways * cap

    def row(*dims):
        return pl.BlockSpec((1,) + dims, lambda i: (i,) + (0,) * len(dims))

    def whole(*dims):
        return pl.BlockSpec(dims, lambda i: (0,) * len(dims))

    mix, gsec, gg, dgu, dd = pl.pallas_call(
        functools.partial(expert_kernel, ways, cap),
        grid=(rows,),
        out_shape=[shape(rows, row_len, width), shape(rows, row_len, width), shape(rows, local, row_len, dtype=f32),
                   shape(local, width, 2 * hid, dtype=f32), shape(local, hid, width, dtype=f32)],
        in_specs=[row(2, row_len), row(row_len, width), row(row_len, width), whole(experts, width), whole(seg, seg),
                  whole(local, width, 2 * hid), whole(local, hid, width)],
        out_specs=[row(row_len, width), row(row_len, width), row(local, row_len), whole(local, width, 2 * hid), whole(local, hid, width)],
        scratch_shapes=[pltpu.VMEM((experts, seg), jnp.int32), pltpu.VMEM((experts, seg), f32),
                        pltpu.VMEM((ways, slots, seg), bf16), pltpu.VMEM((seg, 2 * width), bf16),
                        pltpu.VMEM((local, per, width), bf16), pltpu.VMEM((local, per, width), bf16),
                        pltpu.VMEM((local, per, 1), f32), pltpu.VMEM((ways, slots, 2 * width), bf16),
                        pltpu.VMEM((ways, slots, 1), f32)],
        compiler_params=params, name="experts",
    )(routes_t, second_all, cot_all, w_router_t, upper, wgu, w_down)

    def home(item):
        return lax.all_to_all(item.reshape((ways, own) + item.shape[1:]), "expert", split_axis=0, concat_axis=0, tiled=True)

    mix_parts, gsec_parts, gg_parts = home(mix), home(gsec), home(gg)
    gg_all = gg_parts.transpose(1, 0, 2, 3).reshape(own, experts, row_len)
    cot_own = lax.dynamic_slice_in_dim(cot_all, mine * own, own, 0)
    routes_own = lax.dynamic_slice_in_dim(routes_t, mine * own, own, 0)

    def backward(r):
        first, q, k, v, lse, mixed, res, sec = saved[r]
        big = (row_len, width)
        return pl.pallas_call(
            functools.partial(backward_kernel, seg, size),
            out_shape=[shape(*big), shape(1, width, dtype=f32), shape(width, 3 * width, dtype=f32), shape(width, width, dtype=f32),
                       shape(1, width, dtype=f32), shape(experts, width, dtype=f32)],
            in_specs=vmem(22), out_specs=vmem(6),
            scratch_shapes=[pltpu.VMEM(big, f32), pltpu.VMEM(big, bf16), pltpu.VMEM(big, bf16), pltpu.VMEM((8, row_len), f32),
                            pltpu.VMEM(big, f32), pltpu.VMEM(big, f32), pltpu.VMEM((row_len, 3 * width), bf16),
                            pltpu.VMEM((2, row_len, size), bf16), pltpu.VMEM((2, row_len, size), bf16)],
            compiler_params=params, name="attend_backward",
        )(routes_own[r], gg_all[r], gsec_parts[:, r], cot_own[r], x_rows[r], cosine[r], sine[r], series[r][:, None], series[r][None, :],
          g1, w_all, w_out, g2, w_router_t, first, q, k, v, lse, mixed, res, sec)

    grads = [backward(r) for r in range(own)]
    out_rows = jnp.stack([s[6] for s in saved]) + jnp.sum(mix_parts.astype(f32), axis=0)
    gtok = jnp.stack([g[0] for g in grads])

    def to_places(item):
        return lax.all_to_all(item, "expert", split_axis=1, concat_axis=0, tiled=True)

    output = to_places(out_rows.astype(bf16))
    grad_tokens = to_places(gtok).astype(f32)
    sums = [functools.reduce(lambda a, b: a + b, [g[n] for g in grads]) for n in range(1, 6)]
    gn1, gw, gout, gn2, grt = lax.psum(tuple(sums), ("dp", "expert"))
    dgu, dd = lax.psum((dgu.astype(bf16), dd.astype(bf16)), "dp")
    dgu, dd = dgu.astype(f32), dd.astype(f32)
    return (output, grad_tokens, gn1[0], gw[:, :width], gw[:, width : 2 * width], gw[:, 2 * width :], gout, gn2[0], grt.T,
            dgu[:, :, :hid], dgu[:, :, hid:], dd)


def solution(mesh):
    split, copied = P("dp", "expert", None), P()
    per_expert = P("expert", None, None)
    return jax.shard_map(
        body,
        mesh=mesh,
        in_specs=(split, P("dp", None), split, split) + (copied,) * 7 + (per_expert,) * 3,
        out_specs=(split, split) + (copied,) * 7 + (per_expert,) * 3,
        check_vma=False,
    )
```

```python
import functools
import math

import jax
import jax.numpy as jnp
import numpy as np
from jax import lax
from jax.experimental import pallas as pl
from jax.experimental.pallas import tpu as pltpu
from jax.sharding import PartitionSpec as P

HEAD_DIM = 64
PAIR = 128
epsilon = 1e-06
masked_out = -1e30
f32 = jnp.float32
bf16 = jnp.bfloat16
i32 = jnp.int32
MESH = pl.DeviceIdType.MESH
LIMIT = 63 * 1024 * 1024


def nn(a, b):
    return lax.dot_general(a, b, (((1,), (0,)), ((), ())), preferred_element_type=f32)


def nt(a, b):
    return lax.dot_general(a, b, (((1,), (1,)), ((), ())), preferred_element_type=f32)


def tn(a, b):
    return lax.dot_general(a, b, (((0,), (0,)), ((), ())), preferred_element_type=f32)


def iota(shape, dim):
    return lax.broadcasted_iota(i32, shape, dim)


def aligned(start, size, unit):
    return pl.ds(pl.multiple_of(start, unit), size)


def rms_factor(values):
    return lax.rsqrt(jnp.mean(values * values, axis=-1, keepdims=True) + epsilon)


def norm_back(values, gain, grads):
    factor = rms_factor(values)
    unit = values * factor
    weighted = grads * gain
    inner = jnp.mean(weighted * unit, axis=-1, keepdims=True)
    return factor * (weighted - unit * inner), jnp.sum(grads * unit, axis=0, keepdims=True)


def swap_halves(values):
    half = HEAD_DIM // 2
    lane = iota(values.shape, 1) % HEAD_DIM
    return jnp.where(lane < half, pltpu.roll(values, PAIR - half, 1), pltpu.roll(values, half, 1))


def rope(values, cosine, sine):
    return values * cosine + swap_halves(values) * sine


def rope_back(values, cosine, sine):
    return values * cosine - swap_halves(values) * sine


def one_head(values, which):
    return jnp.where(iota(values.shape, 1) // HEAD_DIM == which, values, jnp.zeros_like(values))


class Place:
    def __init__(self, dp_size, ways):
        self.dp, self.col = lax.axis_index("dp"), lax.axis_index("expert")
        self.ways, self.chips = ways, dp_size // 2
        self.core, self.chip = self.dp % 2, self.dp // 2
        self.side, self.deep = self.chip % 2, self.chip // 2
        self.depth = self.chips // 2
        self.ring = self.deep + self.side * (self.chips - 1 - 2 * self.deep)
        self.group = self.ways * 2
        self.member = self.col * 2 + self.side

    def at(self, chip, core, col):
        return {"dp": chip * 2 + core, "expert": col}

    def mate(self):
        return self.at(self.chip, 1 - self.core, self.col)

    def on_ring(self, step):
        place = (self.ring + step + self.chips) % self.chips
        turn = place // (self.chips // 2)
        deep = place + turn * (self.chips - 1 - 2 * place)
        return self.at(2 * deep + turn, self.core, self.col)

    def in_group(self, step):
        other = (self.member + step) % self.group
        return self.at(self.deep * 2 + other % 2, self.core, other // 2)

    def in_depth(self, step):
        return self.at(((self.deep + step) % self.depth) * 2 + self.side, self.core, self.col)

    def everyone(self):
        return (
            [self.mate(), self.on_ring(1), self.on_ring(-1)]
            + [self.in_group(s) for s in range(1, self.group)]
            + [self.in_depth(s) for s in range(1, self.depth)]
        )


def greet(others):
    barrier = pltpu.get_barrier_semaphore()
    for other in others:
        pl.semaphore_signal(barrier, inc=1, device_id=other, device_id_type=MESH)
    pl.semaphore_wait(barrier, len(others))


def push(src, dst, sends, recvs, index, device):
    copy = pltpu.make_async_remote_copy(
        src_ref=src, dst_ref=dst, send_sem=sends.at[index], recv_sem=recvs.at[index], device_id=device, device_id_type=MESH
    )
    copy.start()
    return copy


def ring_sums(place, sums, from_mate, arrived, sems):
    n = place.chips
    core_sems, ring_sems, gather_sems, mate_sems, free_sem = sems
    parts = range(len(sums))
    by_rows = [arrived[p].shape[3] == sums[p].shape[2] for p in parts]
    copies = []
    firsts = [push(sums[p].at[1 - place.core], from_mate[p], *core_sems, p, place.mate()) for p in parts]
    yield

    def cut(p, way, index):
        rows, cols = arrived[p].shape[2:]
        if by_rows[p]:
            return aligned((way * n + index) * rows, rows, 16), pl.ds(0, cols)
        return aligned(index * rows, rows, 16), pl.ds(way * cols, cols)

    def own(p, way, index):
        rows, cols = cut(p, way, index)
        return sums[p][place.core, rows, cols].astype(f32) + from_mate[p][rows, cols].astype(f32)

    inbound, sent = {}, {}
    for step in range(n - 1):
        for p in parts:
            if step == 0:
                firsts[p].wait()
            for way in range(2):
                sign = 1 - 2 * way
                if step > 0:
                    sent[p, way].wait_send()
                index = (place.ring - sign * (1 + step) + 2 * n) % n
                total = own(p, way, index)
                if step > 0:
                    inbound[p, way].wait_recv()
                    total = total + arrived[p][way, step - 1].astype(f32)
                rows, cols = cut(p, way, index)
                sums[p][place.core, rows, cols] = total.astype(bf16)
                here = sums[p].at[place.core, rows, cols]
                copy = push(here, arrived[p].at[way, step], *ring_sems, (p, way, step), place.on_ring(sign))
                inbound[p, way] = sent[p, way] = copy
        if step == 0:
            pl.semaphore_signal(free_sem, inc=1, device_id=place.mate(), device_id_type=MESH)
        yield
    pl.semaphore_wait(free_sem, 1)
    to_mate = []
    for step in range(n):
        for p in parts:
            for way in range(2):
                sign = 1 - 2 * way
                index = (place.ring - sign * step + 2 * n) % n
                rows, cols = cut(p, way, index)
                inbound[p, way].wait_recv()
                if step == 0:
                    sent[p, way].wait_send()
                    total = own(p, way, index) + arrived[p][way, n - 2].astype(f32)
                    sums[p][place.core, rows, cols] = total.astype(bf16)
                here = sums[p].at[place.core, rows, cols]
                if step < n - 1:
                    copy = push(here, here, *gather_sems, (p, way, step), place.on_ring(sign))
                    inbound[p, way] = copy
                    copies.append(copy)
                to_mate.append(push(here, here, *mate_sems, (p, way, step), place.mate()))
        yield
    for copy in copies:
        copy.wait_send()
    for copy in to_mate:
        copy.wait()
    yield


def spread_sums(place, rows, mine, out, from_mate, shares, depths, sems):
    core_sems, share_sems, depth_sems, gather_sems, mate_sems = sems
    group, depth = place.group, place.depth
    piece = rows // group
    base, away = aligned(place.core * rows, rows, 16), aligned((1 - place.core) * rows, rows, 16)
    first = push(mine.at[away, :], from_mate, *core_sems, 0, place.mate())
    yield
    first.wait()
    mine[base, :] = (mine[base, :].astype(f32) + from_mate[...].astype(f32)).astype(bf16)
    copies = []
    for step in range(1, group):
        other = (place.member + step) % group
        cut = aligned(place.core * rows + other * piece, piece, 16)
        copies.append(push(mine.at[cut, :], shares.at[place.member], *share_sems, step, place.in_group(step)))
    yield
    own = aligned(place.core * rows + place.member * piece, piece, 16)
    shares[place.member] = mine[own, :]
    for copy in copies:
        copy.wait_recv()
    total = shares[0].astype(f32)
    for n in range(1, group):
        total = total + shares[n].astype(f32)
    depths[place.deep] = total.astype(bf16)
    across = [
        push(depths.at[place.deep], depths.at[place.deep], *depth_sems, step, place.in_depth(step)) for step in range(1, depth)
    ]
    yield
    for copy in across:
        copy.wait_recv()
    total = depths[0].astype(f32)
    for n in range(1, depth):
        total = total + depths[n].astype(f32)
    out[own, :] = total.astype(bf16)
    gathers = [push(out.at[own, :], out.at[own, :], *gather_sems, step, place.in_group(step)) for step in range(1, group)]
    yield
    for copy in gathers:
        copy.wait_recv()
    last = push(out.at[base, :], out.at[base, :], *mate_sems, 0, place.mate())
    yield
    for copy in copies + across + gathers:
        copy.wait_send()
    last.wait()
    yield


class Sizes:
    def __init__(self, dp_size, tokens, w_router, w_gate):
        self.dp, self.ways = dp_size, tokens[0]
        self.seg, self.width = tokens[1], tokens[2]
        self.length = self.seg * self.ways
        self.experts = w_router[1]
        self.local, self.hid = w_gate[0], w_gate[2]
        self.cap = -(-max(2, 3 * self.seg // self.experts) // 16) * 16
        self.slots = self.local * self.cap
        self.per = self.ways * self.cap
        self.size = 256
        self.blocks = self.length // self.size
        self.heads = self.width // HEAD_DIM
        self.pairs = self.width // PAIR
        self.chips = dp_size // 2
        self.depth = self.chips // 2
        self.group = self.ways * 2
        self.extra = -(-(self.experts + 1) // 16) * 16
        unit = 16 * self.group
        tiles = 3 * self.width
        extras = 3 * self.extra

        def padded(rows):
            return -(-rows // (2 * unit)) * unit

        self.stages = [padded(tiles + extras)] + [padded(tiles)] * self.pairs + [padded(extras)]
        self.tiles = tiles

    def plain(self, block):
        return (block + 1) * self.size <= self.length - self.seg


def series_tables(z, place, lengths_ref, cos_ref, sin_ref, opening_ref, table_ref):
    count = lengths_ref.shape[1]
    start = 0
    starts = [start]
    for n in range(count):
        start = start + lengths_ref[place.col, n]
        starts.append(start)
    pos = iota((1, z.length), 1)
    opening = jnp.zeros((1, z.length), i32)
    lane = iota((1, PAIR), 1)
    low = jnp.full((1, PAIR), 2 * z.length, i32)
    high = jnp.full((1, PAIR), 2 * z.length, i32)
    table_ref[...] = jnp.zeros_like(table_ref)
    for n, at in enumerate(starts):
        opening = jnp.maximum(opening, jnp.where(pos >= at, at, 0))
        low = jnp.where(lane == n, at, low)
        if n > 0:
            high = jnp.where(lane == n - 1, at, high)
        row = jnp.minimum(at, z.length - 1)
        table_ref[n : n + 1, :PAIR] = cos_ref[pl.ds(row, 1), :]
        table_ref[n : n + 1, PAIR:] = sin_ref[pl.ds(row, 1), :]
    opening_ref[...] = opening
    table = table_ref[...]
    parts = []
    for n in range(3):
        parts.append(table.astype(bf16))
        table = table - parts[-1].astype(f32)
    sign = jnp.where(iota((1, PAIR), 1) % HEAD_DIM < HEAD_DIM // 2, -1.0, 1.0)
    for block in range(z.blocks):
        rows = pl.ds(block * z.size, z.size)
        at = iota((z.size, PAIR), 0) + block * z.size
        picks = jnp.where((at >= low) & (at < high), 1.0, 0.0).astype(bf16)
        base = nn(picks, parts[0]) + (nn(picks, parts[1]) + nn(picks, parts[2]))
        cs, ss = base[:, :PAIR], base[:, PAIR:]
        cp, sp = cos_ref[rows, :], sin_ref[rows, :]
        cos_ref[rows, :] = cp * cs + sp * ss
        sin_ref[rows, :] = (sp * cs - cp * ss) * sign


def project(z, r, rows):
    x = r.x[rows, :].astype(f32)
    first = (x * rms_factor(x) * r.norm_one[...][None, :]).astype(bf16)
    r.first[rows, :] = first
    cosine, sine = r.cos[rows, :], r.sin[rows, :]
    raw = nn(first, r.w_qkv[...])
    for pair in range(z.pairs):
        cut = pl.ds(pair * PAIR, PAIR)
        at = pair * 3 * PAIR
        r.q[rows, cut] = rope(raw[:, at : at + PAIR], cosine, sine).astype(bf16) * HEAD_DIM ** (-0.5)
        r.k[rows, cut] = rope(raw[:, at + PAIR : at + 2 * PAIR], cosine, sine).astype(bf16)
        value = raw[:, at + 2 * PAIR : at + 3 * PAIR].astype(bf16)
        r.v[rows, cut] = value
        r.vt[cut, rows] = value.T


def bias_rows(z, r, block):
    plain = [b for b in range(z.blocks) if z.plain(b)]
    if block in plain:
        return 0, block * z.size
    row = z.size if plain else 0
    for b in range(block):
        if b not in plain:
            row += (b + 1) * z.size
    return row, 0


def bias_total(z):
    plain = [b for b in range(z.blocks) if z.plain(b)]
    return (z.size if plain else 0) + sum((b + 1) * z.size for b in range(z.blocks) if b not in plain)


def make_bias(z, r, block):
    row, low = bias_rows(z, r, block)
    count = (block + 1) * z.size - low
    keys = iota((count, z.size), 0) + low
    queries = iota((count, z.size), 1) + block * z.size
    allowed = keys <= queries
    if not z.plain(block):
        allowed = allowed & (keys >= r.opening[:, block * z.size : (block + 1) * z.size])
    r.bias[pl.ds(row, count), :] = jnp.where(allowed, 0.0, masked_out)


def scores(z, r, block, at, cut, q_head):
    row, low = bias_rows(z, r, block)
    s = nt(r.k[pl.ds(at, z.size), cut], q_head)
    if at >= low:
        s = s + r.bias[pl.ds(row + at - low, z.size), :]
    return s


def attend(z, r, block):
    keys = (block + 1) * z.size
    rows = pl.ds(block * z.size, z.size)
    for pair in range(z.pairs):
        cut = pl.ds(pair * PAIR, PAIR)
        q = r.q[rows, cut]
        outs = []
        for half in range(2):
            q_head = one_head(q, half)
            parts = [scores(z, r, block, at, cut, q_head) for at in range(0, keys, z.size)]
            peak = functools.reduce(jnp.maximum, [jnp.max(s, axis=0, keepdims=True) for s in parts])
            total = jnp.zeros((1, z.size), f32)
            for n, s in enumerate(parts):
                e = jnp.exp(s - peak)
                total = total + jnp.sum(e, axis=0, keepdims=True)
                r.p[half, n * z.size : (n + 1) * z.size, :] = e.astype(bf16)
            head = pair * 2 + half
            r.lse[pl.ds(head, 1), rows] = peak + jnp.log(total)
            o = nn(r.vt[pl.ds(head * HEAD_DIM, HEAD_DIM), :keys], r.p[half, :keys, :])
            outs.append(o * (1.0 / total))
        r.mixed[rows, cut] = jnp.concatenate(outs, axis=0).T.astype(bf16)


def routing(z, routes, second, w_router_t):
    logits = nt(w_router_t, second)
    expert = iota(logits.shape, 0)
    hits = expert == routes[0:1, :], expert == routes[1:2, :]
    l0, l1 = (jnp.sum(jnp.where(hit, logits, 0.0), axis=0, keepdims=True) for hit in hits)
    peak = jnp.maximum(l0, l1)
    e0, e1 = jnp.exp(l0 - peak), jnp.exp(l1 - peak)
    scale = 1.0 / (e0 + e1)
    return hits, (e0 * scale, e1 * scale)


def expert_group(z, r, place, owner, step, slot):
    width, hid, cap = z.width, z.hid, z.cap
    base = place.col * z.local
    for n in range(z.ways):
        rows = pl.ds(n * z.seg, z.seg)
        second = r.second[owner, rows, :]
        hits, gates = routing(z, r.routes[owner, :, rows], second, r.wrt[...])
        hit = hits[0] | hits[1]
        rank = nn(hit.astype(bf16), r.upper[...])
        r.slot[...] = jnp.where(hit, rank, -1.0).astype(i32)
        r.gate[...] = jnp.where(hits[0], gates[0], 0.0) + jnp.where(hits[1], gates[1], 0.0)

        def fill_table(e, carry, n=n):
            cut = aligned(e * cap, cap, 16)
            mine = iota((cap, z.seg), 0) == r.slot[pl.ds(base + e, 1), :]
            r.table[n, cut, :] = jnp.where(mine, 1.0, 0.0).astype(bf16)
            r.gslot[n, cut, 0:1] = jnp.sum(jnp.where(mine, r.gate[pl.ds(base + e, 1), :], 0.0), axis=1, keepdims=True)
            return carry

        lax.fori_loop(0, z.local, fill_table, 0)
        r.y[: z.seg, :width] = second
        r.y[: z.seg, width:] = r.cot[owner, rows, :]
        taken = nn(r.table[n], r.y[: z.seg, :]).astype(bf16)
        for e in range(z.local):
            to = pl.ds(e * z.per + n * cap, cap)
            r.sent[to, :] = taken[e * cap : (e + 1) * cap, :width]
            r.cots[to, :] = taken[e * cap : (e + 1) * cap, width:]
    def one_expert(e, carry):
        to = aligned(e * z.per, z.per, 16)
        cut = aligned(e * cap, cap, 16)
        sent = r.sent[to, :]
        cot = r.cots[to, :].astype(f32)
        gate = jnp.concatenate([r.gslot[n, cut, 0:1] for n in range(z.ways)], axis=0)
        gate_pre = nn(sent, r.wg[e])
        up_pre = nn(sent, r.wu[e])
        sigma = jax.nn.sigmoid(gate_pre)
        active = gate_pre * sigma
        hidden = (active * up_pre).astype(bf16)
        made = nn(hidden, r.wd[e]).astype(bf16).astype(f32)
        gmade = (gate * cot).astype(bf16)
        ghid = nt(gmade, r.wd[e])
        slope = sigma * (1.0 + gate_pre * (1.0 - sigma))
        dgate = (ghid * up_pre * slope).astype(bf16)
        dup = (ghid * active).astype(bf16)
        gsent = (nt(dgate, r.wg[e]) + nt(dup, r.wu[e])).astype(bf16)
        r.hidden[to, :] = hidden
        r.gmade[to, :] = gmade
        r.dgate[to, :] = dgate
        r.dup[to, :] = dup
        gg = jnp.sum(made * cot, axis=1, keepdims=True)
        weighted = (gate * made).astype(bf16)
        for n in range(z.ways):
            lay = aligned(n * z.slots + e * cap, cap, 16)
            r.y[lay, :width] = weighted[n * cap : (n + 1) * cap]
            r.y[lay, width:] = gsent[n * cap : (n + 1) * cap]
            r.gslot[n, cut, 1:2] = gg[n * cap : (n + 1) * cap]
        return carry

    lax.fori_loop(0, z.local, one_expert, 0)
    r.gg_out[step] = jnp.zeros(r.gg_out.shape[1:], f32)
    for n in range(z.ways):
        rows = pl.ds(n * z.seg, z.seg)
        back = tn(r.table[n], r.y[n * z.slots : (n + 1) * z.slots, :])
        r.gsec[slot, rows, :] = back[:, width:].astype(bf16)
        own = jnp.where(step == 0, r.res[rows, :], 0.0)
        r.mix[rows, :] = (own + back[:, :width]).astype(bf16)
        for e in range(z.local):
            cut = pl.ds(e * cap, cap)
            r.gg_out[step, e : e + 1, rows] = jnp.sum(
                r.table[n, cut, :].astype(f32) * r.gslot[n, cut, 1:2], axis=0, keepdims=True
            )


def through_router(z, r, rows):
    second = r.second_own(rows)
    hits, (g0, g1) = routing(z, r.routes_own(rows), second, r.wrt[...])
    gg = jnp.concatenate([r.gg_in[p, : z.local, rows] for p in range(z.ways)], axis=0)
    gg0, gg1 = (jnp.sum(jnp.where(hit, gg, 0.0), axis=0, keepdims=True) for hit in hits)
    inner = g0 * gg0 + g1 * gg1
    glog = jnp.where(hits[0], g0 * (gg0 - inner), 0.0) + jnp.where(hits[1], g1 * (gg1 - inner), 0.0)
    glog = glog.astype(bf16)
    gsec = r.gsec[0, rows, :].astype(f32)
    if z.ways > 2:
        fetch = pltpu.make_async_copy(r.gsec_in.at[:, rows, :], r.gsec_block, r.local_sems.at[7])
        fetch.start()
        fetch.wait()
    for p in range(z.ways - 1):
        gsec = gsec + (r.gsec_block[p] if z.ways > 2 else r.gsec_in[p, rows, :]).astype(f32)
    return second, glog, gsec + tn(glog, r.wrt[...])


def before_attention(z, r):
    heads = (iota((8, z.width), 1) // HEAD_DIM == iota((8, z.width), 0)).astype(bf16)
    gn2 = jnp.zeros((1, z.width), f32)
    grt = jnp.zeros((z.experts, z.width), f32)
    for block in range(z.blocks):
        rows = pl.ds(block * z.size, z.size)
        second, glog, gsec = through_router(z, r, rows)
        grt = grt + nn(glog, second)
        part, gain = norm_back(r.res[rows, :], r.norm_two[...][None, :], gsec)
        gn2 = gn2 + gain
        gres = r.cot_own(rows).astype(f32) + part
        r.gres[rows, :] = gres
        ga = gres.astype(bf16)
        r.ga[rows, :] = ga
        gm = nt(ga, r.w_out[...]).astype(bf16)
        r.gm[rows, :] = gm
        prod = gm.astype(f32) * r.mixed[rows, :].astype(f32)
        high = prod.astype(bf16)
        rest = (prod - high.astype(f32)).astype(bf16)
        r.delta[:, rows] = nt(heads, high) + nt(heads, rest)
    return gn2, grt


def attend_back(z, r, block, pair):
    keys = (block + 1) * z.size
    rows = pl.ds(block * z.size, z.size)
    cut = pl.ds(pair * PAIR, PAIR)
    q, gm = r.q[rows, cut], r.gm[rows, cut]
    q_heads = [one_head(q, half) for half in range(2)]
    gm_heads = [one_head(gm, half) for half in range(2)]
    dq = []
    for half in range(2):
        head = pair * 2 + half
        lse = r.lse[pl.ds(head, 1), rows]
        delta = r.delta[pl.ds(head, 1), rows]
        for at in range(0, keys, z.size):
            cols = pl.ds(at, z.size)
            p = jnp.exp(scores(z, r, block, at, cut, q_heads[half]) - lse)
            dp = nt(r.v[cols, cut], gm_heads[half])
            r.p[half, cols, :] = p.astype(bf16)
            r.ds[half][cols, :] = (p * (dp - delta)).astype(bf16)
        dq.append(tn(r.ds[half][:keys, :], r.k[:keys, cut]))
    dv = nn(r.p[0, :keys, :], gm_heads[0]) + nn(r.p[1, :keys, :], gm_heads[1])
    dk = nn(r.ds[0][:keys, :], q_heads[0]) + nn(r.ds[1][:keys, :], q_heads[1])
    last = keys - z.size
    if block > 0:
        r.dv[:last, :] += dv[:last]
        r.dk[:last, :] += dk[:last]
    r.dv[last:keys, :] = dv[last:]
    r.dk[last:keys, :] = dk[last:]
    dq = jnp.where(iota((z.size, PAIR), 1) < HEAD_DIM, dq[0], dq[1]) * HEAD_DIM ** (-0.5)
    r.graws[pair][rows, :PAIR] = rope_back(dq, r.cos[rows, :], r.sin[rows, :]).astype(bf16)


def pair_back(z, r, pair):
    r.graws[pair][:, PAIR : 2 * PAIR] = rope_back(r.dk[...], r.cos[...], r.sin[...]).astype(bf16)
    r.graws[pair][:, 2 * PAIR :] = r.dv[...].astype(bf16)
    return tn(r.first[...], r.graws[pair][...])


def fill_stage(z, ref, wide, extra):
    at = 0
    if wide is not None:
        for n in range(3):
            ref[pl.ds(n * z.width, z.width), :] = wide[:, n * PAIR : (n + 1) * PAIR].astype(bf16)
        at = z.tiles
    if extra is not None:
        gap = jnp.zeros((z.extra - extra.shape[0], z.width), f32)
        extra = jnp.concatenate([extra, gap], axis=0).astype(bf16)
        for n in range(3):
            ref[pl.ds(at, z.extra), :] = extra[:, n * PAIR : (n + 1) * PAIR]
            at += z.extra
    if at < ref.shape[0]:
        ref[pl.ds(at, ref.shape[0] - at), :] = jnp.zeros((ref.shape[0] - at, PAIR), bf16)


class Names:
    pass


def layer_kernel(z, ins, outs, scratch, *refs):
    r = Names()
    for (name, *_), ref in zip(ins + outs + scratch, refs, strict=True):
        setattr(r, name, ref)
    place = Place(z.dp, z.ways)
    me, ways, seg = place.col, z.ways, z.seg
    peers = [(step, (me + step) % ways) for step in range(1, ways)]

    def on(col):
        return {"expert": col}

    def local_copy(src, dst, index):
        return pltpu.make_async_copy(src, dst, r.local_sems.at[index])

    own_seg = aligned(me * seg, seg, 16)
    own_lanes = aligned(me * seg, seg, 128)
    loads = [
        local_copy(r.tokens.at[me], r.x.at[own_seg, :], 0),
        local_copy(r.w_gate, r.wg, 1),
        local_copy(r.w_up, r.wu, 2),
        local_copy(r.w_down, r.wd, 3),
        local_copy(r.cotangent, r.cot.at[:, own_seg, :], 4),
        local_copy(r.routes_t, r.routes.at[:, :, own_lanes], 5),
        local_copy(r.cp, r.cos, 6),
        local_copy(r.sp, r.sin, 7),
    ]
    for copy in loads:
        copy.start()
    greet(place.everyone())

    def token_copy(step, col):
        return pltpu.make_async_remote_copy(
            src_ref=r.tokens.at[col], dst_ref=r.x.at[own_seg, :], send_sem=r.x_send.at[step], recv_sem=r.x_recv.at[step],
            device_id=on(col), device_id_type=MESH)

    def route_copy(step, col):
        return pltpu.make_async_remote_copy(
            src_ref=r.routes_t, dst_ref=r.routes.at[:, :, own_lanes], send_sem=r.rt_send.at[step], recv_sem=r.rt_recv.at[step],
            device_id=on(col), device_id_type=MESH)

    def cot_copy(row, kind, step, col):
        return pltpu.make_async_remote_copy(
            src_ref=r.cotangent.at[row], dst_ref=r.cot.at[row, own_seg, :], send_sem=r.cot_send.at[kind, step],
            recv_sem=r.cot_recv.at[kind, step], device_id=on(col), device_id_type=MESH)

    def second_copy(block, step, col):
        rows = pl.ds(block * z.size, z.size)
        return pltpu.make_async_remote_copy(
            src_ref=r.second.at[me, rows, :], dst_ref=r.second.at[me, rows, :], send_sem=r.sec_send.at[block, step],
            recv_sem=r.sec_recv.at[block, step], device_id=on(col), device_id_type=MESH)

    tokens_out = [token_copy(step, col) for step, col in peers]
    routes_out = [route_copy(step, col) for step, col in peers]
    for copy in tokens_out + routes_out:
        copy.start()

    for pair in range(z.pairs):
        cut = pl.ds(pair * PAIR, PAIR)
        for n, w in enumerate((r.w_query, r.w_key, r.w_value)):
            r.w_qkv[:, pl.ds((pair * 3 + n) * PAIR, PAIR)] = w[:, cut]
    r.wrt = r.w_router
    r.upper[...] = jnp.where(iota((seg, seg), 0) < iota((seg, seg), 1), 1.0, 0.0).astype(bf16)
    loads[6].wait()
    loads[7].wait()
    series_tables(z, place, r.lengths, r.cos, r.sin, r.opening, r.starts)
    for block in range(z.blocks):
        if not z.plain(block) or block == 0:
            make_bias(z, r, block)
    unit = min(z.size, seg)
    loads[0].wait()
    for n in range(seg // unit):
        project(z, r, aligned(me * seg + n * unit, unit, 128))
    for copy in tokens_out:
        copy.wait()
    cots_out = {}
    for step, col in peers:
        cots_out[0, step] = cot_copy(col, 0, step, col)
        cots_out[0, step].start()
    for step, col in peers:
        for n in range(seg // unit):
            project(z, r, aligned(col * seg + n * unit, unit, 128))
    seconds_out = []
    for block in range(z.blocks):
        rows = pl.ds(block * z.size, z.size)
        attend(z, r, block)
        residual = r.x[rows, :].astype(f32) + nn(r.mixed[rows, :], r.w_out[...])
        r.res[rows, :] = residual
        r.second[me, rows, :] = (residual * rms_factor(residual) * r.norm_two[...][None, :]).astype(bf16)
        for step, col in peers:
            seconds_out.append(second_copy(block, step, col))
            seconds_out[-1].start()
    for step, col in peers:
        for kind in range(1, ways):
            cots_out[kind, step] = cot_copy((col + kind) % ways, kind, step, col)
            cots_out[kind, step].start()
    for copy in loads[1:6]:
        copy.wait()
    for copy in routes_out:
        copy.wait()

    def slot_of(step):
        return (step > 0) * (1 + (step + 1) % 2) if ways > 2 else step

    def send_back(step, owner):
        return [
            pltpu.make_async_remote_copy(
                src_ref=r.gsec.at[slot_of(step)], dst_ref=r.gsec_in.at[step - 1], send_sem=r.back_send.at[0, step],
                recv_sem=r.back_recv.at[0, step], device_id=on(owner), device_id_type=MESH),
            pltpu.make_async_remote_copy(
                src_ref=r.gg_out.at[step], dst_ref=r.gg_in.at[me], send_sem=r.back_send.at[1, step],
                recv_sem=r.back_recv.at[1, step], device_id=on(owner), device_id_type=MESH),
        ]

    def group_step(step, carry):
        owner = (me + step) % ways

        @pl.when(step > 0)
        def _():
            for block in range(z.blocks):
                second_copy(block, ways - step, owner).wait_recv()

        for other in range(1, ways):
            cot_copy(owner, step, other, owner).wait_recv()
        @pl.when(step > 2)
        def _():
            for copy in send_back(step - 2, (owner + ways - 2) % ways):
                copy.wait_send()

        expert_group(z, r, place, owner, step, slot_of(step))
        keep = local_copy(r.mix, r.mix_out.at[step], 6)
        keep.start()
        keep.wait()

        @pl.when(step > 0)
        def _():
            for copy in send_back(step, owner):
                copy.start()

        return carry

    half = z.local // 2
    sums = (r.grad_gate, r.grad_up, r.grad_down)

    def weight_grads(n, carry):
        e = (n + (1 - place.core) * half) % z.local
        side = e // half
        to = aligned(e * z.per, z.per, 16)
        wide, deep = aligned(e % half * z.width, z.width, 16), aligned(e % half * z.hid, z.hid, 16)
        sent, hidden = r.sent[to, :], r.hidden[to, :]
        r.grad_gate[side, wide, :] = (r.grad_gate[side, wide, :].astype(f32) + tn(sent, r.dgate[to, :])).astype(bf16)
        r.grad_up[side, wide, :] = (r.grad_up[side, wide, :].astype(f32) + tn(sent, r.dup[to, :])).astype(bf16)
        r.grad_down[side, deep, :] = (r.grad_down[side, deep, :].astype(f32) + tn(hidden, r.gmade[to, :])).astype(bf16)
        return carry

    ring = ring_sums(place, sums, (r.fm0, r.fm1, r.fm2), (r.ar0, r.ar1, r.ar2),
                     ((r.rc_s, r.rc_r), (r.rs_s, r.rs_r), (r.rg_s, r.rg_r), (r.rm_s, r.rm_r), r.ring_free))

    for ref in sums:
        ref[...] = jnp.zeros_like(ref)

    def whole_step(step, carry):
        group_step(step, carry)

        @pl.when(step < ways - 1)
        def _():
            lax.fori_loop(0, z.local, weight_grads, 0)

        return carry

    lax.fori_loop(0, ways, whole_step, 0)
    lax.fori_loop(0, half, weight_grads, 0)
    next(ring)
    lax.fori_loop(half, z.local, weight_grads, 0)
    r.gg_in[me] = r.gg_out[0]
    running = [ring]

    def tick(count=1):
        for _ in range(count):
            for task in list(running):
                if next(task, "end") == "end":
                    running.remove(task)

    tick()
    for step, owner in peers:
        for copy in send_back(step, owner):
            copy.wait_recv()
            if step > ways - 3:
                copy.wait_send()
    keep_outs = []
    for n in range(ways):
        keep_outs.append(local_copy(r.mix_out.at[n, own_seg, :], r.out_in.at[me, (me + n) % ways], 8 + n))
        keep_outs[-1].start()
    outs_sent = []
    for step, col in peers:
        for n in range(ways):
            copy = pltpu.make_async_remote_copy(
                src_ref=r.mix_out.at[n, aligned(col * seg, seg, 16), :], dst_ref=r.out_in.at[me, (me + n) % ways],
                send_sem=r.out_send.at[n, step], recv_sem=r.out_recv.at[n, step], device_id=on(col), device_id_type=MESH)
            copy.start()
            outs_sent.append(copy)

    r.second_own = lambda rows: r.second[me, rows, :]
    r.routes_own = lambda rows: r.routes[me, :, rows]
    r.cot_own = lambda rows: r.cot[me, rows, :]

    def stage(n):
        own = [getattr(r, f"st{n}_{part}") for part in ("send", "out", "mate", "shares", "depths")]
        sems = [(getattr(r, f"st{n}_{k}s"), getattr(r, f"st{n}_{k}r")) for k in ("c", "g", "d", "a", "m")]
        return spread_sums(place, z.stages[n], *own, sems)

    grads_sent = []

    r.gres, r.gtok = r.res, r.sent.at[: z.length, :]
    r.ga, r.gm = r.sent.at[: z.length, :], r.cots.at[: z.length, :]
    r.graws = [r.gmade.at[: z.length, :], r.hidden.at[: z.length, : z.width], r.dgate.at[: z.length, : z.width]]
    r.ds = [r.dup.at[: z.length, : z.size], r.dup.at[: z.length, z.size : 2 * z.size]]
    gn2, grt = before_attention(z, r)
    fill_stage(z, r.st0_send, tn(r.mixed[...], r.ga[...]), jnp.concatenate([grt, gn2], axis=0))
    running.append(stage(0))
    for pair in range(z.pairs):
        work = 0
        for block in range(z.blocks):
            attend_back(z, r, block, pair)
            work += block + 1
            if work >= 3:
                tick()
                work = 0
        wide = pair_back(z, r, pair)
        fill_stage(z, getattr(r, f"st{pair + 1}_send"), wide, None)
        running.append(stage(pair + 1))
        tick()
    gn1 = jnp.zeros((1, z.width), f32)
    for n in range(ways):
        for m in range(seg // unit):
            rows = pl.ds(n * seg + m * unit, unit)
            gfirst = functools.reduce(
                lambda a, b: a + b,
                [nt(r.graws[p][rows, :], r.w_qkv[:, pl.ds(p * 3 * PAIR, 3 * PAIR)]) for p in range(z.pairs)],
            )
            part, gain = norm_back(r.x[rows, :].astype(f32), r.norm_one[...][None, :], gfirst)
            gn1 = gn1 + gain
            r.gtok[rows, :] = (r.gres[rows, :] + part).astype(bf16)
    for step, col in peers:
        copy = pltpu.make_async_remote_copy(
            src_ref=r.gtok.at[aligned(col * seg, seg, 16), :], dst_ref=r.grad_tokens.at[me], send_sem=r.gt_send.at[step],
            recv_sem=r.gt_recv.at[step], device_id=on(col), device_id_type=MESH)
        copy.start()
        grads_sent.append(copy)
    r.grad_tokens[me] = r.gtok[own_seg, :]
    fill_stage(z, getattr(r, f"st{z.pairs + 1}_send"), None, gn1)
    running.append(stage(z.pairs + 1))
    tick()
    for copy in keep_outs + outs_sent:
        copy.wait()
    while running:
        tick()
    for copy in grads_sent:
        copy.wait()
    for copy in seconds_out + list(cots_out.values()):
        copy.wait_send()
    for n in range(3):
        r.grad_out[:, pl.ds(n * PAIR, PAIR)] = r.st0_out[pl.ds(n * z.width, z.width), :].astype(f32)
        cut = pl.ds(n * PAIR, PAIR)
        extra = r.st0_out[pl.ds(z.tiles + n * z.extra, z.extra), :].astype(f32)
        r.grad_router[:, cut] = extra[: z.experts]
        r.grad_norm_two[:, cut] = extra[z.experts : z.experts + 1]
        r.grad_norm_one[:, cut] = getattr(r, f"st{z.pairs + 1}_out")[pl.ds(n * z.extra, z.extra), :].astype(f32)[0:1]
    for pair in range(z.pairs):
        cut = pl.ds(pair * PAIR, PAIR)
        for n, ref in enumerate((r.grad_query, r.grad_key, r.grad_value)):
            ref[:, cut] = getattr(r, f"st{pair + 1}_out")[pl.ds(n * z.width, z.width), :].astype(f32)


def rope_tables(length):
    half = HEAD_DIM // 2
    inverse = np.exp(np.arange(half) * (-2.0 * math.log(10000.0) / HEAD_DIM))
    angle = np.tile(np.arange(length)[:, None] * inverse[None, :], (1, 4))
    return np.cos(angle).astype(np.float32), np.sin(angle).astype(np.float32)


def body(tokens, lengths, routes, cotangent, norm_one, w_query, w_key, w_value, w_out, norm_two, w_router, w_gate, w_up, w_down):
    z = Sizes(lax.axis_size("dp"), tokens.shape, w_router.shape, w_gate.shape)
    assert z.ways == lax.axis_size("expert") and z.local % 2 == 0
    L, D, W, H = z.length, z.width, z.ways, z.hid
    half = z.local // 2
    cp, sp = rope_tables(L)
    hbm, near = pl.BlockSpec(memory_space=pl.ANY), pl.BlockSpec(memory_space=pltpu.VMEM)
    ins = [
        ("tokens", hbm, tokens), ("cotangent", hbm, cotangent), ("routes_t", hbm, routes.transpose(0, 2, 1)),
        ("lengths", pl.BlockSpec(memory_space=pltpu.SMEM), lengths), ("cp", hbm, jnp.asarray(cp)), ("sp", hbm, jnp.asarray(sp)),
        ("norm_one", near, norm_one), ("norm_two", near, norm_two),
        ("w_query", near, w_query), ("w_key", near, w_key), ("w_value", near, w_value), ("w_out", near, w_out),
        ("w_router", near, w_router.T), ("w_gate", hbm, w_gate), ("w_up", hbm, w_up), ("w_down", hbm, w_down),
    ]
    outs = [
        ("out_in", (W, W, z.seg, D), bf16), ("mix_out", (W, L, D), bf16), ("grad_tokens", (W, z.seg, D), bf16),
        ("grad_gate", (2, half * D, H), bf16), ("grad_up", (2, half * D, H), bf16), ("grad_down", (2, half * H, D), bf16),
        ("grad_query", (D, D), f32), ("grad_key", (D, D), f32), ("grad_value", (D, D), f32), ("grad_out", (D, D), f32),
        ("grad_norm_one", (1, D), f32), ("grad_norm_two", (1, D), f32), ("grad_router", (z.experts, D), f32),
    ]
    n = z.chips
    pieces = [(half * D // n, H // 2), (half * D // n, H // 2), (half * H // (2 * n), D)]
    halves = [(half * D, H), (half * D, H), (half * H, D)]
    scratch = [
        ("x", (L, D), bf16), ("cot", (W, L, D), bf16), ("routes", (W, 2, L), i32),
        ("cos", (L, PAIR), f32), ("sin", (L, PAIR), f32), ("opening", (1, L), i32), ("starts", (PAIR, 2 * PAIR), f32),
        ("w_qkv", (D, 3 * D), bf16),
        ("first", (L, D), bf16), ("q", (L, D), bf16), ("k", (L, D), bf16), ("v", (L, D), bf16), ("vt", (D, L), bf16),
        ("bias", (bias_total(z), z.size), f32), ("p", (2, L, z.size), bf16),
        ("lse", (8, L), f32), ("mixed", (L, D), bf16), ("res", (L, D), f32), ("second", (W, L, D), bf16),


        ("gsec", (min(W, 3), L, D), bf16), ("mix", (L, D), bf16),
        ("gg_out", (W, 8, L), f32), ("gg_in", (W, 8, L), f32),

    ]
    if W > 2:
        outs.append(("gsec_in", (W - 1, L, D), bf16))
        scratch.append(("gsec_block", (W - 1, z.size, D), bf16))
    else:
        scratch.append(("gsec_in", (1, L, D), bf16))
    tall = max(z.local * z.per, L)
    scratch += [
        ("upper", (z.seg, z.seg), bf16), ("slot", (z.experts, z.seg), i32), ("gate", (z.experts, z.seg), f32),
        ("wg", (z.local, D, H), bf16), ("wu", (z.local, D, H), bf16), ("wd", (z.local, H, D), bf16),
        ("table", (W, z.slots, z.seg), bf16), ("gslot", (W, z.slots, 2), f32),
        ("y", (max(W * z.slots, z.seg), 2 * D), bf16), ("delta", (8, L), f32), ("dk", (L, PAIR), f32), ("dv", (L, PAIR), f32),
        ("sent", (tall, D), bf16), ("cots", (tall, D), bf16), ("gmade", (tall, D), bf16),
        ("hidden", (tall, H), bf16), ("dgate", (tall, H), bf16), ("dup", (tall, H), bf16),
    ]
    for m in range(3):
        scratch.append((f"fm{m}", halves[m], bf16))
        scratch.append((f"ar{m}", (2, n - 1) + pieces[m], bf16))
    for m, rows in enumerate(z.stages):
        piece = rows // z.group
        scratch += [(f"st{m}_send", (2 * rows, PAIR), bf16), (f"st{m}_out", (2 * rows, PAIR), bf16), (f"st{m}_mate", (rows, PAIR), bf16),
                    (f"st{m}_shares", (z.group, piece, PAIR), bf16), (f"st{m}_depths", (z.depth, piece, PAIR), bf16)]
        for kind, count in (("c", 1), ("g", z.group), ("d", z.depth), ("a", z.group), ("m", 1)):
            scratch += [(f"st{m}_{kind}s", (count,), None), (f"st{m}_{kind}r", (count,), None)]
    for name, dims in (("x", (W,)), ("rt", (W,)), ("cot", (W, W)), ("sec", (z.blocks, W)), ("back", (2, W)), ("out", (W, W)), ("gt", (W,))):
        scratch += [(f"{name}_send", dims, None), (f"{name}_recv", dims, None)]
    for name, dims in (("rc", (3,)), ("rs", (3, 2, n - 1)), ("rg", (3, 2, n - 1)), ("rm", (3, 2, n))):
        scratch += [(f"{name}_s", dims, None), (f"{name}_r", dims, None)]
    scratch.append(("ring_free", (), "regular"))
    scratch.append(("local_sems", (8 + W,), None))
    results = pl.pallas_call(
        functools.partial(layer_kernel, z, ins, outs, scratch),
        out_shape=[jax.ShapeDtypeStruct(dims, kind) for _, dims, kind in outs],
        in_specs=[spec for _, spec, _ in ins],
        out_specs=[hbm if name in ("out_in", "mix_out", "gsec_in") else near for name, *_ in outs],
        scratch_shapes=[
            pltpu.SemaphoreType.REGULAR if t == "regular" else pltpu.SemaphoreType.DMA(d) if t is None else pltpu.VMEM(d, t)
            for _, d, t in scratch
        ],
        compiler_params=pltpu.CompilerParams(vmem_limit_bytes=LIMIT, collective_id=0, has_side_effects=True),
        name="layer",
    )(*[item for _, _, item in ins])
    parts, _, gtok, gate, up, down, gq, gk, gv, gout, gn1, gn2, grt = results[:13]
    output = functools.reduce(lambda a, b: a + b, [parts[n].astype(f32) for n in range(W)]).astype(bf16)
    shape = w_gate.shape
    return (output, gtok.astype(f32), gn1[0], gq, gk, gv, gout, gn2[0], grt.T,
            gate.reshape(shape).astype(f32), up.reshape(shape).astype(f32), down.reshape(w_down.shape).astype(f32))


def solution(mesh):
    split, copied = P("dp", "expert", None), P()
    per_expert = P("expert", None, None)
    return jax.shard_map(
        body,
        mesh=mesh,
        in_specs=(split, P("dp", None), split, split) + (copied,) * 7 + (per_expert,) * 3,
        out_specs=(split, split) + (copied,) * 7 + (per_expert,) * 3,
        check_vma=False,
    )
```

```python
import functools
import math

import jax
import jax.numpy as jnp
import numpy as np
from jax import lax
from jax.experimental import pallas as pl
from jax.experimental.pallas import tpu as pltpu
from jax.sharding import PartitionSpec as P

HEAD_DIM = 64
PAIR = 128
epsilon = 1e-06
masked_out = -1e30
f32 = jnp.float32
bf16 = jnp.bfloat16
i32 = jnp.int32
MESH = pl.DeviceIdType.MESH
LIMIT = 63 * 1024 * 1024
EARLY, LATE = 3.3, 4.4
STEPS = ("c", "w", "n", "d", "nb", "wb", "cb")


def nn(a, b):
    return lax.dot_general(a, b, (((1,), (0,)), ((), ())), preferred_element_type=f32)


def nt(a, b):
    return lax.dot_general(a, b, (((1,), (1,)), ((), ())), preferred_element_type=f32)


def tn(a, b):
    return lax.dot_general(a, b, (((0,), (0,)), ((), ())), preferred_element_type=f32)


def iota(shape, dim):
    return lax.broadcasted_iota(i32, shape, dim)


def aligned(start, size, unit):
    return pl.ds(pl.multiple_of(start, unit), size)


def rms_factor(values):
    return lax.rsqrt(jnp.mean(values * values, axis=-1, keepdims=True) + epsilon)


def norm_back(values, gain, grads):
    factor = rms_factor(values)
    unit = values * factor
    weighted = grads * gain
    inner = jnp.mean(weighted * unit, axis=-1, keepdims=True)
    return factor * (weighted - unit * inner), jnp.sum(grads * unit, axis=0, keepdims=True)


def swap_halves(values):
    half = HEAD_DIM // 2
    lane = iota(values.shape, 1) % HEAD_DIM
    return jnp.where(lane < half, pltpu.roll(values, PAIR - half, 1), pltpu.roll(values, half, 1))


def rope(values, cosine, sine):
    return values * cosine + swap_halves(values) * sine


def rope_back(values, cosine, sine):
    return values * cosine - swap_halves(values) * sine


def one_head(values, which):
    return jnp.where(iota(values.shape, 1) // HEAD_DIM == which, values, jnp.zeros_like(values))


class Place:
    def __init__(self, dp_size, ways):
        self.dp, self.col = lax.axis_index("dp"), lax.axis_index("expert")
        self.ways, self.chips = ways, dp_size // 2
        self.core, self.chip = self.dp % 2, self.dp // 2
        self.side, self.deep = self.chip % 2, self.chip // 2
        self.depth = self.chips // 2
        self.ring = self.deep + self.side * (self.chips - 1 - 2 * self.deep)
        self.group = self.ways * 2
        self.member = self.col * 2 + self.side

    def at(self, chip, core, col):
        return {"dp": chip * 2 + core, "expert": col}

    def mate(self):
        return self.at(self.chip, 1 - self.core, self.col)

    def on_ring(self, step):
        place = (self.ring + step + self.chips) % self.chips
        turn = place // (self.chips // 2)
        deep = place + turn * (self.chips - 1 - 2 * place)
        return self.at(2 * deep + turn, self.core, self.col)

    def in_column(self, step):
        return self.at(self.chip, self.core, (self.col + step) % self.ways)

    def across(self):
        return self.at(self.deep * 2 + 1 - self.side, self.core, self.col)

    def other_chip(self, step):
        return self.at((self.chip + step) % self.chips, self.core, self.col)

    def deeper(self, level):
        unit = 1 << level
        return self.at((self.deep + unit * (1 - 2 * (self.deep // unit % 2))) * 2 + self.side, self.core, self.col)

    def everyone(self):
        return (
            [self.mate()]
            + [self.in_column(s) for s in range(1, self.ways)]
            + [self.other_chip(s) for s in range(1, self.chips)]
        )


class Pump:
    def __init__(self):
        self.tasks = []

    def add(self, task, every):
        next(task)
        self.tasks.append([task, every, 0.0])

    def __call__(self, work):
        for item in list(self.tasks):
            item[2] += work
            while item[2] >= item[1] and item in self.tasks:
                item[2] -= item[1]
                if next(item[0], "end") == "end":
                    self.tasks.remove(item)

    def drain(self):
        while self.tasks:
            self(1.1)


def greet(others):
    barrier = pltpu.get_barrier_semaphore()
    for other in others:
        pl.semaphore_signal(barrier, inc=1, device_id=other, device_id_type=MESH)
    pl.semaphore_wait(barrier, len(others))


def push(src, dst, sends, recvs, index, device):
    copy = pltpu.make_async_remote_copy(
        src_ref=src, dst_ref=dst, send_sem=sends.at[index], recv_sem=recvs.at[index], device_id=device, device_id_type=MESH
    )
    copy.start()
    return copy


def ring_sums(place, sums, from_mate, arrived, sems):
    n = place.chips
    core_sems, ring_sems, gather_sems, mate_sems, free_sem = sems
    parts = range(len(sums))
    by_rows = [arrived[p].shape[3] == sums[p].shape[2] for p in parts]
    copies = []
    firsts = [push(sums[p].at[1 - place.core], from_mate[p], *core_sems, p, place.mate()) for p in parts]
    yield

    def cut(p, way, index):
        rows, cols = arrived[p].shape[2:]
        if by_rows[p]:
            return aligned((way * n + index) * rows, rows, 16), pl.ds(0, cols)
        return aligned(index * rows, rows, 16), pl.ds(way * cols, cols)

    def own(p, way, index):
        rows, cols = cut(p, way, index)
        return sums[p][place.core, rows, cols].astype(f32) + from_mate[p][rows, cols].astype(f32)

    inbound, sent = {}, {}
    for step in range(n - 1):
        for p in parts:
            if step == 0:
                firsts[p].wait()
            for way in range(2):
                sign = 1 - 2 * way
                if step > 0:
                    sent[p, way].wait_send()
                index = (place.ring - sign * (1 + step) + 2 * n) % n
                total = own(p, way, index)
                if step > 0:
                    inbound[p, way].wait_recv()
                    total = total + arrived[p][way, step - 1].astype(f32)
                rows, cols = cut(p, way, index)
                sums[p][place.core, rows, cols] = total.astype(bf16)
                here = sums[p].at[place.core, rows, cols]
                copy = push(here, arrived[p].at[way, step], *ring_sems, (p, way, step), place.on_ring(sign))
                inbound[p, way] = sent[p, way] = copy
            if step == 0 and p == parts[-1]:
                pl.semaphore_signal(free_sem, inc=1, device_id=place.mate(), device_id_type=MESH)
            yield
    pl.semaphore_wait(free_sem, 1)
    to_mate = []
    for step in range(n):
        for p in parts:
            for way in range(2):
                sign = 1 - 2 * way
                index = (place.ring - sign * step + 2 * n) % n
                rows, cols = cut(p, way, index)
                inbound[p, way].wait_recv()
                if step == 0:
                    sent[p, way].wait_send()
                    total = own(p, way, index) + arrived[p][way, n - 2].astype(f32)
                    sums[p][place.core, rows, cols] = total.astype(bf16)
                here = sums[p].at[place.core, rows, cols]
                if step < n - 1:
                    copy = push(here, here, *gather_sems, (p, way, step), place.on_ring(sign))
                    inbound[p, way] = copy
                    copies.append(copy)
                to_mate.append(push(here, here, *mate_sems, (p, way, step), place.mate()))
            yield
    for copy in copies:
        copy.wait_send()
    for copy in to_mate:
        copy.wait()
    yield


def spread_sums(place, rows, flat, mine, out, from_mate, shares, near, deeps, sems):
    core_sems, share_sems, near_sems, deep_sems, near_back, share_back, core_back = sems
    ways, chips = place.ways, place.chips
    wide = rows // ways
    piece = wide // (chips if flat else 2)
    half, away = aligned(place.core * rows, rows, 16), aligned((1 - place.core) * rows, rows, 16)

    def part(ref, index, size, base=0):
        return ref.at[aligned(base + index * size, size, 16), :]

    first = push(mine.at[away, :], from_mate, *core_sems, 0, place.mate())
    yield
    first.wait()
    mine[half, :] = (mine[half, :].astype(f32) + from_mate[...].astype(f32)).astype(bf16)
    base = place.core * rows
    copies = [
        push(part(mine, (place.col + s) % ways, wide, base), shares.at[place.col], *share_sems, s, place.in_column(s))
        for s in range(1, ways)
    ]
    yield
    shares[place.col] = part(mine, place.col, wide, base)[...]
    for copy in copies:
        copy.wait_recv()
    total = shares[0].astype(f32)
    for n in range(1, ways):
        total = total + shares[n].astype(f32)
    near[0:wide, :] = total.astype(bf16)
    if flat:
        copies += [
            push(part(near, (place.chip + s) % chips, piece), deeps.at[place.chip], *near_sems, s, place.other_chip(s))
            for s in range(1, chips)
        ]
        yield
        deeps[place.chip] = part(near, place.chip, piece)[...]
        for copy in copies[ways - 1 :]:
            copy.wait_recv()
        total = deeps[0].astype(f32)
        for n in range(1, chips):
            total = total + deeps[n].astype(f32)
        own = part(out, place.chip, piece, base + place.col * wide)
        own[...] = total.astype(bf16)
        backs = [push(own, own, *near_back, s, place.other_chip(s)) for s in range(1, chips)]
        copies += backs
        yield
        for copy in backs:
            copy.wait_recv()
    else:
        yield from halving(place, near, deeps, out, part, base, wide, piece, copies, near_sems, deep_sems, near_back)
    own = part(out, place.col, wide, base)
    gathers = [push(own, own, *share_back, s, place.in_column(s)) for s in range(1, ways)]
    yield
    for copy in gathers:
        copy.wait_recv()
    last = push(out.at[half, :], out.at[half, :], *core_back, 0, place.mate())
    yield
    for copy in copies + gathers:
        copy.wait_send()
    last.wait()
    yield


def halving(place, near, deeps, out, part, base, wide, piece, copies, near_sems, deep_sems, near_back):
    copies.append(push(part(near, 1 - place.side, piece), near.at[wide : wide + piece, :], *near_sems, 0, place.across()))
    yield
    copies[-1].wait_recv()
    total = part(near, place.side, piece)[...].astype(f32) + near[wide : wide + piece, :].astype(f32)
    deeps[0, 0] = total.astype(bf16)
    levels = place.depth.bit_length() - 1
    for n in range(levels):
        copies.append(push(deeps.at[n, 0], deeps.at[n, 1], *deep_sems, n, place.deeper(n)))
        yield
        copies[-1].wait_recv()
        total = deeps[n, 0].astype(f32) + deeps[n, 1].astype(f32)
        if n < levels - 1:
            deeps[n + 1, 0] = total.astype(bf16)
    own = part(out, place.member, piece, base)
    own[...] = total.astype(bf16)
    copies.append(push(own, own, *near_back, 0, place.across()))
    yield
    copies[-1].wait_recv()


class Sizes:
    def __init__(self, dp_size, tokens, w_router, w_gate):
        self.dp, self.ways = dp_size, tokens[0]
        self.seg, self.width = tokens[1], tokens[2]
        self.length = self.seg * self.ways
        self.experts = w_router[1]
        self.local, self.hid = w_gate[0], w_gate[2]
        self.cap = -(-max(2, 3 * self.seg // self.experts) // 16) * 16
        self.slots = self.local * self.cap
        self.per = self.ways * self.cap
        self.size = 256
        self.blocks = self.length // self.size
        self.heads = self.width // HEAD_DIM
        self.pairs = self.width // PAIR
        self.chips = dp_size // 2
        self.depth = self.chips // 2
        self.group = self.ways * 2
        self.extra = -(-(self.experts + 1) // 16) * 16
        self.tiles = 3 * self.width
        sizes = [2 * self.tiles + 3 * self.extra] + [self.tiles] * (self.pairs - 1)
        units = [32 * self.group] * (self.pairs - 1) + [32 * self.ways * self.chips]
        self.stages = [-(-size // unit) * unit // 2 for size, unit in zip(sizes, units, strict=True)]

    def plain(self, block):
        return (block + 1) * self.size <= self.length - self.seg


def series_tables(z, place, lengths_ref, cos_ref, sin_ref, opening_ref, table_ref):
    count = lengths_ref.shape[1]
    start = 0
    starts = [start]
    for n in range(count):
        start = start + lengths_ref[place.col, n]
        starts.append(start)
    pos = iota((1, z.length), 1)
    opening = jnp.zeros((1, z.length), i32)
    lane = iota((1, PAIR), 1)
    low = jnp.full((1, PAIR), 2 * z.length, i32)
    high = jnp.full((1, PAIR), 2 * z.length, i32)
    table_ref[...] = jnp.zeros_like(table_ref)
    for n, at in enumerate(starts):
        opening = jnp.maximum(opening, jnp.where(pos >= at, at, 0))
        low = jnp.where(lane == n, at, low)
        if n > 0:
            high = jnp.where(lane == n - 1, at, high)
        row = jnp.minimum(at, z.length - 1)
        table_ref[n : n + 1, :PAIR] = cos_ref[pl.ds(row, 1), :]
        table_ref[n : n + 1, PAIR:] = sin_ref[pl.ds(row, 1), :]
    opening_ref[...] = opening
    table = table_ref[...]
    parts = []
    for n in range(3):
        parts.append(table.astype(bf16))
        table = table - parts[-1].astype(f32)
    sign = jnp.where(iota((1, PAIR), 1) % HEAD_DIM < HEAD_DIM // 2, -1.0, 1.0)
    for block in range(z.blocks):
        rows = pl.ds(block * z.size, z.size)
        at = iota((z.size, PAIR), 0) + block * z.size
        picks = jnp.where((at >= low) & (at < high), 1.0, 0.0).astype(bf16)
        base = nn(picks, parts[0]) + (nn(picks, parts[1]) + nn(picks, parts[2]))
        cs, ss = base[:, :PAIR], base[:, PAIR:]
        cp, sp = cos_ref[rows, :], sin_ref[rows, :]
        cos_ref[rows, :] = cp * cs + sp * ss
        sin_ref[rows, :] = (sp * cs - cp * ss) * sign


def project(z, r, rows):
    x = r.x[rows, :].astype(f32)
    first = (x * rms_factor(x) * r.norm_one[...][None, :]).astype(bf16)
    r.first[rows, :] = first
    cosine, sine = r.cos[rows, :], r.sin[rows, :]
    raw = nn(first, r.w_qkv[...])
    for pair in range(z.pairs):
        cut = pl.ds(pair * PAIR, PAIR)
        at = pair * 3 * PAIR
        r.q[rows, cut] = rope(raw[:, at : at + PAIR], cosine, sine).astype(bf16) * HEAD_DIM ** (-0.5)
        r.k[rows, cut] = rope(raw[:, at + PAIR : at + 2 * PAIR], cosine, sine).astype(bf16)
        value = raw[:, at + 2 * PAIR : at + 3 * PAIR].astype(bf16)
        r.v[rows, cut] = value
        r.vt[cut, rows] = value.T


def bias_rows(z, r, block):
    plain = [b for b in range(z.blocks) if z.plain(b)]
    if block in plain:
        return 0, block * z.size
    row = z.size if plain else 0
    for b in range(block):
        if b not in plain:
            row += (b + 1) * z.size
    return row, 0


def bias_total(z):
    plain = [b for b in range(z.blocks) if z.plain(b)]
    return (z.size if plain else 0) + sum((b + 1) * z.size for b in range(z.blocks) if b not in plain)


def make_bias(z, r, block):
    row, low = bias_rows(z, r, block)
    count = (block + 1) * z.size - low
    keys = iota((count, z.size), 0) + low
    queries = iota((count, z.size), 1) + block * z.size
    allowed = keys <= queries
    if not z.plain(block):
        allowed = allowed & (keys >= r.opening[:, block * z.size : (block + 1) * z.size])
    r.bias[pl.ds(row, count), :] = jnp.where(allowed, 0.0, masked_out)


def scores(z, r, block, at, cut, q_head):
    row, low = bias_rows(z, r, block)
    s = nt(r.k[pl.ds(at, z.size), cut], q_head)
    if at >= low:
        s = s + r.bias[pl.ds(row + at - low, z.size), :]
    return s


def attend(z, r, block):
    keys = (block + 1) * z.size
    rows = pl.ds(block * z.size, z.size)
    for pair in range(z.pairs):
        cut = pl.ds(pair * PAIR, PAIR)
        q = r.q[rows, cut]
        outs = []
        for half in range(2):
            q_head = one_head(q, half)
            parts = [scores(z, r, block, at, cut, q_head) for at in range(0, keys, z.size)]
            peak = functools.reduce(jnp.maximum, [jnp.max(s, axis=0, keepdims=True) for s in parts])
            total = jnp.zeros((1, z.size), f32)
            for n, s in enumerate(parts):
                e = jnp.exp(s - peak)
                total = total + jnp.sum(e, axis=0, keepdims=True)
                r.p[half, n * z.size : (n + 1) * z.size, :] = e.astype(bf16)
            head = pair * 2 + half
            r.lse[pl.ds(head, 1), rows] = peak + jnp.log(total)
            o = nn(r.vt[pl.ds(head * HEAD_DIM, HEAD_DIM), :keys], r.p[half, :keys, :])
            outs.append(o * (1.0 / total))
        r.mixed[rows, cut] = jnp.concatenate(outs, axis=0).T.astype(bf16)


def routing(z, routes, second, w_router_t):
    logits = nt(w_router_t, second)
    expert = iota(logits.shape, 0)
    hits = expert == routes[0:1, :], expert == routes[1:2, :]
    l0, l1 = (jnp.sum(jnp.where(hit, logits, 0.0), axis=0, keepdims=True) for hit in hits)
    peak = jnp.maximum(l0, l1)
    e0, e1 = jnp.exp(l0 - peak), jnp.exp(l1 - peak)
    scale = 1.0 / (e0 + e1)
    return hits, (e0 * scale, e1 * scale)


def expert_group(z, r, place, owner, segs, step, slot, own):
    width, hid, cap = z.width, z.hid, z.cap
    per = len(segs) * cap
    places = [aligned(at * z.seg, z.seg, 128) for at in segs]
    base = place.col * z.local
    for n, rows in enumerate(places):
        second = r.second[owner, rows, :]
        hits, gates = routing(z, r.routes[owner, :, rows], second, r.wrt[...])
        hit = hits[0] | hits[1]
        rank = nn(hit.astype(bf16), r.upper[...])
        r.slot[...] = jnp.where(hit, rank, -1.0).astype(i32)
        r.gate[...] = jnp.where(hits[0], gates[0], 0.0) + jnp.where(hits[1], gates[1], 0.0)

        def fill_table(e, carry, n=n):
            cut = aligned(e * cap, cap, 16)
            mine = iota((cap, z.seg), 0) == r.slot[pl.ds(base + e, 1), :]
            r.table[n, cut, :] = jnp.where(mine, 1.0, 0.0).astype(bf16)
            r.gslot[n, cut, 0:1] = jnp.sum(jnp.where(mine, r.gate[pl.ds(base + e, 1), :], 0.0), axis=1, keepdims=True)
            return carry

        lax.fori_loop(0, z.local, fill_table, 0)
        r.y[: z.seg, :width] = second
        r.y[: z.seg, width:] = r.cot[owner, rows, :]
        taken = nn(r.table[n], r.y[: z.seg, :]).astype(bf16)
        for e in range(z.local):
            to = pl.ds(e * per + n * cap, cap)
            r.sent[to, :] = taken[e * cap : (e + 1) * cap, :width]
            r.cots[to, :] = taken[e * cap : (e + 1) * cap, width:]

    def one_expert(e, carry):
        to = aligned(e * per, per, 16)
        cut = aligned(e * cap, cap, 16)
        sent = r.sent[to, :]
        cot = r.cots[to, :].astype(f32)
        gate = jnp.concatenate([r.gslot[n, cut, 0:1] for n in range(len(segs))], axis=0)
        gate_pre = nn(sent, r.wg[e])
        up_pre = nn(sent, r.wu[e])
        sigma = jax.nn.sigmoid(gate_pre)
        active = gate_pre * sigma
        hidden = (active * up_pre).astype(bf16)
        made = nn(hidden, r.wd[e]).astype(bf16).astype(f32)
        gmade = (gate * cot).astype(bf16)
        ghid = nt(gmade, r.wd[e])
        slope = sigma * (1.0 + gate_pre * (1.0 - sigma))
        dgate = (ghid * up_pre * slope).astype(bf16)
        dup = (ghid * active).astype(bf16)
        gsent = (nt(dgate, r.wg[e]) + nt(dup, r.wu[e])).astype(bf16)
        r.hidden[to, :] = hidden
        r.gmade[to, :] = gmade
        r.dgate[to, :] = dgate
        r.dup[to, :] = dup
        gg = jnp.sum(made * cot, axis=1, keepdims=True)
        weighted = (gate * made).astype(bf16)
        for n in range(len(segs)):
            lay = aligned(n * z.slots + e * cap, cap, 16)
            r.y[lay, :width] = weighted[n * cap : (n + 1) * cap]
            r.y[lay, width:] = gsent[n * cap : (n + 1) * cap]
            r.gslot[n, cut, 1:2] = gg[n * cap : (n + 1) * cap]
        return carry

    lax.fori_loop(0, z.local, one_expert, 0)
    for n, rows in enumerate(places):
        back = tn(r.table[n], r.y[n * z.slots : (n + 1) * z.slots, :])
        r.gsec[slot, rows, :] = back[:, width:].astype(bf16)
        r.mix[rows, :] = (r.res[rows, :] + back[:, :width] if own else back[:, :width]).astype(bf16)
        for e in range(z.local):
            cut = pl.ds(e * cap, cap)
            r.gg_out[step, e : e + 1, rows] = jnp.sum(
                r.table[n, cut, :].astype(f32) * r.gslot[n, cut, 1:2], axis=0, keepdims=True
            )
        keep = pltpu.make_async_copy(r.mix.at[rows, :], r.mix_out.at[step, rows, :], r.local_sems.at[6])
        keep.start()
        keep.wait()


def through_router(z, r, rows):
    second = r.second_own(rows)
    hits, (g0, g1) = routing(z, r.routes_own(rows), second, r.wrt[...])
    gg = jnp.concatenate([r.gg_in[p, : z.local, rows] for p in range(z.ways)], axis=0)
    gg0, gg1 = (jnp.sum(jnp.where(hit, gg, 0.0), axis=0, keepdims=True) for hit in hits)
    inner = g0 * gg0 + g1 * gg1
    glog = jnp.where(hits[0], g0 * (gg0 - inner), 0.0) + jnp.where(hits[1], g1 * (gg1 - inner), 0.0)
    glog = glog.astype(bf16)
    gsec = r.gsec[0, rows, :].astype(f32)
    if z.ways > 2:
        fetch = pltpu.make_async_copy(r.gsec_in.at[:, rows, :], r.gsec_block, r.local_sems.at[7])
        fetch.start()
        fetch.wait()
    for p in range(z.ways - 1):
        gsec = gsec + (r.gsec_block[p] if z.ways > 2 else r.gsec_in[p, rows, :]).astype(f32)
    return second, glog, gsec + tn(glog, r.wrt[...])


def before_attention(z, r, pump):
    heads = (iota((8, z.width), 1) // HEAD_DIM == iota((8, z.width), 0)).astype(bf16)
    gn2 = jnp.zeros((1, z.width), f32)
    grt = jnp.zeros((z.experts, z.width), f32)
    for block in range(z.blocks):
        rows = pl.ds(block * z.size, z.size)
        second, glog, gsec = through_router(z, r, rows)
        grt = grt + nn(glog, second)
        part, gain = norm_back(r.res[rows, :], r.norm_two[...][None, :], gsec)
        gn2 = gn2 + gain
        gres = r.cot_own(rows).astype(f32) + part
        r.gres[rows, :] = gres
        ga = gres.astype(bf16)
        r.ga[rows, :] = ga
        gm = nt(ga, r.w_out[...]).astype(bf16)
        r.gm[rows, :] = gm
        prod = gm.astype(f32) * r.mixed[rows, :].astype(f32)
        high = prod.astype(bf16)
        rest = (prod - high.astype(f32)).astype(bf16)
        r.delta[:, rows] = nt(heads, high) + nt(heads, rest)
        pump(1.0)
    return gn2, grt


def attend_back(z, r, block, pair, pump):
    keys = (block + 1) * z.size
    rows = pl.ds(block * z.size, z.size)
    cut = pl.ds(pair * PAIR, PAIR)
    q, gm = r.q[rows, cut], r.gm[rows, cut]
    q_heads = [one_head(q, half) for half in range(2)]
    gm_heads = [one_head(gm, half) for half in range(2)]
    dq = []
    for half in range(2):
        head = pair * 2 + half
        lse = r.lse[pl.ds(head, 1), rows]
        delta = r.delta[pl.ds(head, 1), rows]
        for at in range(0, keys, z.size):
            cols = pl.ds(at, z.size)
            p = jnp.exp(scores(z, r, block, at, cut, q_heads[half]) - lse)
            dp = nt(r.v[cols, cut], gm_heads[half])
            r.p[half, cols, :] = p.astype(bf16)
            r.ds[half][cols, :] = (p * (dp - delta)).astype(bf16)
        dq.append(tn(r.ds[half][:keys, :], r.k[:keys, cut]))
        pump(0.22 * (block + 1))
    dv = nn(r.p[0, :keys, :], gm_heads[0]) + nn(r.p[1, :keys, :], gm_heads[1])
    dk = nn(r.ds[0][:keys, :], q_heads[0]) + nn(r.ds[1][:keys, :], q_heads[1])
    last = keys - z.size
    if block > 0:
        r.dv[:last, :] += dv[:last]
        r.dk[:last, :] += dk[:last]
    r.dv[last:keys, :] = dv[last:]
    r.dk[last:keys, :] = dk[last:]
    dq = jnp.where(iota((z.size, PAIR), 1) < HEAD_DIM, dq[0], dq[1]) * HEAD_DIM ** (-0.5)
    pump(0.25 * (block + 1))
    r.graws[pair][rows, :PAIR] = rope_back(dq, r.cos[rows, :], r.sin[rows, :]).astype(bf16)


def pair_back(z, r, pair):
    r.graws[pair][:, PAIR : 2 * PAIR] = rope_back(r.dk[...], r.cos[...], r.sin[...]).astype(bf16)
    r.graws[pair][:, 2 * PAIR :] = r.dv[...].astype(bf16)
    return tn(r.first[...], r.graws[pair][...])


def fill_tiles(z, ref, at, wide):
    for n in range(3):
        ref[pl.ds(at + n * z.width, z.width), :] = wide[:, n * PAIR : (n + 1) * PAIR].astype(bf16)


def fill_rest(z, ref, at, extra):
    if extra is not None:
        gap = jnp.zeros((z.extra - extra.shape[0], z.width), f32)
        extra = jnp.concatenate([extra, gap], axis=0).astype(bf16)
        for n in range(3):
            ref[pl.ds(at, z.extra), :] = extra[:, n * PAIR : (n + 1) * PAIR]
            at += z.extra
    if at < ref.shape[0]:
        ref[pl.ds(at, ref.shape[0] - at), :] = jnp.zeros((ref.shape[0] - at, PAIR), bf16)


class Names:
    pass


def layer_kernel(z, ins, outs, scratch, *refs):
    r = Names()
    for (name, *_), ref in zip(ins + outs + scratch, refs, strict=True):
        setattr(r, name, ref)
    place = Place(z.dp, z.ways)
    me, ways, seg = place.col, z.ways, z.seg
    peers = [(step, (me + step) % ways) for step in range(1, ways)]

    def on(col):
        return {"expert": col}

    def local_copy(src, dst, index):
        return pltpu.make_async_copy(src, dst, r.local_sems.at[index])

    own_seg = aligned(me * seg, seg, 16)
    own_lanes = aligned(me * seg, seg, 128)
    loads = [
        local_copy(r.tokens.at[me], r.x.at[own_seg, :], 0),
        local_copy(r.w_gate, r.wg, 1),
        local_copy(r.w_up, r.wu, 2),
        local_copy(r.w_down, r.wd, 3),
        local_copy(r.cotangent, r.cot.at[:, own_seg, :], 4),
        local_copy(r.routes_t, r.routes.at[:, :, own_lanes], 5),
        local_copy(r.cp, r.cos, 6),
        local_copy(r.sp, r.sin, 7),
    ]
    for copy in loads:
        copy.start()
    greet(place.everyone())

    def token_copy(step, col):
        return pltpu.make_async_remote_copy(
            src_ref=r.tokens.at[col], dst_ref=r.x.at[own_seg, :], send_sem=r.x_send.at[step], recv_sem=r.x_recv.at[step],
            device_id=on(col), device_id_type=MESH)

    def route_copy(step, col):
        return pltpu.make_async_remote_copy(
            src_ref=r.routes_t, dst_ref=r.routes.at[:, :, own_lanes], send_sem=r.rt_send.at[step], recv_sem=r.rt_recv.at[step],
            device_id=on(col), device_id_type=MESH)

    def cot_copy(row, kind, step, col):
        return pltpu.make_async_remote_copy(
            src_ref=r.cotangent.at[row], dst_ref=r.cot.at[row, own_seg, :], send_sem=r.cot_send.at[kind, step],
            recv_sem=r.cot_recv.at[kind, step], device_id=on(col), device_id_type=MESH)

    def second_copy(block, step, col):
        rows = pl.ds(block * z.size, z.size)
        return pltpu.make_async_remote_copy(
            src_ref=r.second.at[me, rows, :], dst_ref=r.second.at[me, rows, :], send_sem=r.sec_send.at[block, step],
            recv_sem=r.sec_recv.at[block, step], device_id=on(col), device_id_type=MESH)

    tokens_out = [token_copy(step, col) for step, col in peers]
    routes_out = [route_copy(step, col) for step, col in peers]
    for copy in tokens_out + routes_out:
        copy.start()

    for pair in range(z.pairs):
        cut = pl.ds(pair * PAIR, PAIR)
        for n, w in enumerate((r.w_query, r.w_key, r.w_value)):
            r.w_qkv[:, pl.ds((pair * 3 + n) * PAIR, PAIR)] = w[:, cut]
    r.wrt = r.w_router
    r.upper[...] = jnp.where(iota((seg, seg), 0) < iota((seg, seg), 1), 1.0, 0.0).astype(bf16)
    loads[6].wait()
    loads[7].wait()
    series_tables(z, place, r.lengths, r.cos, r.sin, r.opening, r.starts)
    for block in range(z.blocks):
        if not z.plain(block) or block == 0:
            make_bias(z, r, block)
    unit = min(z.size, seg)
    loads[0].wait()
    for n in range(seg // unit):
        project(z, r, aligned(me * seg + n * unit, unit, 128))
    for copy in tokens_out:
        copy.wait()
    cots_out = {}
    for step, col in peers:
        for kind in range(1, ways):
            cots_out[kind, step] = cot_copy((col + kind) % ways, kind, step, col)
            cots_out[kind, step].start()
    for step, col in peers:
        for n in range(seg // unit):
            project(z, r, aligned(col * seg + n * unit, unit, 128))
    seconds_out = []
    for block in range(z.blocks):
        rows = pl.ds(block * z.size, z.size)
        attend(z, r, block)
        residual = r.x[rows, :].astype(f32) + nn(r.mixed[rows, :], r.w_out[...])
        r.res[rows, :] = residual
        r.second[me, rows, :] = (residual * rms_factor(residual) * r.norm_two[...][None, :]).astype(bf16)
        for step, col in peers:
            seconds_out.append(second_copy(block, step, col))
            seconds_out[-1].start()
    for step, col in peers:
        cots_out[0, step] = cot_copy(col, 0, step, col)
        cots_out[0, step].start()
    for copy in loads[1:6]:
        copy.wait()
    for copy in routes_out:
        copy.wait()

    def slot_of(step):
        return (step > 0) * (1 + (step + 1) % 2) if ways > 2 else step

    def send_back(step, owner):
        return [
            pltpu.make_async_remote_copy(
                src_ref=r.gsec.at[slot_of(step)], dst_ref=r.gsec_in.at[step - 1], send_sem=r.back_send.at[0, step],
                recv_sem=r.back_recv.at[0, step], device_id=on(owner), device_id_type=MESH),
            pltpu.make_async_remote_copy(
                src_ref=r.gg_out.at[step], dst_ref=r.gg_in.at[me], send_sem=r.back_send.at[1, step],
                recv_sem=r.back_recv.at[1, step], device_id=on(owner), device_id_type=MESH),
        ]

    half = z.local // 2
    sums = (r.grad_gate, r.grad_up, r.grad_down)

    def weight_grads(count, first):
        per = count * z.cap

        def one(n, carry):
            e = (n + (1 - place.core) * half) % z.local
            side = e // half
            to = aligned(e * per, per, 16)
            wide, deep = aligned(e % half * z.width, z.width, 16), aligned(e % half * z.hid, z.hid, 16)
            sent, hidden = r.sent[to, :], r.hidden[to, :]
            grads = tn(sent, r.dgate[to, :]), tn(sent, r.dup[to, :]), tn(hidden, r.gmade[to, :])
            for ref, rows, grad in zip(sums, (wide, wide, deep), grads, strict=True):
                ref[side, rows, :] = (grad if first else ref[side, rows, :].astype(f32) + grad).astype(bf16)
            return carry

        return one

    ring = ring_sums(place, sums, (r.fm0, r.fm1, r.fm2), (r.ar0, r.ar1, r.ar2),
                     ((r.rc_s, r.rc_r), (r.rs_s, r.rs_r), (r.rg_s, r.rg_r), (r.rm_s, r.rm_r), r.ring_free))

    r.gg_out[...] = jnp.zeros_like(r.gg_out)
    expert_group(z, r, place, me, [me], 0, 0, True)
    lax.fori_loop(0, z.local, weight_grads(1, True), 0)

    def other_row(step, carry):
        owner = (me + step) % ways
        for block in range(z.blocks):
            second_copy(block, ways - step, owner).wait_recv()
        for other in range(1, ways):
            cot_copy(owner, step, other, owner).wait_recv()

        @pl.when(step > 2)
        def _():
            for copy in send_back(step - 2, (owner + ways - 2) % ways):
                copy.wait_send()

        expert_group(z, r, place, owner, list(range(ways)), step, slot_of(step), False)
        for copy in send_back(step, owner):
            copy.start()
        lax.fori_loop(0, z.local, weight_grads(ways, False), 0)
        return carry

    lax.fori_loop(1, ways, other_row, 0)
    for step, col in peers:
        cot_copy(me, 0, step, col).wait_recv()
    expert_group(z, r, place, me, [col for _, col in peers], 0, 0, True)
    last_grads = weight_grads(ways - 1, False)
    lax.fori_loop(0, half, last_grads, 0)
    next(ring)
    lax.fori_loop(half, z.local, last_grads, 0)
    r.gg_in[me] = r.gg_out[0]
    pump = Pump()
    pump.add(ring, 1.05)
    pump(6.4)
    for step, owner in peers:
        for copy in send_back(step, owner):
            copy.wait_recv()
            if step > ways - 3:
                copy.wait_send()
    keep_outs = []
    for n in range(ways):
        keep_outs.append(local_copy(r.mix_out.at[n, own_seg, :], r.out_in.at[me, (me + n) % ways], 8 + n))
        keep_outs[-1].start()
    outs_sent = []

    def send_outputs():
        chunk = max(seg // 4, 16)
        for step, col in peers:
            for n in range(ways):
                for m in range(seg // chunk):
                    copy = pltpu.make_async_remote_copy(
                        src_ref=r.mix_out.at[n, aligned(col * seg + m * chunk, chunk, 16), :],
                        dst_ref=r.out_in.at[me, (me + n) % ways, pl.ds(m * chunk, chunk), :],
                        send_sem=r.out_send.at[n, step, m], recv_sem=r.out_recv.at[n, step, m], device_id=on(col), device_id_type=MESH)
                    copy.start()
                    outs_sent.append(copy)
                    yield

    pump.add(send_outputs(), 3.0 / max(1, ways - 1) ** 2)
    r.second_own = lambda rows: r.second[me, rows, :]
    r.routes_own = lambda rows: r.routes[me, :, rows]
    r.cot_own = lambda rows: r.cot[me, rows, :]

    def stage(n):
        own = [getattr(r, f"st{n}_{part}") for part in ("send", "out", "mate", "shares", "near", "deeps")]
        sems = [(getattr(r, f"st{n}_{k}s"), getattr(r, f"st{n}_{k}r")) for k in STEPS]
        return spread_sums(place, z.stages[n], n == z.pairs - 1, *own, sems)

    grads_sent = []

    r.gres, r.gtok = r.res, r.sent.at[: z.length, :]
    r.ga, r.gm = r.sent.at[: z.length, :], r.cots.at[: z.length, :]
    r.graws = [r.gmade.at[: z.length, :], r.hidden.at[: z.length, : z.width], r.dgate.at[: z.length, : z.width]]
    r.ds = [r.dup.at[: z.length, : z.size], r.dup.at[: z.length, z.size : 2 * z.size]]
    gn2, grt = before_attention(z, r, pump)
    fill_tiles(z, r.st0_send, z.tiles, tn(r.mixed[...], r.ga[...]))
    fill_rest(z, r.st0_send, 2 * z.tiles, jnp.concatenate([grt, gn2], axis=0))
    for pair in range(z.pairs):
        for block in range(z.blocks):
            attend_back(z, r, block, pair, pump)
        wide = pair_back(z, r, pair)
        send = getattr(r, f"st{pair}_send")
        fill_tiles(z, send, 0, wide)
        if pair > 0:
            fill_rest(z, send, z.tiles, None)
        pump.add(stage(pair), EARLY if pair < z.pairs - 1 else LATE)
    for step, col in peers + [(0, me)]:
        for m in range(seg // unit):
            rows = aligned(col * seg + m * unit, unit, 128)
            gfirst = functools.reduce(
                lambda a, b: a + b,
                [nt(r.graws[p][rows, :], r.w_qkv[:, pl.ds(p * 3 * PAIR, 3 * PAIR)]) for p in range(z.pairs)],
            )
            part, _ = norm_back(r.x[rows, :].astype(f32), r.norm_one[...][None, :], gfirst)
            r.gtok[rows, :] = (r.gres[rows, :] + part).astype(bf16)
            if step > 0:
                copy = pltpu.make_async_remote_copy(
                    src_ref=r.gtok.at[rows, :], dst_ref=r.grad_tokens.at[me, pl.ds(m * unit, unit), :],
                    send_sem=r.gt_send.at[step, m], recv_sem=r.gt_recv.at[step, m], device_id=on(col), device_id_type=MESH)
                copy.start()
                grads_sent.append(copy)
            pump(0.8)
    r.grad_tokens[me] = r.gtok[own_seg, :]
    pump.drain()
    for copy in keep_outs + outs_sent:
        copy.wait()
    for copy in grads_sent:
        copy.wait()
    for copy in seconds_out + list(cots_out.values()):
        copy.wait_send()
    for n in range(3):
        cut = pl.ds(n * PAIR, PAIR)
        r.grad_out[:, cut] = r.st0_out[pl.ds(z.tiles + n * z.width, z.width), :]
        extra = r.st0_out[pl.ds(2 * z.tiles + n * z.extra, z.extra), :].astype(f32)
        r.grad_router[:, cut] = extra[: z.experts]
        r.grad_norm_two[:, cut] = extra[z.experts : z.experts + 1]
    total = jnp.zeros((z.width, PAIR), f32)
    for pair in range(z.pairs):
        cut = pl.ds(pair * PAIR, PAIR)
        ref = getattr(r, f"st{pair}_out")
        for n, (grad, w) in enumerate(((r.grad_query, r.w_query), (r.grad_key, r.w_key), (r.grad_value, r.w_value))):
            tile = ref[pl.ds(n * z.width, z.width), :]
            grad[:, cut] = tile
            total = total + tile.astype(f32) * w[:, cut].astype(f32)
    r.grad_norm_one[...] = jnp.sum(total.T, axis=0, keepdims=True) / r.norm_one[...][None, :]


def rope_tables(length):
    half = HEAD_DIM // 2
    inverse = np.exp(np.arange(half) * (-2.0 * math.log(10000.0) / HEAD_DIM))
    angle = np.tile(np.arange(length)[:, None] * inverse[None, :], (1, 4))
    return np.cos(angle).astype(np.float32), np.sin(angle).astype(np.float32)


def body(tokens, lengths, routes, cotangent, norm_one, w_query, w_key, w_value, w_out, norm_two, w_router, w_gate, w_up, w_down):
    z = Sizes(lax.axis_size("dp"), tokens.shape, w_router.shape, w_gate.shape)
    assert z.ways == lax.axis_size("expert") and z.local % 2 == 0
    L, D, W, H = z.length, z.width, z.ways, z.hid
    half = z.local // 2
    cp, sp = rope_tables(L)
    hbm, near = pl.BlockSpec(memory_space=pl.ANY), pl.BlockSpec(memory_space=pltpu.VMEM)
    ins = [
        ("tokens", hbm, tokens), ("cotangent", hbm, cotangent), ("routes_t", hbm, routes.transpose(0, 2, 1)),
        ("lengths", pl.BlockSpec(memory_space=pltpu.SMEM), lengths), ("cp", hbm, jnp.asarray(cp)), ("sp", hbm, jnp.asarray(sp)),
        ("norm_one", near, norm_one), ("norm_two", near, norm_two),
        ("w_query", near, w_query), ("w_key", near, w_key), ("w_value", near, w_value), ("w_out", near, w_out),
        ("w_router", near, w_router.T), ("w_gate", hbm, w_gate), ("w_up", hbm, w_up), ("w_down", hbm, w_down),
    ]
    outs = [
        ("out_in", (W, W, z.seg, D), bf16), ("mix_out", (W, L, D), bf16), ("grad_tokens", (W, z.seg, D), bf16),
        ("grad_gate", (2, half * D, H), bf16), ("grad_up", (2, half * D, H), bf16), ("grad_down", (2, half * H, D), bf16),
        ("grad_query", (D, D), bf16), ("grad_key", (D, D), bf16), ("grad_value", (D, D), bf16), ("grad_out", (D, D), bf16),
        ("grad_norm_one", (1, D), f32), ("grad_norm_two", (1, D), f32), ("grad_router", (z.experts, D), f32),
    ]
    n = z.chips
    pieces = [(half * D // n, H // 2), (half * D // n, H // 2), (half * H // (2 * n), D)]
    halves = [(half * D, H), (half * D, H), (half * H, D)]
    scratch = [
        ("x", (L, D), bf16), ("cot", (W, L, D), bf16), ("routes", (W, 2, L), i32),
        ("cos", (L, PAIR), f32), ("sin", (L, PAIR), f32), ("opening", (1, L), i32), ("starts", (PAIR, 2 * PAIR), f32),
        ("w_qkv", (D, 3 * D), bf16),
        ("first", (L, D), bf16), ("q", (L, D), bf16), ("k", (L, D), bf16), ("v", (L, D), bf16), ("vt", (D, L), bf16),
        ("bias", (bias_total(z), z.size), f32), ("p", (2, L, z.size), bf16),
        ("lse", (8, L), f32), ("mixed", (L, D), bf16), ("res", (L, D), f32), ("second", (W, L, D), bf16),


        ("gsec", (min(W, 3), L, D), bf16), ("mix", (L, D), bf16),
        ("gg_out", (W, 8, L), f32), ("gg_in", (W, 8, L), f32),

    ]
    if W > 2:
        outs.append(("gsec_in", (W - 1, L, D), bf16))
        scratch.append(("gsec_block", (W - 1, z.size, D), bf16))
    else:
        scratch.append(("gsec_in", (1, L, D), bf16))
    tall = max(z.local * z.per, L)
    scratch += [
        ("upper", (z.seg, z.seg), bf16), ("slot", (z.experts, z.seg), i32), ("gate", (z.experts, z.seg), f32),
        ("wg", (z.local, D, H), bf16), ("wu", (z.local, D, H), bf16), ("wd", (z.local, H, D), bf16),
        ("table", (W, z.slots, z.seg), bf16), ("gslot", (W, z.slots, 2), f32),
        ("y", (max(W * z.slots, z.seg), 2 * D), bf16), ("delta", (8, L), f32), ("dk", (L, PAIR), f32), ("dv", (L, PAIR), f32),
        ("sent", (tall, D), bf16), ("cots", (tall, D), bf16), ("gmade", (tall, D), bf16),
        ("hidden", (tall, H), bf16), ("dgate", (tall, H), bf16), ("dup", (tall, H), bf16),
    ]
    for m in range(3):
        scratch.append((f"fm{m}", halves[m], bf16))
        scratch.append((f"ar{m}", (2, n - 1) + pieces[m], bf16))
    levels = z.depth.bit_length() - 1
    for m, rows in enumerate(z.stages):
        wide = rows // W
        piece = wide // (z.chips if m == z.pairs - 1 else 2)
        deeps = (z.chips, piece, PAIR) if m == z.pairs - 1 else (levels, 2, piece, PAIR)
        scratch += [(f"st{m}_send", (2 * rows, PAIR), bf16), (f"st{m}_out", (2 * rows, PAIR), bf16), (f"st{m}_mate", (rows, PAIR), bf16),
                    (f"st{m}_shares", (W, wide, PAIR), bf16), (f"st{m}_near", (wide + piece, PAIR), bf16), (f"st{m}_deeps", deeps, bf16)]
        for kind, count in zip(STEPS, (1, W, z.chips, levels, z.chips, W, 1), strict=True):
            scratch += [(f"st{m}_{kind}s", (count,), None), (f"st{m}_{kind}r", (count,), None)]
    for name, dims in (("x", (W,)), ("rt", (W,)), ("cot", (W, W)), ("sec", (z.blocks, W)), ("back", (2, W)), ("out", (W, W, 4)), ("gt", (W, z.seg // min(z.size, z.seg)))):
        scratch += [(f"{name}_send", dims, None), (f"{name}_recv", dims, None)]
    for name, dims in (("rc", (3,)), ("rs", (3, 2, n - 1)), ("rg", (3, 2, n - 1)), ("rm", (3, 2, n))):
        scratch += [(f"{name}_s", dims, None), (f"{name}_r", dims, None)]
    scratch.append(("ring_free", (), "regular"))
    scratch.append(("local_sems", (8 + W,), None))
    results = pl.pallas_call(
        functools.partial(layer_kernel, z, ins, outs, scratch),
        out_shape=[jax.ShapeDtypeStruct(dims, kind) for _, dims, kind in outs],
        in_specs=[spec for _, spec, _ in ins],
        out_specs=[hbm if name in ("out_in", "mix_out", "gsec_in") else near for name, *_ in outs],
        scratch_shapes=[
            pltpu.SemaphoreType.REGULAR if t == "regular" else pltpu.SemaphoreType.DMA(d) if t is None else pltpu.VMEM(d, t)
            for _, d, t in scratch
        ],
        compiler_params=pltpu.CompilerParams(vmem_limit_bytes=LIMIT, collective_id=0, has_side_effects=True),
        name="layer",
    )(*[item for _, _, item in ins])
    parts, _, gtok, *rest = results[:13]
    return finish(z, parts.reshape(W, W * z.seg, D), gtok.reshape(W * z.seg, D), *rest)


def finish_kernel(ways, steps, *refs):
    count = len(refs) // 2
    ins, outs = refs[:count], refs[count:]
    total = functools.reduce(lambda a, b: a + b, [ins[0][n].astype(f32) for n in range(ways)])
    outs[0][...] = total.astype(bf16)
    for src, dst in zip(ins[1:9], outs[1:9], strict=True):
        dst[...] = src[...].astype(f32)

    @pl.when(pl.program_id(0) == steps - 1)
    def _():
        for src, dst in zip(ins[9:11], outs[9:11], strict=True):
            dst[...] = src[0, :]
        outs[11][...] = ins[11][...]


def finish(z, parts, gtok, gate, up, down, gq, gk, gv, gout, gn1, gn2, grt):
    D, W, H = z.width, z.ways, z.hid
    steps = 8
    wide, deep = z.local * D, z.local * H
    args = [parts, gtok, gate.reshape(wide, H), up.reshape(wide, H), down.reshape(deep, D), gq, gk, gv, gout, gn1, gn2, grt]

    def rows(count, cols):
        return pl.BlockSpec((count // steps, cols), lambda i: (i, 0))

    sliced = [rows(W * z.seg, D), rows(wide, H), rows(wide, H), rows(deep, D)] + [rows(D, D)] * 4
    one = pl.BlockSpec((1, D), lambda i: (0, 0))
    flat = pl.BlockSpec((D,), lambda i: (0,))
    router = pl.BlockSpec(grt.shape, lambda i: (0, 0))
    shapes = [((W * z.seg, D), bf16), ((W * z.seg, D), f32), ((wide, H), f32), ((wide, H), f32), ((deep, D), f32)]
    shapes += [((D, D), f32)] * 4 + [((D,), f32)] * 2 + [(grt.shape, f32)]
    out, gtok, gate, up, down, gq, gk, gv, gout, gn1, gn2, grt = pl.pallas_call(
        functools.partial(finish_kernel, W, steps),
        grid=(steps,),
        out_shape=[jax.ShapeDtypeStruct(*s) for s in shapes],
        in_specs=[pl.BlockSpec((W, W * z.seg // steps, D), lambda i: (0, i, 0))] + sliced + [one, one, router],
        out_specs=[rows(W * z.seg, D)] + sliced + [flat, flat, router],
        name="finish",
    )(*args)
    places = (W, z.seg, D)
    return (out.reshape(places), gtok.reshape(places), gn1, gq, gk, gv, gout, gn2, grt.T,
            gate.reshape(z.local, D, H), up.reshape(z.local, D, H), down.reshape(z.local, H, D))


def solution(mesh):
    split, copied = P("dp", "expert", None), P()
    per_expert = P("expert", None, None)
    return jax.shard_map(
        body,
        mesh=mesh,
        in_specs=(split, P("dp", None), split, split) + (copied,) * 7 + (per_expert,) * 3,
        out_specs=(split, split) + (copied,) * 7 + (per_expert,) * 3,
        check_vma=False,
    )
```

```python
import functools
import math

import jax
import jax.numpy as jnp
import numpy as np
from jax import lax
from jax.experimental import pallas as pl
from jax.experimental.pallas import tpu as pltpu
from jax.sharding import PartitionSpec as P

HEAD_DIM = 64
PAIR = 128
epsilon = 1e-06
masked_out = -1e30
f32 = jnp.float32
bf16 = jnp.bfloat16
i32 = jnp.int32
MESH = pl.DeviceIdType.MESH
LIMIT = 63 * 1024 * 1024
EARLY, LATE = 3.3, 3.3
STEPS = ("c", "w", "n", "d", "nb", "wb", "cb")
SMALL = ("grad_query", "grad_key", "grad_value", "grad_out", "grad_norm_one", "grad_norm_two", "grad_router")


def nn(a, b):
    return lax.dot_general(a, b, (((1,), (0,)), ((), ())), preferred_element_type=f32)


def nt(a, b):
    return lax.dot_general(a, b, (((1,), (1,)), ((), ())), preferred_element_type=f32)


def tn(a, b):
    return lax.dot_general(a, b, (((0,), (0,)), ((), ())), preferred_element_type=f32)


def iota(shape, dim):
    return lax.broadcasted_iota(i32, shape, dim)


def aligned(start, size, unit):
    return pl.ds(pl.multiple_of(start, unit), size)


def rms_factor(values):
    return lax.rsqrt(jnp.mean(values * values, axis=-1, keepdims=True) + epsilon)


def norm_back(values, gain, grads):
    factor = rms_factor(values)
    unit = values * factor
    weighted = grads * gain
    inner = jnp.mean(weighted * unit, axis=-1, keepdims=True)
    return factor * (weighted - unit * inner), jnp.sum(grads * unit, axis=0, keepdims=True)


def swap_halves(values):
    half = HEAD_DIM // 2
    lane = iota(values.shape, 1) % HEAD_DIM
    return jnp.where(lane < half, pltpu.roll(values, PAIR - half, 1), pltpu.roll(values, half, 1))


def rope(values, cosine, sine):
    return values * cosine + swap_halves(values) * sine


def rope_back(values, cosine, sine):
    return values * cosine - swap_halves(values) * sine


def one_head(values, which):
    return jnp.where(iota(values.shape, 1) // HEAD_DIM == which, values, jnp.zeros_like(values))


class Place:
    def __init__(self, dp_size, ways):
        self.dp, self.col = lax.axis_index("dp"), lax.axis_index("expert")
        self.ways, self.chips = ways, dp_size // 2
        self.core, self.chip = self.dp % 2, self.dp // 2
        self.side, self.deep = self.chip % 2, self.chip // 2
        self.depth = self.chips // 2
        self.ring = self.deep + self.side * (self.chips - 1 - 2 * self.deep)
        self.group = self.ways * 2
        self.member = self.col * 2 + self.side

    def at(self, chip, core, col):
        return {"dp": chip * 2 + core, "expert": col}

    def mate(self):
        return self.at(self.chip, 1 - self.core, self.col)

    def on_ring(self, step):
        place = (self.ring + step + self.chips) % self.chips
        turn = place // (self.chips // 2)
        deep = place + turn * (self.chips - 1 - 2 * place)
        return self.at(2 * deep + turn, self.core, self.col)

    def in_column(self, step):
        return self.at(self.chip, self.core, (self.col + step) % self.ways)

    def across(self):
        return self.at(self.deep * 2 + 1 - self.side, self.core, self.col)

    def other_chip(self, step):
        return self.at((self.chip + step) % self.chips, self.core, self.col)

    def deeper(self, level):
        unit = 1 << level
        return self.at((self.deep + unit * (1 - 2 * (self.deep // unit % 2))) * 2 + self.side, self.core, self.col)

    def everyone(self):
        return (
            [self.mate()]
            + [self.in_column(s) for s in range(1, self.ways)]
            + [self.other_chip(s) for s in range(1, self.chips)]
        )


class Pump:
    def __init__(self):
        self.tasks = []

    def add(self, task, every):
        next(task)
        self.tasks.append([task, every, 0.0])

    def __call__(self, work):
        for item in list(self.tasks):
            item[2] += work
            while item[2] >= item[1] and item in self.tasks:
                item[2] -= item[1]
                if next(item[0], "end") == "end":
                    self.tasks.remove(item)

    def drain(self):
        while self.tasks:
            self(1.1)


def greet(others):
    barrier = pltpu.get_barrier_semaphore()
    for other in others:
        pl.semaphore_signal(barrier, inc=1, device_id=other, device_id_type=MESH)
    pl.semaphore_wait(barrier, len(others))


def push(src, dst, sends, recvs, index, device):
    copy = pltpu.make_async_remote_copy(
        src_ref=src, dst_ref=dst, send_sem=sends.at[index], recv_sem=recvs.at[index], device_id=device, device_id_type=MESH
    )
    copy.start()
    return copy


def ring_sums(place, sums, from_mate, arrived, sems):
    n = place.chips
    core_sems, ring_sems, gather_sems, mate_sems, free_sem = sems
    parts = range(len(sums))
    by_rows = [arrived[p].shape[3] == sums[p].shape[2] for p in parts]
    copies = []
    firsts = [push(sums[p].at[1 - place.core], from_mate[p], *core_sems, p, place.mate()) for p in parts]
    yield

    def cut(p, way, index):
        rows, cols = arrived[p].shape[2:]
        if by_rows[p]:
            return aligned((way * n + index) * rows, rows, 16), pl.ds(0, cols)
        return aligned(index * rows, rows, 16), pl.ds(way * cols, cols)

    def own(p, way, index):
        rows, cols = cut(p, way, index)
        return sums[p][place.core, rows, cols].astype(f32) + from_mate[p][rows, cols].astype(f32)

    inbound, sent = {}, {}
    for step in range(n - 1):
        for p in parts:
            if step == 0:
                firsts[p].wait()
            for way in range(2):
                sign = 1 - 2 * way
                if step > 0:
                    sent[p, way].wait_send()
                index = (place.ring - sign * (1 + step) + 2 * n) % n
                total = own(p, way, index)
                if step > 0:
                    inbound[p, way].wait_recv()
                    total = total + arrived[p][way, step - 1].astype(f32)
                rows, cols = cut(p, way, index)
                sums[p][place.core, rows, cols] = total.astype(bf16)
                here = sums[p].at[place.core, rows, cols]
                copy = push(here, arrived[p].at[way, step], *ring_sems, (p, way, step), place.on_ring(sign))
                inbound[p, way] = sent[p, way] = copy
            if step == 0 and p == parts[-1]:
                pl.semaphore_signal(free_sem, inc=1, device_id=place.mate(), device_id_type=MESH)
            yield
    pl.semaphore_wait(free_sem, 1)
    to_mate = []
    for step in range(n):
        for p in parts:
            for way in range(2):
                sign = 1 - 2 * way
                index = (place.ring - sign * step + 2 * n) % n
                rows, cols = cut(p, way, index)
                inbound[p, way].wait_recv()
                if step == 0:
                    sent[p, way].wait_send()
                    total = own(p, way, index) + arrived[p][way, n - 2].astype(f32)
                    sums[p][place.core, rows, cols] = total.astype(bf16)
                here = sums[p].at[place.core, rows, cols]
                if step < n - 1:
                    copy = push(here, here, *gather_sems, (p, way, step), place.on_ring(sign))
                    inbound[p, way] = copy
                    copies.append(copy)
                to_mate.append(push(here, here, *mate_sems, (p, way, step), place.mate()))
            yield
    for copy in copies:
        copy.wait_send()
    for copy in to_mate:
        copy.wait()
    yield


def spread_sums(place, rows, flat, mine, out, from_mate, shares, near, deeps, sems):
    core_sems, share_sems, near_sems, deep_sems, near_back, share_back, core_back = sems
    ways, chips = place.ways, place.chips
    wide = rows // ways
    piece = wide // (chips if flat else 2)
    half, away = aligned(place.core * rows, rows, 16), aligned((1 - place.core) * rows, rows, 16)

    def part(ref, index, size, base=0):
        return ref.at[aligned(base + index * size, size, 16), :]

    first = push(mine.at[away, :], from_mate, *core_sems, 0, place.mate())
    yield
    first.wait()
    mine[half, :] = (mine[half, :].astype(f32) + from_mate[...].astype(f32)).astype(bf16)
    base = place.core * rows
    copies = [
        push(part(mine, (place.col + s) % ways, wide, base), shares.at[place.col], *share_sems, s, place.in_column(s))
        for s in range(1, ways)
    ]
    yield
    shares[place.col] = part(mine, place.col, wide, base)[...]
    for copy in copies:
        copy.wait_recv()
    total = shares[0].astype(f32)
    for n in range(1, ways):
        total = total + shares[n].astype(f32)
    near[0:wide, :] = total.astype(bf16)
    if flat:
        copies += [
            push(part(near, (place.chip + s) % chips, piece), deeps.at[place.chip], *near_sems, s, place.other_chip(s))
            for s in range(1, chips)
        ]
        yield
        deeps[place.chip] = part(near, place.chip, piece)[...]
        for copy in copies[ways - 1 :]:
            copy.wait_recv()
        total = deeps[0].astype(f32)
        for n in range(1, chips):
            total = total + deeps[n].astype(f32)
        own = part(out, place.chip, piece, base + place.col * wide)
        own[...] = total.astype(bf16)
        backs = [push(own, own, *near_back, s, place.other_chip(s)) for s in range(1, chips)]
        copies += backs
        yield
        for copy in backs:
            copy.wait_recv()
    else:
        yield from halving(place, near, deeps, out, part, base, wide, piece, copies, near_sems, deep_sems, near_back)
    own = part(out, place.col, wide, base)
    gathers = [push(own, own, *share_back, s, place.in_column(s)) for s in range(1, ways)]
    yield
    for copy in gathers:
        copy.wait_recv()
    last = push(out.at[half, :], out.at[half, :], *core_back, 0, place.mate())
    yield
    for copy in copies + gathers:
        copy.wait_send()
    last.wait()
    yield


def halving(place, near, deeps, out, part, base, wide, piece, copies, near_sems, deep_sems, near_back):
    copies.append(push(part(near, 1 - place.side, piece), near.at[wide : wide + piece, :], *near_sems, 0, place.across()))
    yield
    copies[-1].wait_recv()
    total = part(near, place.side, piece)[...].astype(f32) + near[wide : wide + piece, :].astype(f32)
    deeps[0, 0] = total.astype(bf16)
    levels = place.depth.bit_length() - 1
    for n in range(levels):
        copies.append(push(deeps.at[n, 0], deeps.at[n, 1], *deep_sems, n, place.deeper(n)))
        yield
        copies[-1].wait_recv()
        total = deeps[n, 0].astype(f32) + deeps[n, 1].astype(f32)
        if n < levels - 1:
            deeps[n + 1, 0] = total.astype(bf16)
    own = part(out, place.member, piece, base)
    own[...] = total.astype(bf16)
    copies.append(push(own, own, *near_back, 0, place.across()))
    yield
    copies[-1].wait_recv()


class Sizes:
    def __init__(self, dp_size, tokens, w_router, w_gate):
        self.dp, self.ways = dp_size, tokens[0]
        self.seg, self.width = tokens[1], tokens[2]
        self.length = self.seg * self.ways
        self.experts = w_router[1]
        self.local, self.hid = w_gate[0], w_gate[2]
        self.cap = -(-max(2, 3 * self.seg // self.experts) // 16) * 16
        self.slots = self.local * self.cap
        self.per = self.ways * self.cap
        self.size = 256
        self.blocks = self.length // self.size
        self.heads = self.width // HEAD_DIM
        self.pairs = self.width // PAIR
        self.chips = dp_size // 2
        self.depth = self.chips // 2
        self.group = self.ways * 2
        self.extra = -(-(self.experts + 1) // 16) * 16
        self.tiles = 3 * self.width
        sizes = [2 * self.tiles + 3 * self.extra] + [self.tiles] * (self.pairs - 1)
        units = [32 * self.group] * (self.pairs - 1) + [32 * self.ways * self.chips]
        self.stages = [-(-size // unit) * unit // 2 for size, unit in zip(sizes, units, strict=True)]

    def plain(self, block):
        return (block + 1) * self.size <= self.length - self.seg


def series_tables(z, place, lengths_ref, cos_ref, sin_ref, opening_ref, table_ref):
    count = lengths_ref.shape[1]
    start = 0
    starts = [start]
    for n in range(count):
        start = start + lengths_ref[place.col, n]
        starts.append(start)
    pos = iota((1, z.length), 1)
    opening = jnp.zeros((1, z.length), i32)
    lane = iota((1, PAIR), 1)
    low = jnp.full((1, PAIR), 2 * z.length, i32)
    high = jnp.full((1, PAIR), 2 * z.length, i32)
    table_ref[...] = jnp.zeros_like(table_ref)
    for n, at in enumerate(starts):
        opening = jnp.maximum(opening, jnp.where(pos >= at, at, 0))
        low = jnp.where(lane == n, at, low)
        if n > 0:
            high = jnp.where(lane == n - 1, at, high)
        row = jnp.minimum(at, z.length - 1)
        table_ref[n : n + 1, :PAIR] = cos_ref[pl.ds(row, 1), :]
        table_ref[n : n + 1, PAIR:] = sin_ref[pl.ds(row, 1), :]
    opening_ref[...] = opening
    table = table_ref[...]
    parts = []
    for n in range(3):
        parts.append(table.astype(bf16))
        table = table - parts[-1].astype(f32)
    sign = jnp.where(iota((1, PAIR), 1) % HEAD_DIM < HEAD_DIM // 2, -1.0, 1.0)
    for block in range(z.blocks):
        rows = pl.ds(block * z.size, z.size)
        at = iota((z.size, PAIR), 0) + block * z.size
        picks = jnp.where((at >= low) & (at < high), 1.0, 0.0).astype(bf16)
        base = nn(picks, parts[0]) + (nn(picks, parts[1]) + nn(picks, parts[2]))
        cs, ss = base[:, :PAIR], base[:, PAIR:]
        cp, sp = cos_ref[rows, :], sin_ref[rows, :]
        cos_ref[rows, :] = cp * cs + sp * ss
        sin_ref[rows, :] = (sp * cs - cp * ss) * sign


def project(z, r, rows):
    x = r.x[rows, :].astype(f32)
    first = (x * rms_factor(x) * r.norm_one[...][None, :]).astype(bf16)
    r.first[rows, :] = first
    cosine, sine = r.cos[rows, :], r.sin[rows, :]
    raw = nn(first, r.w_qkv[...])
    for pair in range(z.pairs):
        cut = pl.ds(pair * PAIR, PAIR)
        at = pair * 3 * PAIR
        r.q[rows, cut] = rope(raw[:, at : at + PAIR], cosine, sine).astype(bf16) * HEAD_DIM ** (-0.5)
        r.k[rows, cut] = rope(raw[:, at + PAIR : at + 2 * PAIR], cosine, sine).astype(bf16)
        value = raw[:, at + 2 * PAIR : at + 3 * PAIR].astype(bf16)
        r.v[rows, cut] = value
        r.vt[cut, rows] = value.T


def bias_rows(z, r, block):
    plain = [b for b in range(z.blocks) if z.plain(b)]
    if block in plain:
        return 0, block * z.size
    row = z.size if plain else 0
    for b in range(block):
        if b not in plain:
            row += (b + 1) * z.size
    return row, 0


def bias_total(z):
    plain = [b for b in range(z.blocks) if z.plain(b)]
    return (z.size if plain else 0) + sum((b + 1) * z.size for b in range(z.blocks) if b not in plain)


def make_bias(z, r, block):
    row, low = bias_rows(z, r, block)
    count = (block + 1) * z.size - low
    keys = iota((count, z.size), 0) + low
    queries = iota((count, z.size), 1) + block * z.size
    allowed = keys <= queries
    if not z.plain(block):
        allowed = allowed & (keys >= r.opening[:, block * z.size : (block + 1) * z.size])
    r.bias[pl.ds(row, count), :] = jnp.where(allowed, 0.0, masked_out)


def scores(z, r, block, at, cut, q_head):
    row, low = bias_rows(z, r, block)
    s = nt(r.k[pl.ds(at, z.size), cut], q_head)
    if at >= low:
        s = s + r.bias[pl.ds(row + at - low, z.size), :]
    return s


def attend(z, r, block):
    keys = (block + 1) * z.size
    rows = pl.ds(block * z.size, z.size)
    for pair in range(z.pairs):
        cut = pl.ds(pair * PAIR, PAIR)
        q = r.q[rows, cut]
        outs = []
        for half in range(2):
            q_head = one_head(q, half)
            parts = [scores(z, r, block, at, cut, q_head) for at in range(0, keys, z.size)]
            peak = functools.reduce(jnp.maximum, [jnp.max(s, axis=0, keepdims=True) for s in parts])
            total = jnp.zeros((1, z.size), f32)
            for n, s in enumerate(parts):
                e = jnp.exp(s - peak)
                total = total + jnp.sum(e, axis=0, keepdims=True)
                r.p[half, n * z.size : (n + 1) * z.size, :] = e.astype(bf16)
            head = pair * 2 + half
            r.lse[pl.ds(head, 1), rows] = peak + jnp.log(total)
            o = nn(r.vt[pl.ds(head * HEAD_DIM, HEAD_DIM), :keys], r.p[half, :keys, :])
            outs.append(o * (1.0 / total))
        r.mixed[rows, cut] = jnp.concatenate(outs, axis=0).T.astype(bf16)


def routing(z, routes, second, w_router_t):
    logits = nt(w_router_t, second)
    expert = iota(logits.shape, 0)
    hits = expert == routes[0:1, :], expert == routes[1:2, :]
    l0, l1 = (jnp.sum(jnp.where(hit, logits, 0.0), axis=0, keepdims=True) for hit in hits)
    peak = jnp.maximum(l0, l1)
    e0, e1 = jnp.exp(l0 - peak), jnp.exp(l1 - peak)
    scale = 1.0 / (e0 + e1)
    return hits, (e0 * scale, e1 * scale)


def expert_group(z, r, place, owner, segs, first, last, step, slot, own):
    places = [(n, aligned(segs[n] * z.seg, z.seg, 128)) for n in range(first, last)]
    for n, rows in places:
        send_tokens(z, r, place, owner, n, rows)
    run_experts(z, r, first, last)
    for n, rows in places:
        bring_back(z, r, n, rows, step, slot, own)


def send_tokens(z, r, place, owner, n, rows):
    width, cap = z.width, z.cap
    base = place.col * z.local
    second = r.second[owner, rows, :]
    hits, gates = routing(z, r.routes[owner, :, rows], second, r.wrt[...])
    hit = hits[0] | hits[1]
    rank = nn(hit.astype(bf16), r.upper[...])
    r.slot[...] = jnp.where(hit, rank, -1.0).astype(i32)
    r.gate[...] = jnp.where(hits[0], gates[0], 0.0) + jnp.where(hits[1], gates[1], 0.0)

    def fill_table(e, carry):
        cut = aligned(e * cap, cap, 16)
        mine = iota((cap, z.seg), 0) == r.slot[pl.ds(base + e, 1), :]
        r.table[n, cut, :] = jnp.where(mine, 1.0, 0.0).astype(bf16)
        r.gslot[n, cut, 0:1] = jnp.sum(jnp.where(mine, r.gate[pl.ds(base + e, 1), :], 0.0), axis=1, keepdims=True)
        return carry

    lax.fori_loop(0, z.local, fill_table, 0)
    r.y[: z.seg, :width] = second
    r.y[: z.seg, width:] = r.cot[owner, rows, :]
    taken = nn(r.table[n], r.y[: z.seg, :]).astype(bf16)
    for e in range(z.local):
        to = pl.ds(e * z.per + n * cap, cap)
        r.sent[to, :] = taken[e * cap : (e + 1) * cap, :width]
        r.cots[to, :] = taken[e * cap : (e + 1) * cap, width:]


def run_experts(z, r, first, last):
    width, hid, cap = z.width, z.hid, z.cap
    size = (last - first) * cap

    def one_expert(e, carry):
        to = aligned(e * z.per + first * cap, size, 16)
        cut = aligned(e * cap, cap, 16)
        sent = r.sent[to, :]
        cot = r.cots[to, :].astype(f32)
        gate = jnp.concatenate([r.gslot[n, cut, 0:1] for n in range(first, last)], axis=0)
        gate_pre = nn(sent, r.wg[e])
        up_pre = nn(sent, r.wu[e])
        sigma = jax.nn.sigmoid(gate_pre)
        active = gate_pre * sigma
        hidden = (active * up_pre).astype(bf16)
        made = nn(hidden, r.wd[e]).astype(bf16).astype(f32)
        gmade = (gate * cot).astype(bf16)
        ghid = nt(gmade, r.wd[e])
        slope = sigma * (1.0 + gate_pre * (1.0 - sigma))
        dgate = (ghid * up_pre * slope).astype(bf16)
        dup = (ghid * active).astype(bf16)
        gsent = (nt(dgate, r.wg[e]) + nt(dup, r.wu[e])).astype(bf16)
        r.hidden[to, :] = hidden
        r.gmade[to, :] = gmade
        r.dgate[to, :] = dgate
        r.dup[to, :] = dup
        gg = jnp.sum(made * cot, axis=1, keepdims=True)
        weighted = (gate * made).astype(bf16)
        for n in range(first, last):
            lay = aligned(n * z.slots + e * cap, cap, 16)
            part = slice((n - first) * cap, (n - first + 1) * cap)
            r.y[lay, :width] = weighted[part]
            r.y[lay, width:] = gsent[part]
            r.gslot[n, cut, 1:2] = gg[part]
        return carry

    lax.fori_loop(0, z.local, one_expert, 0)


def bring_back(z, r, n, rows, step, slot, own):
    width, cap = z.width, z.cap
    back = tn(r.table[n], r.y[n * z.slots : (n + 1) * z.slots, :])
    r.gsec[slot, rows, :] = back[:, width:].astype(bf16)
    r.mix[rows, :] = (r.res[rows, :] + back[:, :width] if own else back[:, :width]).astype(bf16)
    for e in range(z.local):
        cut = pl.ds(e * cap, cap)
        r.gg_out[step, e : e + 1, rows] = jnp.sum(
            r.table[n, cut, :].astype(f32) * r.gslot[n, cut, 1:2], axis=0, keepdims=True
        )
    keep = pltpu.make_async_copy(r.mix.at[rows, :], r.mix_out.at[step, rows, :], r.local_sems.at[6])
    keep.start()
    keep.wait()


def through_router(z, r, rows):
    second = r.second_own(rows)
    hits, (g0, g1) = routing(z, r.routes_own(rows), second, r.wrt[...])
    gg = jnp.concatenate([r.gg_in[p, : z.local, rows] for p in range(z.ways)], axis=0)
    gg0, gg1 = (jnp.sum(jnp.where(hit, gg, 0.0), axis=0, keepdims=True) for hit in hits)
    inner = g0 * gg0 + g1 * gg1
    glog = jnp.where(hits[0], g0 * (gg0 - inner), 0.0) + jnp.where(hits[1], g1 * (gg1 - inner), 0.0)
    glog = glog.astype(bf16)
    gsec = r.gsec[0, rows, :].astype(f32)
    if z.ways > 2:
        fetch = pltpu.make_async_copy(r.gsec_in.at[:, rows, :], r.gsec_block, r.local_sems.at[7])
        fetch.start()
        fetch.wait()
    for p in range(z.ways - 1):
        gsec = gsec + (r.gsec_block[p] if z.ways > 2 else r.gsec_in[p, rows, :]).astype(f32)
    return second, glog, gsec + tn(glog, r.wrt[...])


def before_attention(z, r, pump):
    heads = (iota((8, z.width), 1) // HEAD_DIM == iota((8, z.width), 0)).astype(bf16)
    gn2 = jnp.zeros((1, z.width), f32)
    grt = jnp.zeros((z.experts, z.width), f32)
    for block in range(z.blocks):
        rows = pl.ds(block * z.size, z.size)
        second, glog, gsec = through_router(z, r, rows)
        grt = grt + nn(glog, second)
        part, gain = norm_back(r.res[rows, :], r.norm_two[...][None, :], gsec)
        gn2 = gn2 + gain
        gres = r.cot_own(rows).astype(f32) + part
        r.gres[rows, :] = gres
        ga = gres.astype(bf16)
        r.ga[rows, :] = ga
        gm = nt(ga, r.w_out[...]).astype(bf16)
        r.gm[rows, :] = gm
        prod = gm.astype(f32) * r.mixed[rows, :].astype(f32)
        high = prod.astype(bf16)
        rest = (prod - high.astype(f32)).astype(bf16)
        r.delta[:, rows] = nt(heads, high) + nt(heads, rest)
        pump(1.0)
    return gn2, grt


def attend_back(z, r, block, pair, pump):
    keys = (block + 1) * z.size
    rows = pl.ds(block * z.size, z.size)
    cut = pl.ds(pair * PAIR, PAIR)
    q, gm = r.q[rows, cut], r.gm[rows, cut]
    q_heads = [one_head(q, half) for half in range(2)]
    gm_heads = [one_head(gm, half) for half in range(2)]
    dq = []
    for half in range(2):
        head = pair * 2 + half
        lse = r.lse[pl.ds(head, 1), rows]
        delta = r.delta[pl.ds(head, 1), rows]
        for at in range(0, keys, z.size):
            cols = pl.ds(at, z.size)
            p = jnp.exp(scores(z, r, block, at, cut, q_heads[half]) - lse)
            dp = nt(r.v[cols, cut], gm_heads[half])
            r.p[half, cols, :] = p.astype(bf16)
            r.ds[half][cols, :] = (p * (dp - delta)).astype(bf16)
        dq.append(tn(r.ds[half][:keys, :], r.k[:keys, cut]))
        pump(0.22 * (block + 1))
    dv = nn(r.p[0, :keys, :], gm_heads[0]) + nn(r.p[1, :keys, :], gm_heads[1])
    dk = nn(r.ds[0][:keys, :], q_heads[0]) + nn(r.ds[1][:keys, :], q_heads[1])
    last = keys - z.size
    if block > 0:
        r.dv[:last, :] += dv[:last]
        r.dk[:last, :] += dk[:last]
    r.dv[last:keys, :] = dv[last:]
    r.dk[last:keys, :] = dk[last:]
    dq = jnp.where(iota((z.size, PAIR), 1) < HEAD_DIM, dq[0], dq[1]) * HEAD_DIM ** (-0.5)
    pump(0.25 * (block + 1))
    r.graws[pair][rows, :PAIR] = rope_back(dq, r.cos[rows, :], r.sin[rows, :]).astype(bf16)


def pair_back(z, r, pair):
    r.graws[pair][:, PAIR : 2 * PAIR] = rope_back(r.dk[...], r.cos[...], r.sin[...]).astype(bf16)
    r.graws[pair][:, 2 * PAIR :] = r.dv[...].astype(bf16)
    return tn(r.first[...], r.graws[pair][...])


def fill_tiles(z, ref, at, wide):
    for n in range(3):
        ref[pl.ds(at + n * z.width, z.width), :] = wide[:, n * PAIR : (n + 1) * PAIR].astype(bf16)


def fill_rest(z, ref, at, extra):
    if extra is not None:
        gap = jnp.zeros((z.extra - extra.shape[0], z.width), f32)
        extra = jnp.concatenate([extra, gap], axis=0).astype(bf16)
        for n in range(3):
            ref[pl.ds(at, z.extra), :] = extra[:, n * PAIR : (n + 1) * PAIR]
            at += z.extra
    if at < ref.shape[0]:
        ref[pl.ds(at, ref.shape[0] - at), :] = jnp.zeros((ref.shape[0] - at, PAIR), bf16)


class Names:
    pass


def layer_kernel(z, ins, outs, scratch, *refs):
    r = Names()
    for (name, *_), ref in zip(ins + outs + scratch, refs, strict=True):
        setattr(r, name, ref)
    place = Place(z.dp, z.ways)
    me, ways, seg = place.col, z.ways, z.seg
    peers = [(step, (me + step) % ways) for step in range(1, ways)]

    def on(col):
        return {"expert": col}

    def local_copy(src, dst, index):
        return pltpu.make_async_copy(src, dst, r.local_sems.at[index])

    own_seg = aligned(me * seg, seg, 16)
    own_lanes = aligned(me * seg, seg, 128)
    loads = [
        local_copy(r.tokens.at[me], r.x.at[own_seg, :], 0),
        local_copy(r.w_gate, r.wg, 1),
        local_copy(r.w_up, r.wu, 2),
        local_copy(r.w_down, r.wd, 3),
        local_copy(r.cotangent, r.cot.at[:, own_seg, :], 4),
        local_copy(r.routes_t, r.routes.at[:, :, own_lanes], 5),
        local_copy(r.cp, r.cos, 6),
        local_copy(r.sp, r.sin, 7),
    ]
    for copy in loads:
        copy.start()
    greet(place.everyone())

    def token_copy(step, col):
        return pltpu.make_async_remote_copy(
            src_ref=r.tokens.at[col], dst_ref=r.x.at[own_seg, :], send_sem=r.x_send.at[step], recv_sem=r.x_recv.at[step],
            device_id=on(col), device_id_type=MESH)

    def route_copy(step, col):
        return pltpu.make_async_remote_copy(
            src_ref=r.routes_t, dst_ref=r.routes.at[:, :, own_lanes], send_sem=r.rt_send.at[step], recv_sem=r.rt_recv.at[step],
            device_id=on(col), device_id_type=MESH)

    def cot_copy(row, kind, step, col):
        return pltpu.make_async_remote_copy(
            src_ref=r.cotangent.at[row], dst_ref=r.cot.at[row, own_seg, :], send_sem=r.cot_send.at[kind, step],
            recv_sem=r.cot_recv.at[kind, step], device_id=on(col), device_id_type=MESH)

    def second_copy(block, step, col):
        rows = pl.ds(block * z.size, z.size)
        return pltpu.make_async_remote_copy(
            src_ref=r.second.at[me, rows, :], dst_ref=r.second.at[me, rows, :], send_sem=r.sec_send.at[block, step],
            recv_sem=r.sec_recv.at[block, step], device_id=on(col), device_id_type=MESH)

    tokens_out = [token_copy(step, col) for step, col in peers]
    routes_out = [route_copy(step, col) for step, col in peers]
    for copy in tokens_out + routes_out:
        copy.start()

    for pair in range(z.pairs):
        cut = pl.ds(pair * PAIR, PAIR)
        for n, w in enumerate((r.w_query, r.w_key, r.w_value)):
            r.w_qkv[:, pl.ds((pair * 3 + n) * PAIR, PAIR)] = w[:, cut]
    r.wrt = r.w_router
    r.upper[...] = jnp.where(iota((seg, seg), 0) < iota((seg, seg), 1), 1.0, 0.0).astype(bf16)
    loads[6].wait()
    loads[7].wait()
    series_tables(z, place, r.lengths, r.cos, r.sin, r.opening, r.starts)
    for block in range(z.blocks):
        if not z.plain(block) or block == 0:
            make_bias(z, r, block)
    unit = min(z.size, seg)
    loads[0].wait()
    for n in range(seg // unit):
        project(z, r, aligned(me * seg + n * unit, unit, 128))
    for copy in tokens_out:
        copy.wait()
    cots_out = {}
    for step, col in peers:
        cots_out[0, step] = cot_copy(col, 0, step, col)
        cots_out[0, step].start()
    for step, col in peers:
        for n in range(seg // unit):
            project(z, r, aligned(col * seg + n * unit, unit, 128))
    seconds_out = []
    for block in range(z.blocks):
        rows = pl.ds(block * z.size, z.size)
        attend(z, r, block)
        residual = r.x[rows, :].astype(f32) + nn(r.mixed[rows, :], r.w_out[...])
        r.res[rows, :] = residual
        r.second[me, rows, :] = (residual * rms_factor(residual) * r.norm_two[...][None, :]).astype(bf16)
        for step, col in peers:
            seconds_out.append(second_copy(block, step, col))
            seconds_out[-1].start()
    for step, col in peers:
        for kind in range(1, ways):
            cots_out[kind, step] = cot_copy((col + kind) % ways, kind, step, col)
            cots_out[kind, step].start()
    for copy in loads[1:6]:
        copy.wait()
    for copy in routes_out:
        copy.wait()

    def slot_of(step):
        return (step > 0) * (1 + (step + 1) % 2) if ways > 2 else step

    def send_back(step, owner, first=0, last=ways):
        copies = []
        for n in range(first, last):
            rows = aligned((me + n) % ways * seg, seg, 16)
            copies.append(pltpu.make_async_remote_copy(
                src_ref=r.gsec.at[slot_of(step), rows, :], dst_ref=r.gsec_in.at[step - 1, rows, :], send_sem=r.back_send.at[n, step],
                recv_sem=r.back_recv.at[n, step], device_id=on(owner), device_id_type=MESH))
        if last == ways:
            copies.append(pltpu.make_async_remote_copy(
                src_ref=r.gg_out.at[step], dst_ref=r.gg_in.at[me], send_sem=r.back_send.at[ways, step],
                recv_sem=r.back_recv.at[ways, step], device_id=on(owner), device_id_type=MESH))
        return copies

    half = z.local // 2
    sums = (r.sum_gate, r.sum_up, r.sum_down)

    def weight_grads(first):
        def one(n, carry):
            e = (n + (1 - place.core) * half) % z.local
            side = e // half
            to = aligned(e * z.per, z.per, 16)
            wide, deep = aligned(e % half * z.width, z.width, 16), aligned(e % half * z.hid, z.hid, 16)
            sent, hidden = r.sent[to, :], r.hidden[to, :]
            grads = tn(sent, r.dgate[to, :]), tn(sent, r.dup[to, :]), tn(hidden, r.gmade[to, :])
            for ref, rows, grad in zip(sums, (wide, wide, deep), grads, strict=True):
                ref[side, rows, :] = (grad if first else ref[side, rows, :].astype(f32) + grad).astype(bf16)
            return carry

        return one

    ring = ring_sums(place, sums, (r.fm0, r.fm1, r.fm2), (r.ar0, r.ar1, r.ar2),
                     ((r.rc_s, r.rc_r), (r.rs_s, r.rs_r), (r.rg_s, r.rg_r), (r.rm_s, r.rm_r), r.ring_free))

    r.gg_out[...] = jnp.zeros_like(r.gg_out)
    segs = [(me + n) % ways for n in range(ways)]
    for step, col in peers:
        cot_copy(me, 0, step, col).wait_recv()
    expert_group(z, r, place, me, segs, 0, ways, 0, 0, True)
    lax.fori_loop(0, z.local, weight_grads(True), 0)

    def other_row(step, carry):
        owner = (me + step) % ways
        for block in range(z.blocks):
            second_copy(block, ways - step, owner).wait_recv()

        @pl.when(step > 2)
        def _():
            for copy in send_back(step - 2, (owner + ways - 2) % ways):
                copy.wait_send()

        expert_group(z, r, place, owner, segs, 0, 1, step, slot_of(step), False)
        for copy in send_back(step, owner, 0, 1):
            copy.start()
        for other in range(1, ways):
            cot_copy(owner, step, other, owner).wait_recv()
        expert_group(z, r, place, owner, segs, 1, ways, step, slot_of(step), False)
        for copy in send_back(step, owner, 1, ways):
            copy.start()

        @pl.when(step < ways - 1)
        def _():
            lax.fori_loop(0, z.local, weight_grads(False), 0)

        return carry

    lax.fori_loop(1, ways, other_row, 0)
    last_grads = weight_grads(False)
    lax.fori_loop(0, half, last_grads, 0)
    next(ring)
    lax.fori_loop(half, z.local, last_grads, 0)
    r.gg_in[me] = r.gg_out[0]
    pump = Pump()
    ring_stores = [local_copy(sums[n], (r.grad_gate, r.grad_up, r.grad_down)[n], 1 + n) for n in range(3)]

    def ring_and_store():
        yield from ring
        for copy in ring_stores:
            copy.start()
        yield

    pump.tasks.append([ring_and_store(), 1.05, 0.0])
    pump(6.4)
    for step, owner in peers:
        for copy in send_back(step, owner):
            copy.wait_recv()
            if step > ways - 3:
                copy.wait_send()
    keep_outs = []
    for n in range(ways):
        keep_outs.append(local_copy(r.mix_out.at[n, own_seg, :], r.out_in.at[me, (me + n) % ways], 8 + n))
        keep_outs[-1].start()
    outs_sent = []

    def send_outputs():
        chunk = max(seg // 4, 16)
        for step, col in peers:
            for n in range(ways):
                for m in range(seg // chunk):
                    copy = pltpu.make_async_remote_copy(
                        src_ref=r.mix_out.at[n, aligned(col * seg + m * chunk, chunk, 16), :],
                        dst_ref=r.out_in.at[me, (me + n) % ways, pl.ds(m * chunk, chunk), :],
                        send_sem=r.out_send.at[n, step, m], recv_sem=r.out_recv.at[n, step, m], device_id=on(col), device_id_type=MESH)
                    copy.start()
                    outs_sent.append(copy)
                    yield

    pump.add(send_outputs(), 3.0 / max(1, ways - 1) ** 2)
    r.second_own = lambda rows: r.second[me, rows, :]
    r.routes_own = lambda rows: r.routes[me, :, rows]
    r.cot_own = lambda rows: r.cot[me, rows, :]

    def stage(n):
        own = [getattr(r, f"st{n}_{part}") for part in ("send", "out", "mate", "shares", "near", "deeps")]
        sems = [(getattr(r, f"st{n}_{k}s"), getattr(r, f"st{n}_{k}r")) for k in STEPS]
        return spread_sums(place, z.stages[n], n == z.pairs - 1, *own, sems)

    grads_sent = []

    r.gres, r.gtok = r.res, r.sent.at[: z.length, :]
    r.ga, r.gm = r.sent.at[: z.length, :], r.cots.at[: z.length, :]
    r.graws = [r.gmade.at[: z.length, :], r.hidden.at[: z.length, : z.width], r.dgate.at[: z.length, : z.width]]
    r.ds = [r.dup.at[: z.length, : z.size], r.dup.at[: z.length, z.size : 2 * z.size]]
    gn2, grt = before_attention(z, r, pump)
    fill_tiles(z, r.st0_send, z.tiles, tn(r.mixed[...], r.ga[...]))
    fill_rest(z, r.st0_send, 2 * z.tiles, jnp.concatenate([grt, gn2], axis=0))
    for pair in range(z.pairs):
        for block in range(z.blocks):
            attend_back(z, r, block, pair, pump)
        wide = pair_back(z, r, pair)
        send = getattr(r, f"st{pair}_send")
        fill_tiles(z, send, 0, wide)
        if pair > 0:
            fill_rest(z, send, z.tiles, None)
        if pair < z.pairs - 1:
            pump.add(stage(pair), EARLY)
    late = stage(z.pairs - 1)
    next(late)
    for step, col in peers + [(0, me)]:
        for m in range(seg // unit):
            rows = aligned(col * seg + m * unit, unit, 128)
            gfirst = functools.reduce(
                lambda a, b: a + b,
                [nt(r.graws[p][rows, :], r.w_qkv[:, pl.ds(p * 3 * PAIR, 3 * PAIR)]) for p in range(z.pairs)],
            )
            part, _ = norm_back(r.x[rows, :].astype(f32), r.norm_one[...][None, :], gfirst)
            r.gtok[rows, :] = (r.gres[rows, :] + part).astype(bf16)
            pump(0.8)
        if step == 1:
            next(late)
    for step, col in peers:
        copy = pltpu.make_async_remote_copy(
            src_ref=r.gtok.at[aligned(col * seg, seg, 16), :], dst_ref=r.grad_tokens.at[me],
            send_sem=r.gt_send.at[step], recv_sem=r.gt_recv.at[step], device_id=on(col), device_id_type=MESH)
        copy.start()
        grads_sent.append(copy)
    pump.tasks.append([late, LATE, LATE])
    own_store = local_copy(r.gtok.at[own_seg, :], r.grad_tokens.at[me], 4)
    own_store.start()
    pump.drain()
    for copy in ring_stores + [own_store]:
        copy.wait()
    for copy in keep_outs + outs_sent:
        copy.wait()
    for copy in grads_sent:
        copy.wait()
    for copy in seconds_out + list(cots_out.values()):
        copy.wait_send()
    for n in range(3):
        cut = pl.ds(n * PAIR, PAIR)
        r.grad_out[:, cut] = r.st0_out[pl.ds(z.tiles + n * z.width, z.width), :]
        extra = r.st0_out[pl.ds(2 * z.tiles + n * z.extra, z.extra), :].astype(f32)
        r.grad_router[:, cut] = extra[: z.experts]
        r.grad_norm_two[:, cut] = extra[z.experts : z.experts + 1]
    total = jnp.zeros((z.width, PAIR), f32)
    for pair in range(z.pairs):
        cut = pl.ds(pair * PAIR, PAIR)
        ref = getattr(r, f"st{pair}_out")
        for n, (grad, w) in enumerate(((r.grad_query, r.w_query), (r.grad_key, r.w_key), (r.grad_value, r.w_value))):
            tile = ref[pl.ds(n * z.width, z.width), :]
            grad[:, cut] = tile
            total = total + tile.astype(f32) * w[:, cut].astype(f32)
    r.grad_norm_one[...] = jnp.sum(total.T, axis=0, keepdims=True) / r.norm_one[...][None, :]


def rope_tables(length):
    half = HEAD_DIM // 2
    inverse = np.exp(np.arange(half) * (-2.0 * math.log(10000.0) / HEAD_DIM))
    angle = np.tile(np.arange(length)[:, None] * inverse[None, :], (1, 4))
    return np.cos(angle).astype(np.float32), np.sin(angle).astype(np.float32)


def body(tokens, lengths, routes, cotangent, norm_one, w_query, w_key, w_value, w_out, norm_two, w_router, w_gate, w_up, w_down):
    z = Sizes(lax.axis_size("dp"), tokens.shape, w_router.shape, w_gate.shape)
    assert z.ways == lax.axis_size("expert") and z.local % 2 == 0
    L, D, W, H = z.length, z.width, z.ways, z.hid
    half = z.local // 2
    cp, sp = rope_tables(L)
    hbm, near = pl.BlockSpec(memory_space=pl.ANY), pl.BlockSpec(memory_space=pltpu.VMEM)
    ins = [
        ("tokens", hbm, tokens), ("cotangent", hbm, cotangent), ("routes_t", hbm, routes.transpose(0, 2, 1)),
        ("lengths", pl.BlockSpec(memory_space=pltpu.SMEM), lengths), ("cp", hbm, jnp.asarray(cp)), ("sp", hbm, jnp.asarray(sp)),
        ("norm_one", near, norm_one), ("norm_two", near, norm_two),
        ("w_query", near, w_query), ("w_key", near, w_key), ("w_value", near, w_value), ("w_out", near, w_out),
        ("w_router", near, w_router.T), ("w_gate", hbm, w_gate), ("w_up", hbm, w_up), ("w_down", hbm, w_down),
    ]
    outs = [
        ("out_in", (W, W, z.seg, D), bf16), ("mix_out", (W, L, D), bf16), ("grad_tokens", (W, z.seg, D), bf16),
        ("grad_gate", (2, half * D, H), bf16), ("grad_up", (2, half * D, H), bf16), ("grad_down", (2, half * H, D), bf16),
        ("grad_query", (D, D), bf16), ("grad_key", (D, D), bf16), ("grad_value", (D, D), bf16), ("grad_out", (D, D), bf16),
        ("grad_norm_one", (1, D), f32), ("grad_norm_two", (1, D), f32), ("grad_router", (z.experts, D), f32),
    ]
    n = z.chips
    pieces = [(half * D // n, H // 2), (half * D // n, H // 2), (half * H // (2 * n), D)]
    halves = [(half * D, H), (half * D, H), (half * H, D)]
    scratch = [
        ("x", (L, D), bf16), ("cot", (W, L, D), bf16), ("routes", (W, 2, L), i32),
        ("cos", (L, PAIR), f32), ("sin", (L, PAIR), f32), ("opening", (1, L), i32), ("starts", (PAIR, 2 * PAIR), f32),
        ("w_qkv", (D, 3 * D), bf16),
        ("first", (L, D), bf16), ("q", (L, D), bf16), ("k", (L, D), bf16), ("v", (L, D), bf16), ("vt", (D, L), bf16),
        ("bias", (bias_total(z), z.size), f32), ("p", (2, L, z.size), bf16),
        ("lse", (8, L), f32), ("mixed", (L, D), bf16), ("res", (L, D), f32), ("second", (W, L, D), bf16),


        ("gsec", (min(W, 3), L, D), bf16), ("mix", (L, D), bf16),
        ("gg_out", (W, 8, L), f32), ("gg_in", (W, 8, L), f32),

    ]
    if W > 2:
        outs.append(("gsec_in", (W - 1, L, D), bf16))
        scratch.append(("gsec_block", (W - 1, z.size, D), bf16))
    else:
        scratch.append(("gsec_in", (1, L, D), bf16))
    scratch += [("sum_gate", (2,) + halves[0], bf16), ("sum_up", (2,) + halves[1], bf16), ("sum_down", (2,) + halves[2], bf16)]
    tall = max(z.local * z.per, L)
    scratch += [
        ("upper", (z.seg, z.seg), bf16), ("slot", (z.experts, z.seg), i32), ("gate", (z.experts, z.seg), f32),
        ("wg", (z.local, D, H), bf16), ("wu", (z.local, D, H), bf16), ("wd", (z.local, H, D), bf16),
        ("table", (W, z.slots, z.seg), bf16), ("gslot", (W, z.slots, 2), f32),
        ("y", (max(W * z.slots, z.seg), 2 * D), bf16), ("delta", (8, L), f32), ("dk", (L, PAIR), f32), ("dv", (L, PAIR), f32),
        ("sent", (tall, D), bf16), ("cots", (tall, D), bf16), ("gmade", (tall, D), bf16),
        ("hidden", (tall, H), bf16), ("dgate", (tall, H), bf16), ("dup", (tall, H), bf16),
    ]
    for m in range(3):
        scratch.append((f"fm{m}", halves[m], bf16))
        scratch.append((f"ar{m}", (2, n - 1) + pieces[m], bf16))
    levels = z.depth.bit_length() - 1
    for m, rows in enumerate(z.stages):
        wide = rows // W
        piece = wide // (z.chips if m == z.pairs - 1 else 2)
        deeps = (z.chips, piece, PAIR) if m == z.pairs - 1 else (levels, 2, piece, PAIR)
        scratch += [(f"st{m}_send", (2 * rows, PAIR), bf16), (f"st{m}_out", (2 * rows, PAIR), bf16), (f"st{m}_mate", (rows, PAIR), bf16),
                    (f"st{m}_shares", (W, wide, PAIR), bf16), (f"st{m}_near", (wide + piece, PAIR), bf16), (f"st{m}_deeps", deeps, bf16)]
        for kind, count in zip(STEPS, (1, W, z.chips, levels, z.chips, W, 1), strict=True):
            scratch += [(f"st{m}_{kind}s", (count,), None), (f"st{m}_{kind}r", (count,), None)]
    for name, dims in (("x", (W,)), ("rt", (W,)), ("cot", (W, W)), ("sec", (z.blocks, W)), ("back", (W + 1, W)), ("out", (W, W, 4)), ("gt", (W,))):
        scratch += [(f"{name}_send", dims, None), (f"{name}_recv", dims, None)]
    for name, dims in (("rc", (3,)), ("rs", (3, 2, n - 1)), ("rg", (3, 2, n - 1)), ("rm", (3, 2, n))):
        scratch += [(f"{name}_s", dims, None), (f"{name}_r", dims, None)]
    scratch.append(("ring_free", (), "regular"))
    scratch.append(("local_sems", (8 + W,), None))
    results = pl.pallas_call(
        functools.partial(layer_kernel, z, ins, outs, scratch),
        out_shape=[jax.ShapeDtypeStruct(dims, kind) for _, dims, kind in outs],
        in_specs=[spec for _, spec, _ in ins],
        out_specs=[near if name in SMALL else hbm for name, *_ in outs],
        scratch_shapes=[
            pltpu.SemaphoreType.REGULAR if t == "regular" else pltpu.SemaphoreType.DMA(d) if t is None else pltpu.VMEM(d, t)
            for _, d, t in scratch
        ],
        compiler_params=pltpu.CompilerParams(vmem_limit_bytes=LIMIT, collective_id=0, has_side_effects=True),
        name="layer",
    )(*[item for _, _, item in ins])
    parts, _, gtok, *rest = results[:13]
    return finish(z, parts.reshape(W, W * z.seg, D), gtok.reshape(W * z.seg, D), *rest)


def finish_kernel(ways, steps, *refs):
    count = len(refs) // 2
    ins, outs = refs[:count], refs[count:]
    total = functools.reduce(lambda a, b: a + b, [ins[0][n].astype(f32) for n in range(ways)])
    outs[0][...] = total.astype(bf16)
    for src, dst in zip(ins[1:9], outs[1:9], strict=True):
        dst[...] = src[...].astype(f32)

    @pl.when(pl.program_id(0) == steps - 1)
    def _():
        for src, dst in zip(ins[9:11], outs[9:11], strict=True):
            dst[...] = src[0, :]
        outs[11][...] = ins[11][...]


def finish(z, parts, gtok, gate, up, down, gq, gk, gv, gout, gn1, gn2, grt):
    D, W, H = z.width, z.ways, z.hid
    steps = 4
    wide, deep = z.local * D, z.local * H
    args = [parts, gtok, gate.reshape(wide, H), up.reshape(wide, H), down.reshape(deep, D), gq, gk, gv, gout, gn1, gn2, grt]

    def rows(count, cols):
        return pl.BlockSpec((count // steps, cols), lambda i: (i, 0))

    sliced = [rows(W * z.seg, D), rows(wide, H), rows(wide, H), rows(deep, D)] + [rows(D, D)] * 4
    one = pl.BlockSpec((1, D), lambda i: (0, 0))
    flat = pl.BlockSpec((D,), lambda i: (0,))
    router = pl.BlockSpec(grt.shape, lambda i: (0, 0))
    shapes = [((W * z.seg, D), bf16), ((W * z.seg, D), f32), ((wide, H), f32), ((wide, H), f32), ((deep, D), f32)]
    shapes += [((D, D), f32)] * 4 + [((D,), f32)] * 2 + [(grt.shape, f32)]
    out, gtok, gate, up, down, gq, gk, gv, gout, gn1, gn2, grt = pl.pallas_call(
        functools.partial(finish_kernel, W, steps),
        grid=(steps,),
        out_shape=[jax.ShapeDtypeStruct(*s) for s in shapes],
        in_specs=[pl.BlockSpec((W, W * z.seg // steps, D), lambda i: (0, i, 0))] + sliced + [one, one, router],
        out_specs=[rows(W * z.seg, D)] + sliced + [flat, flat, router],
        compiler_params=pltpu.CompilerParams(vmem_limit_bytes=LIMIT),
        name="finish",
    )(*args)
    places = (W, z.seg, D)
    return (out.reshape(places), gtok.reshape(places), gn1, gq, gk, gv, gout, gn2, grt.T,
            gate.reshape(z.local, D, H), up.reshape(z.local, D, H), down.reshape(z.local, H, D))


def solution(mesh):
    split, copied = P("dp", "expert", None), P()
    per_expert = P("expert", None, None)
    return jax.shard_map(
        body,
        mesh=mesh,
        in_specs=(split, P("dp", None), split, split) + (copied,) * 7 + (per_expert,) * 3,
        out_specs=(split, split) + (copied,) * 7 + (per_expert,) * 3,
        check_vma=False,
    )
```

```python
import functools
import math

import jax
import jax.numpy as jnp
import numpy as np
from jax import lax
from jax.experimental import pallas as pl
from jax.experimental.pallas import tpu as pltpu
from jax.sharding import PartitionSpec as P

HEAD_DIM = 64
PAIR = 128
epsilon = 1e-06
masked_out = -1e30
f32 = jnp.float32
bf16 = jnp.bfloat16
i32 = jnp.int32
MESH = pl.DeviceIdType.MESH
LIMIT = 63 * 1024 * 1024
EARLY, LATE = 3.3, 3.3
STEPS = ("c", "w", "n", "d", "nb", "wb", "cb")
SMALL = ("grad_query", "grad_key", "grad_value", "grad_out", "grad_norm_one", "grad_norm_two", "grad_router")


def nn(a, b):
    return lax.dot_general(a, b, (((1,), (0,)), ((), ())), preferred_element_type=f32)


def nt(a, b):
    return lax.dot_general(a, b, (((1,), (1,)), ((), ())), preferred_element_type=f32)


def tn(a, b):
    return lax.dot_general(a, b, (((0,), (0,)), ((), ())), preferred_element_type=f32)


def iota(shape, dim):
    return lax.broadcasted_iota(i32, shape, dim)


def aligned(start, size, unit):
    return pl.ds(pl.multiple_of(start, unit), size)


def rms_factor(values):
    return lax.rsqrt(jnp.mean(values * values, axis=-1, keepdims=True) + epsilon)


def norm_back(values, gain, grads):
    factor = rms_factor(values)
    unit = values * factor
    weighted = grads * gain
    inner = jnp.mean(weighted * unit, axis=-1, keepdims=True)
    return factor * (weighted - unit * inner), jnp.sum(grads * unit, axis=0, keepdims=True)


def swap_halves(values):
    half = HEAD_DIM // 2
    lane = iota(values.shape, 1) % HEAD_DIM
    return jnp.where(lane < half, pltpu.roll(values, PAIR - half, 1), pltpu.roll(values, half, 1))


def rope(values, cosine, sine):
    return values * cosine + swap_halves(values) * sine


def rope_back(values, cosine, sine):
    return values * cosine - swap_halves(values) * sine


def one_head(values, which):
    return jnp.where(iota(values.shape, 1) // HEAD_DIM == which, values, jnp.zeros_like(values))


class Place:
    def __init__(self, dp_size, ways):
        self.dp, self.col = lax.axis_index("dp"), lax.axis_index("expert")
        self.ways, self.chips = ways, dp_size // 2
        self.core, self.chip = self.dp % 2, self.dp // 2
        self.side, self.deep = self.chip % 2, self.chip // 2
        self.depth = self.chips // 2
        self.ring = self.deep + self.side * (self.chips - 1 - 2 * self.deep)
        self.group = self.ways * 2
        self.member = self.col * 2 + self.side

    def at(self, chip, core, col):
        return {"dp": chip * 2 + core, "expert": col}

    def mate(self):
        return self.at(self.chip, 1 - self.core, self.col)

    def on_ring(self, step):
        place = (self.ring + step + self.chips) % self.chips
        turn = place // (self.chips // 2)
        deep = place + turn * (self.chips - 1 - 2 * place)
        return self.at(2 * deep + turn, self.core, self.col)

    def in_column(self, step):
        return self.at(self.chip, self.core, (self.col + step) % self.ways)

    def across(self):
        return self.at(self.deep * 2 + 1 - self.side, self.core, self.col)

    def other_chip(self, step):
        return self.at((self.chip + step) % self.chips, self.core, self.col)

    def deeper(self, level):
        unit = 1 << level
        return self.at((self.deep + unit * (1 - 2 * (self.deep // unit % 2))) * 2 + self.side, self.core, self.col)

    def everyone(self):
        return (
            [self.mate()]
            + [self.in_column(s) for s in range(1, self.ways)]
            + [self.other_chip(s) for s in range(1, self.chips)]
        )


class Pump:
    def __init__(self):
        self.tasks = []

    def add(self, task, every):
        next(task)
        self.tasks.append([task, every, 0.0])

    def __call__(self, work):
        for item in list(self.tasks):
            item[2] += work
            while item[2] >= item[1] and item in self.tasks:
                item[2] -= item[1]
                if next(item[0], "end") == "end":
                    self.tasks.remove(item)

    def drain(self):
        while self.tasks:
            self(1.1)


def greet(others):
    barrier = pltpu.get_barrier_semaphore()
    for other in others:
        pl.semaphore_signal(barrier, inc=1, device_id=other, device_id_type=MESH)
    pl.semaphore_wait(barrier, len(others))


def push(src, dst, sends, recvs, index, device):
    copy = pltpu.make_async_remote_copy(
        src_ref=src, dst_ref=dst, send_sem=sends.at[index], recv_sem=recvs.at[index], device_id=device, device_id_type=MESH
    )
    copy.start()
    return copy


def ring_sums(place, sums, from_mate, arrived, sems):
    n = place.chips
    core_sems, ring_sems, gather_sems, mate_sems, free_sem = sems
    parts = range(len(sums))
    by_rows = [arrived[p].shape[3] == sums[p].shape[2] for p in parts]
    copies = []
    firsts = [push(sums[p].at[1 - place.core], from_mate[p], *core_sems, p, place.mate()) for p in parts]
    yield

    def cut(p, way, index):
        rows, cols = arrived[p].shape[2:]
        if by_rows[p]:
            return aligned((way * n + index) * rows, rows, 16), pl.ds(0, cols)
        return aligned(index * rows, rows, 16), pl.ds(way * cols, cols)

    def own(p, way, index):
        rows, cols = cut(p, way, index)
        return sums[p][place.core, rows, cols].astype(f32) + from_mate[p][rows, cols].astype(f32)

    inbound, sent = {}, {}
    for step in range(n - 1):
        for p in parts:
            if step == 0:
                firsts[p].wait()
            for way in range(2):
                sign = 1 - 2 * way
                if step > 0:
                    sent[p, way].wait_send()
                index = (place.ring - sign * (1 + step) + 2 * n) % n
                total = own(p, way, index)
                if step > 0:
                    inbound[p, way].wait_recv()
                    total = total + arrived[p][way, step - 1].astype(f32)
                rows, cols = cut(p, way, index)
                sums[p][place.core, rows, cols] = total.astype(bf16)
                here = sums[p].at[place.core, rows, cols]
                copy = push(here, arrived[p].at[way, step], *ring_sems, (p, way, step), place.on_ring(sign))
                inbound[p, way] = sent[p, way] = copy
            if step == 0 and p == parts[-1]:
                pl.semaphore_signal(free_sem, inc=1, device_id=place.mate(), device_id_type=MESH)
            yield
    pl.semaphore_wait(free_sem, 1)
    to_mate = []
    for step in range(n):
        for p in parts:
            for way in range(2):
                sign = 1 - 2 * way
                index = (place.ring - sign * step + 2 * n) % n
                rows, cols = cut(p, way, index)
                inbound[p, way].wait_recv()
                if step == 0:
                    sent[p, way].wait_send()
                    total = own(p, way, index) + arrived[p][way, n - 2].astype(f32)
                    sums[p][place.core, rows, cols] = total.astype(bf16)
                here = sums[p].at[place.core, rows, cols]
                if step < n - 1:
                    copy = push(here, here, *gather_sems, (p, way, step), place.on_ring(sign))
                    inbound[p, way] = copy
                    copies.append(copy)
                to_mate.append(push(here, here, *mate_sems, (p, way, step), place.mate()))
            yield
    for copy in copies:
        copy.wait_send()
    for copy in to_mate:
        copy.wait()
    yield


def spread_sums(place, rows, flat, mine, out, from_mate, shares, near, deeps, sems):
    core_sems, share_sems, near_sems, deep_sems, near_back, share_back, core_back = sems
    ways, chips = place.ways, place.chips
    wide = rows // ways
    piece = wide // (chips if flat else 2)
    half, away = aligned(place.core * rows, rows, 16), aligned((1 - place.core) * rows, rows, 16)

    def part(ref, index, size, base=0):
        return ref.at[aligned(base + index * size, size, 16), :]

    first = push(mine.at[away, :], from_mate, *core_sems, 0, place.mate())
    yield
    first.wait()
    mine[half, :] = (mine[half, :].astype(f32) + from_mate[...].astype(f32)).astype(bf16)
    base = place.core * rows
    copies = [
        push(part(mine, (place.col + s) % ways, wide, base), shares.at[place.col], *share_sems, s, place.in_column(s))
        for s in range(1, ways)
    ]
    yield
    shares[place.col] = part(mine, place.col, wide, base)[...]
    for copy in copies:
        copy.wait_recv()
    total = shares[0].astype(f32)
    for n in range(1, ways):
        total = total + shares[n].astype(f32)
    near[0:wide, :] = total.astype(bf16)
    if flat:
        copies += [
            push(part(near, (place.chip + s) % chips, piece), deeps.at[place.chip], *near_sems, s, place.other_chip(s))
            for s in range(1, chips)
        ]
        yield
        deeps[place.chip] = part(near, place.chip, piece)[...]
        for copy in copies[ways - 1 :]:
            copy.wait_recv()
        total = deeps[0].astype(f32)
        for n in range(1, chips):
            total = total + deeps[n].astype(f32)
        own = part(out, place.chip, piece, base + place.col * wide)
        own[...] = total.astype(bf16)
        backs = [push(own, own, *near_back, s, place.other_chip(s)) for s in range(1, chips)]
        copies += backs
        yield
        for copy in backs:
            copy.wait_recv()
    else:
        yield from halving(place, near, deeps, out, part, base, wide, piece, copies, near_sems, deep_sems, near_back)
    own = part(out, place.col, wide, base)
    gathers = [push(own, own, *share_back, s, place.in_column(s)) for s in range(1, ways)]
    yield
    for copy in gathers:
        copy.wait_recv()
    last = push(out.at[half, :], out.at[half, :], *core_back, 0, place.mate())
    yield
    for copy in copies + gathers:
        copy.wait_send()
    last.wait()
    yield


def halving(place, near, deeps, out, part, base, wide, piece, copies, near_sems, deep_sems, near_back):
    copies.append(push(part(near, 1 - place.side, piece), near.at[wide : wide + piece, :], *near_sems, 0, place.across()))
    yield
    copies[-1].wait_recv()
    total = part(near, place.side, piece)[...].astype(f32) + near[wide : wide + piece, :].astype(f32)
    deeps[0, 0] = total.astype(bf16)
    levels = place.depth.bit_length() - 1
    for n in range(levels):
        copies.append(push(deeps.at[n, 0], deeps.at[n, 1], *deep_sems, n, place.deeper(n)))
        yield
        copies[-1].wait_recv()
        total = deeps[n, 0].astype(f32) + deeps[n, 1].astype(f32)
        if n < levels - 1:
            deeps[n + 1, 0] = total.astype(bf16)
    own = part(out, place.member, piece, base)
    own[...] = total.astype(bf16)
    copies.append(push(own, own, *near_back, 0, place.across()))
    yield
    copies[-1].wait_recv()


class Sizes:
    def __init__(self, dp_size, tokens, w_router, w_gate):
        self.dp, self.ways = dp_size, tokens[0]
        self.seg, self.width = tokens[1], tokens[2]
        self.length = self.seg * self.ways
        self.experts = w_router[1]
        self.local, self.hid = w_gate[0], w_gate[2]
        self.cap = -(-max(2, 3 * self.seg // self.experts) // 16) * 16
        self.slots = self.local * self.cap
        self.per = self.ways * self.cap
        self.size = 256
        self.blocks = self.length // self.size
        self.heads = self.width // HEAD_DIM
        self.pairs = self.width // PAIR
        self.chips = dp_size // 2
        self.depth = self.chips // 2
        self.group = self.ways * 2
        self.extra = -(-(self.experts + 1) // 16) * 16
        self.tiles = 3 * self.width
        sizes = [2 * self.tiles + 3 * self.extra] + [self.tiles] * (self.pairs - 1)
        units = [32 * self.group] * (self.pairs - 1) + [32 * self.ways * self.chips]
        self.stages = [-(-size // unit) * unit // 2 for size, unit in zip(sizes, units, strict=True)]

    def plain(self, block):
        return (block + 1) * self.size <= self.length - self.seg


def series_tables(z, place, lengths_ref, cos_ref, sin_ref, opening_ref, table_ref):
    count = lengths_ref.shape[1]
    start = 0
    starts = [start]
    for n in range(count):
        start = start + lengths_ref[place.col, n]
        starts.append(start)
    pos = iota((1, z.length), 1)
    opening = jnp.zeros((1, z.length), i32)
    lane = iota((1, PAIR), 1)
    low = jnp.full((1, PAIR), 2 * z.length, i32)
    high = jnp.full((1, PAIR), 2 * z.length, i32)
    table_ref[...] = jnp.zeros_like(table_ref)
    for n, at in enumerate(starts):
        opening = jnp.maximum(opening, jnp.where(pos >= at, at, 0))
        low = jnp.where(lane == n, at, low)
        if n > 0:
            high = jnp.where(lane == n - 1, at, high)
        row = jnp.minimum(at, z.length - 1)
        table_ref[n : n + 1, :PAIR] = cos_ref[pl.ds(row, 1), :]
        table_ref[n : n + 1, PAIR:] = sin_ref[pl.ds(row, 1), :]
    opening_ref[...] = opening
    table = table_ref[...]
    parts = []
    for n in range(3):
        parts.append(table.astype(bf16))
        table = table - parts[-1].astype(f32)
    sign = jnp.where(iota((1, PAIR), 1) % HEAD_DIM < HEAD_DIM // 2, -1.0, 1.0)
    for block in range(z.blocks):
        rows = pl.ds(block * z.size, z.size)
        at = iota((z.size, PAIR), 0) + block * z.size
        picks = jnp.where((at >= low) & (at < high), 1.0, 0.0).astype(bf16)
        base = nn(picks, parts[0]) + (nn(picks, parts[1]) + nn(picks, parts[2]))
        cs, ss = base[:, :PAIR], base[:, PAIR:]
        cp, sp = cos_ref[rows, :], sin_ref[rows, :]
        cos_ref[rows, :] = cp * cs + sp * ss
        sin_ref[rows, :] = (sp * cs - cp * ss) * sign


def project(z, r, rows):
    x = r.x[rows, :].astype(f32)
    first = (x * rms_factor(x) * r.norm_one[...][None, :]).astype(bf16)
    r.first[rows, :] = first
    cosine, sine = r.cos[rows, :], r.sin[rows, :]
    raw = nn(first, r.w_qkv[...])
    for pair in range(z.pairs):
        cut = pl.ds(pair * PAIR, PAIR)
        at = pair * 3 * PAIR
        r.q[rows, cut] = rope(raw[:, at : at + PAIR], cosine, sine).astype(bf16) * HEAD_DIM ** (-0.5)
        r.k[rows, cut] = rope(raw[:, at + PAIR : at + 2 * PAIR], cosine, sine).astype(bf16)
        value = raw[:, at + 2 * PAIR : at + 3 * PAIR].astype(bf16)
        r.v[rows, cut] = value
        r.vt[cut, rows] = value.T


def bias_rows(z, r, block):
    plain = [b for b in range(z.blocks) if z.plain(b)]
    if block in plain:
        return 0, block * z.size
    row = z.size if plain else 0
    for b in range(block):
        if b not in plain:
            row += (b + 1) * z.size
    return row, 0


def bias_total(z):
    plain = [b for b in range(z.blocks) if z.plain(b)]
    return (z.size if plain else 0) + sum((b + 1) * z.size for b in range(z.blocks) if b not in plain)


def make_bias(z, r, block):
    row, low = bias_rows(z, r, block)
    count = (block + 1) * z.size - low
    keys = iota((count, z.size), 0) + low
    queries = iota((count, z.size), 1) + block * z.size
    allowed = keys <= queries
    if not z.plain(block):
        allowed = allowed & (keys >= r.opening[:, block * z.size : (block + 1) * z.size])
    r.bias[pl.ds(row, count), :] = jnp.where(allowed, 0.0, masked_out)


def scores(z, r, block, at, cut, q_head):
    row, low = bias_rows(z, r, block)
    s = nt(r.k[pl.ds(at, z.size), cut], q_head)
    if at >= low:
        s = s + r.bias[pl.ds(row + at - low, z.size), :]
    return s


def attend(z, r, block):
    keys = (block + 1) * z.size
    rows = pl.ds(block * z.size, z.size)
    for pair in range(z.pairs):
        cut = pl.ds(pair * PAIR, PAIR)
        q = r.q[rows, cut]
        outs = []
        for half in range(2):
            q_head = one_head(q, half)
            parts = [scores(z, r, block, at, cut, q_head) for at in range(0, keys, z.size)]
            peak = functools.reduce(jnp.maximum, [jnp.max(s, axis=0, keepdims=True) for s in parts])
            total = jnp.zeros((1, z.size), f32)
            for n, s in enumerate(parts):
                e = jnp.exp(s - peak)
                total = total + jnp.sum(e, axis=0, keepdims=True)
                r.p[half, n * z.size : (n + 1) * z.size, :] = e.astype(bf16)
            head = pair * 2 + half
            r.lse[pl.ds(head, 1), rows] = peak + jnp.log(total)
            o = nn(r.vt[pl.ds(head * HEAD_DIM, HEAD_DIM), :keys], r.p[half, :keys, :])
            outs.append(o * (1.0 / total))
        r.mixed[rows, cut] = jnp.concatenate(outs, axis=0).T.astype(bf16)


def routing(z, routes, second, w_router_t):
    logits = nt(w_router_t, second)
    expert = iota(logits.shape, 0)
    hits = expert == routes[0:1, :], expert == routes[1:2, :]
    l0, l1 = (jnp.sum(jnp.where(hit, logits, 0.0), axis=0, keepdims=True) for hit in hits)
    peak = jnp.maximum(l0, l1)
    e0, e1 = jnp.exp(l0 - peak), jnp.exp(l1 - peak)
    scale = 1.0 / (e0 + e1)
    return hits, (e0 * scale, e1 * scale)


def expert_group(z, r, place, owner, segs, first, last, step, slot, own):
    places = [(n, aligned(segs[n] * z.seg, z.seg, 128)) for n in range(first, last)]
    for n, rows in places:
        send_tokens(z, r, place, owner, n, rows)
    run_experts(z, r, first, last)
    for n, rows in places:
        bring_back(z, r, n, rows, step, slot, own)


def send_tokens(z, r, place, owner, n, rows):
    width, cap = z.width, z.cap
    base = place.col * z.local
    second = r.second[owner, rows, :]
    hits, gates = routing(z, r.routes[owner, :, rows], second, r.wrt[...])
    hit = hits[0] | hits[1]
    rank = nn(hit.astype(bf16), r.upper[...])
    r.slot[...] = jnp.where(hit, rank, -1.0).astype(i32)
    r.gate[...] = jnp.where(hits[0], gates[0], 0.0) + jnp.where(hits[1], gates[1], 0.0)

    def fill_table(e, carry):
        cut = aligned(e * cap, cap, 16)
        mine = iota((cap, z.seg), 0) == r.slot[pl.ds(base + e, 1), :]
        r.table[n, cut, :] = jnp.where(mine, 1.0, 0.0).astype(bf16)
        r.gslot[n, cut, 0:1] = jnp.sum(jnp.where(mine, r.gate[pl.ds(base + e, 1), :], 0.0), axis=1, keepdims=True)
        return carry

    lax.fori_loop(0, z.local, fill_table, 0, unroll=4)
    r.y[: z.seg, :width] = second
    r.y[: z.seg, width:] = r.cot[owner, rows, :]
    taken = nn(r.table[n], r.y[: z.seg, :]).astype(bf16)
    for e in range(z.local):
        to = pl.ds(e * z.per + n * cap, cap)
        r.sent[to, :] = taken[e * cap : (e + 1) * cap, :width]
        r.cots[to, :] = taken[e * cap : (e + 1) * cap, width:]


def run_experts(z, r, first, last):
    width, hid, cap = z.width, z.hid, z.cap
    size = (last - first) * cap

    def one_expert(e, carry):
        to = aligned(e * z.per + first * cap, size, 16)
        cut = aligned(e * cap, cap, 16)
        sent = r.sent[to, :]
        cot = r.cots[to, :].astype(f32)
        gate = jnp.concatenate([r.gslot[n, cut, 0:1] for n in range(first, last)], axis=0)
        gate_pre = nn(sent, r.wg[e])
        up_pre = nn(sent, r.wu[e])
        sigma = jax.nn.sigmoid(gate_pre)
        active = gate_pre * sigma
        hidden = (active * up_pre).astype(bf16)
        made = nn(hidden, r.wd[e]).astype(bf16).astype(f32)
        gmade = (gate * cot).astype(bf16)
        ghid = nt(gmade, r.wd[e])
        slope = sigma * (1.0 + gate_pre * (1.0 - sigma))
        dgate = (ghid * up_pre * slope).astype(bf16)
        dup = (ghid * active).astype(bf16)
        gsent = (nt(dgate, r.wg[e]) + nt(dup, r.wu[e])).astype(bf16)
        r.hidden[to, :] = hidden
        r.gmade[to, :] = gmade
        r.dgate[to, :] = dgate
        r.dup[to, :] = dup
        gg = jnp.sum(made * cot, axis=1, keepdims=True)
        weighted = (gate * made).astype(bf16)
        for n in range(first, last):
            lay = aligned(n * z.slots + e * cap, cap, 16)
            part = slice((n - first) * cap, (n - first + 1) * cap)
            r.y[lay, :width] = weighted[part]
            r.y[lay, width:] = gsent[part]
            r.gslot[n, cut, 1:2] = gg[part]
        return carry

    lax.fori_loop(0, z.local, one_expert, 0, unroll=2)


def bring_back(z, r, n, rows, step, slot, own):
    width, cap = z.width, z.cap
    back = tn(r.table[n], r.y[n * z.slots : (n + 1) * z.slots, :])
    r.gsec[slot, rows, :] = back[:, width:].astype(bf16)
    r.mix[rows, :] = (r.res[rows, :] + back[:, :width] if own else back[:, :width]).astype(bf16)
    for e in range(z.local):
        cut = pl.ds(e * cap, cap)
        r.gg_out[step, e : e + 1, rows] = jnp.sum(
            r.table[n, cut, :].astype(f32) * r.gslot[n, cut, 1:2], axis=0, keepdims=True
        )
    keep = pltpu.make_async_copy(r.mix.at[rows, :], r.mix_out.at[step, rows, :], r.local_sems.at[6])
    keep.start()
    keep.wait()


def through_router(z, r, rows):
    second = r.second_own(rows)
    hits, (g0, g1) = routing(z, r.routes_own(rows), second, r.wrt[...])
    gg = jnp.concatenate([r.gg_in[p, : z.local, rows] for p in range(z.ways)], axis=0)
    gg0, gg1 = (jnp.sum(jnp.where(hit, gg, 0.0), axis=0, keepdims=True) for hit in hits)
    inner = g0 * gg0 + g1 * gg1
    glog = jnp.where(hits[0], g0 * (gg0 - inner), 0.0) + jnp.where(hits[1], g1 * (gg1 - inner), 0.0)
    glog = glog.astype(bf16)
    gsec = r.gsec[0, rows, :].astype(f32)
    if z.ways > 2:
        fetch = pltpu.make_async_copy(r.gsec_in.at[:, rows, :], r.gsec_block, r.local_sems.at[7])
        fetch.start()
        fetch.wait()
    for p in range(z.ways - 1):
        gsec = gsec + (r.gsec_block[p] if z.ways > 2 else r.gsec_in[p, rows, :]).astype(f32)
    return second, glog, gsec + tn(glog, r.wrt[...])


def before_attention(z, r, pump):
    heads = (iota((8, z.width), 1) // HEAD_DIM == iota((8, z.width), 0)).astype(bf16)
    gn2 = jnp.zeros((1, z.width), f32)
    grt = jnp.zeros((z.experts, z.width), f32)
    for block in range(z.blocks):
        rows = pl.ds(block * z.size, z.size)
        second, glog, gsec = through_router(z, r, rows)
        grt = grt + nn(glog, second)
        part, gain = norm_back(r.res[rows, :], r.norm_two[...][None, :], gsec)
        gn2 = gn2 + gain
        gres = r.cot_own(rows).astype(f32) + part
        r.gres[rows, :] = gres
        ga = gres.astype(bf16)
        r.ga[rows, :] = ga
        gm = nt(ga, r.w_out[...]).astype(bf16)
        r.gm[rows, :] = gm
        prod = gm.astype(f32) * r.mixed[rows, :].astype(f32)
        high = prod.astype(bf16)
        rest = (prod - high.astype(f32)).astype(bf16)
        r.delta[:, rows] = nt(heads, high) + nt(heads, rest)
        pump(1.0)
    return gn2, grt


def attend_back(z, r, block, pair, pump):
    keys = (block + 1) * z.size
    rows = pl.ds(block * z.size, z.size)
    cut = pl.ds(pair * PAIR, PAIR)
    q, gm = r.q[rows, cut], r.gm[rows, cut]
    q_heads = [one_head(q, half) for half in range(2)]
    gm_heads = [one_head(gm, half) for half in range(2)]
    dq = []
    for half in range(2):
        head = pair * 2 + half
        lse = r.lse[pl.ds(head, 1), rows]
        delta = r.delta[pl.ds(head, 1), rows]
        for at in range(0, keys, z.size):
            cols = pl.ds(at, z.size)
            p = jnp.exp(scores(z, r, block, at, cut, q_heads[half]) - lse)
            dp = nt(r.v[cols, cut], gm_heads[half])
            r.p[half, cols, :] = p.astype(bf16)
            r.ds[half][cols, :] = (p * (dp - delta)).astype(bf16)
        dq.append(tn(r.ds[half][:keys, :], r.k[:keys, cut]))
        pump(0.22 * (block + 1))
    dv = nn(r.p[0, :keys, :], gm_heads[0]) + nn(r.p[1, :keys, :], gm_heads[1])
    dk = nn(r.ds[0][:keys, :], q_heads[0]) + nn(r.ds[1][:keys, :], q_heads[1])
    last = keys - z.size
    if block > 0:
        r.dv[:last, :] += dv[:last]
        r.dk[:last, :] += dk[:last]
    r.dv[last:keys, :] = dv[last:]
    r.dk[last:keys, :] = dk[last:]
    dq = jnp.where(iota((z.size, PAIR), 1) < HEAD_DIM, dq[0], dq[1]) * HEAD_DIM ** (-0.5)
    pump(0.25 * (block + 1))
    r.graws[pair][rows, :PAIR] = rope_back(dq, r.cos[rows, :], r.sin[rows, :]).astype(bf16)


def pair_back(z, r, pair):
    r.graws[pair][:, PAIR : 2 * PAIR] = rope_back(r.dk[...], r.cos[...], r.sin[...]).astype(bf16)
    r.graws[pair][:, 2 * PAIR :] = r.dv[...].astype(bf16)
    return tn(r.first[...], r.graws[pair][...])


def fill_tiles(z, ref, at, wide):
    for n in range(3):
        ref[pl.ds(at + n * z.width, z.width), :] = wide[:, n * PAIR : (n + 1) * PAIR].astype(bf16)


def fill_rest(z, ref, at, extra):
    if extra is not None:
        gap = jnp.zeros((z.extra - extra.shape[0], z.width), f32)
        extra = jnp.concatenate([extra, gap], axis=0).astype(bf16)
        for n in range(3):
            ref[pl.ds(at, z.extra), :] = extra[:, n * PAIR : (n + 1) * PAIR]
            at += z.extra
    if at < ref.shape[0]:
        ref[pl.ds(at, ref.shape[0] - at), :] = jnp.zeros((ref.shape[0] - at, PAIR), bf16)


class Names:
    pass


def layer_kernel(z, ins, outs, scratch, *refs):
    r = Names()
    for (name, *_), ref in zip(ins + outs + scratch, refs, strict=True):
        setattr(r, name, ref)
    place = Place(z.dp, z.ways)
    me, ways, seg = place.col, z.ways, z.seg
    peers = [(step, (me + step) % ways) for step in range(1, ways)]

    def on(col):
        return {"expert": col}

    def local_copy(src, dst, index):
        return pltpu.make_async_copy(src, dst, r.local_sems.at[index])

    own_seg = aligned(me * seg, seg, 16)
    own_lanes = aligned(me * seg, seg, 128)
    loads = [
        local_copy(r.tokens.at[me], r.x.at[own_seg, :], 0),
        local_copy(r.w_gate, r.wg, 1),
        local_copy(r.w_up, r.wu, 2),
        local_copy(r.w_down, r.wd, 3),
        local_copy(r.cotangent, r.cot.at[:, own_seg, :], 4),
        local_copy(r.routes_t, r.routes.at[:, :, own_lanes], 5),
        local_copy(r.cp, r.cos, 6),
        local_copy(r.sp, r.sin, 7),
    ]
    for copy in loads:
        copy.start()
    greet(place.everyone())

    def token_copy(step, col):
        return pltpu.make_async_remote_copy(
            src_ref=r.tokens.at[col], dst_ref=r.x.at[own_seg, :], send_sem=r.x_send.at[step], recv_sem=r.x_recv.at[step],
            device_id=on(col), device_id_type=MESH)

    def route_copy(step, col):
        return pltpu.make_async_remote_copy(
            src_ref=r.routes_t, dst_ref=r.routes.at[:, :, own_lanes], send_sem=r.rt_send.at[step], recv_sem=r.rt_recv.at[step],
            device_id=on(col), device_id_type=MESH)

    def cot_copy(row, kind, step, col):
        return pltpu.make_async_remote_copy(
            src_ref=r.cotangent.at[row], dst_ref=r.cot.at[row, own_seg, :], send_sem=r.cot_send.at[kind, step],
            recv_sem=r.cot_recv.at[kind, step], device_id=on(col), device_id_type=MESH)

    def second_copy(block, step, col):
        rows = pl.ds(block * z.size, z.size)
        return pltpu.make_async_remote_copy(
            src_ref=r.second.at[me, rows, :], dst_ref=r.second.at[me, rows, :], send_sem=r.sec_send.at[block, step],
            recv_sem=r.sec_recv.at[block, step], device_id=on(col), device_id_type=MESH)

    tokens_out = [token_copy(step, col) for step, col in peers]
    routes_out = [route_copy(step, col) for step, col in peers]
    for copy in tokens_out + routes_out:
        copy.start()

    for pair in range(z.pairs):
        cut = pl.ds(pair * PAIR, PAIR)
        for n, w in enumerate((r.w_query, r.w_key, r.w_value)):
            r.w_qkv[:, pl.ds((pair * 3 + n) * PAIR, PAIR)] = w[:, cut]
    r.wrt = r.w_router
    r.upper[...] = jnp.where(iota((seg, seg), 0) < iota((seg, seg), 1), 1.0, 0.0).astype(bf16)
    loads[6].wait()
    loads[7].wait()
    series_tables(z, place, r.lengths, r.cos, r.sin, r.opening, r.starts)
    for block in range(z.blocks):
        if not z.plain(block) or block == 0:
            make_bias(z, r, block)
    unit = min(z.size, seg)
    loads[0].wait()
    for n in range(seg // unit):
        project(z, r, aligned(me * seg + n * unit, unit, 128))
    for copy in tokens_out:
        copy.wait()
    cots_out = {}
    for step, col in peers:
        cots_out[0, step] = cot_copy(col, 0, step, col)
        cots_out[0, step].start()
    for step, col in peers:
        for n in range(seg // unit):
            project(z, r, aligned(col * seg + n * unit, unit, 128))
    seconds_out = []
    for block in range(z.blocks):
        rows = pl.ds(block * z.size, z.size)
        attend(z, r, block)
        residual = r.x[rows, :].astype(f32) + nn(r.mixed[rows, :], r.w_out[...])
        r.res[rows, :] = residual
        r.second[me, rows, :] = (residual * rms_factor(residual) * r.norm_two[...][None, :]).astype(bf16)
        for step, col in peers:
            seconds_out.append(second_copy(block, step, col))
            seconds_out[-1].start()
    for step, col in peers:
        for kind in range(1, ways):
            cots_out[kind, step] = cot_copy((col + kind) % ways, kind, step, col)
            cots_out[kind, step].start()
    for copy in loads[1:6]:
        copy.wait()
    for copy in routes_out:
        copy.wait()

    def slot_of(step):
        return (step > 0) * (1 + (step + 1) % 2) if ways > 2 else step

    def send_back(step, owner, first=0, last=ways):
        copies = []
        for n in range(first, last):
            rows = aligned((me + n) % ways * seg, seg, 16)
            copies.append(pltpu.make_async_remote_copy(
                src_ref=r.gsec.at[slot_of(step), rows, :], dst_ref=r.gsec_in.at[step - 1, rows, :], send_sem=r.back_send.at[n, step],
                recv_sem=r.back_recv.at[n, step], device_id=on(owner), device_id_type=MESH))
        if last == ways:
            copies.append(pltpu.make_async_remote_copy(
                src_ref=r.gg_out.at[step], dst_ref=r.gg_in.at[me], send_sem=r.back_send.at[ways, step],
                recv_sem=r.back_recv.at[ways, step], device_id=on(owner), device_id_type=MESH))
        return copies

    half = z.local // 2
    sums = (r.sum_gate, r.sum_up, r.sum_down)

    def weight_grads(first):
        def one(n, carry):
            e = (n + (1 - place.core) * half) % z.local
            side = e // half
            to = aligned(e * z.per, z.per, 16)
            wide, deep = aligned(e % half * z.width, z.width, 16), aligned(e % half * z.hid, z.hid, 16)
            sent, hidden = r.sent[to, :], r.hidden[to, :]
            grads = tn(sent, r.dgate[to, :]), tn(sent, r.dup[to, :]), tn(hidden, r.gmade[to, :])
            for ref, rows, grad in zip(sums, (wide, wide, deep), grads, strict=True):
                ref[side, rows, :] = (grad if first else ref[side, rows, :].astype(f32) + grad).astype(bf16)
            return carry

        return one

    ring = ring_sums(place, sums, (r.fm0, r.fm1, r.fm2), (r.ar0, r.ar1, r.ar2),
                     ((r.rc_s, r.rc_r), (r.rs_s, r.rs_r), (r.rg_s, r.rg_r), (r.rm_s, r.rm_r), r.ring_free))

    r.gg_out[...] = jnp.zeros_like(r.gg_out)
    segs = [(me + n) % ways for n in range(ways)]
    for step, col in peers:
        cot_copy(me, 0, step, col).wait_recv()
    expert_group(z, r, place, me, segs, 0, ways, 0, 0, True)
    lax.fori_loop(0, z.local, weight_grads(True), 0, unroll=2)

    def other_row(step, carry):
        owner = (me + step) % ways
        for block in range(z.blocks):
            second_copy(block, ways - step, owner).wait_recv()

        @pl.when(step > 2)
        def _():
            for copy in send_back(step - 2, (owner + ways - 2) % ways):
                copy.wait_send()

        expert_group(z, r, place, owner, segs, 0, 1, step, slot_of(step), False)
        for copy in send_back(step, owner, 0, 1):
            copy.start()
        for other in range(1, ways):
            cot_copy(owner, step, other, owner).wait_recv()
        expert_group(z, r, place, owner, segs, 1, ways, step, slot_of(step), False)
        for copy in send_back(step, owner, 1, ways):
            copy.start()

        @pl.when(step < ways - 1)
        def _():
            lax.fori_loop(0, z.local, weight_grads(False), 0)

        return carry

    lax.fori_loop(1, ways, other_row, 0)
    last_grads = weight_grads(False)
    lax.fori_loop(0, half, last_grads, 0, unroll=2)
    next(ring)
    lax.fori_loop(half, z.local, last_grads, 0, unroll=2)
    r.gg_in[me] = r.gg_out[0]
    pump = Pump()
    ring_stores = [local_copy(sums[n], (r.grad_gate, r.grad_up, r.grad_down)[n], 1 + n) for n in range(3)]

    def ring_and_store():
        yield from ring
        for copy in ring_stores:
            copy.start()
        yield

    pump.tasks.append([ring_and_store(), 1.05, 0.0])
    pump(6.4)
    for step, owner in peers:
        for copy in send_back(step, owner):
            copy.wait_recv()
            if step > ways - 3:
                copy.wait_send()
    keep_outs = []
    for n in range(ways):
        keep_outs.append(local_copy(r.mix_out.at[n, own_seg, :], r.out_in.at[me, (me + n) % ways], 8 + n))
        keep_outs[-1].start()
    outs_sent = []

    def send_outputs():
        chunk = max(seg // 4, 16)
        for step, col in peers:
            for n in range(ways):
                for m in range(seg // chunk):
                    copy = pltpu.make_async_remote_copy(
                        src_ref=r.mix_out.at[n, aligned(col * seg + m * chunk, chunk, 16), :],
                        dst_ref=r.out_in.at[me, (me + n) % ways, pl.ds(m * chunk, chunk), :],
                        send_sem=r.out_send.at[n, step, m], recv_sem=r.out_recv.at[n, step, m], device_id=on(col), device_id_type=MESH)
                    copy.start()
                    outs_sent.append(copy)
                    yield

    pump.add(send_outputs(), 3.0 / max(1, ways - 1) ** 2)
    r.second_own = lambda rows: r.second[me, rows, :]
    r.routes_own = lambda rows: r.routes[me, :, rows]
    r.cot_own = lambda rows: r.cot[me, rows, :]

    def stage(n):
        own = [getattr(r, f"st{n}_{part}") for part in ("send", "out", "mate", "shares", "near", "deeps")]
        sems = [(getattr(r, f"st{n}_{k}s"), getattr(r, f"st{n}_{k}r")) for k in STEPS]
        return spread_sums(place, z.stages[n], n == z.pairs - 1, *own, sems)

    grads_sent = []

    r.gres, r.gtok = r.res, r.sent.at[: z.length, :]
    r.ga, r.gm = r.sent.at[: z.length, :], r.cots.at[: z.length, :]
    r.graws = [r.gmade.at[: z.length, :], r.hidden.at[: z.length, : z.width], r.dgate.at[: z.length, : z.width]]
    r.ds = [r.dup.at[: z.length, : z.size], r.dup.at[: z.length, z.size : 2 * z.size]]
    gn2, grt = before_attention(z, r, pump)
    fill_tiles(z, r.st0_send, z.tiles, tn(r.mixed[...], r.ga[...]))
    fill_rest(z, r.st0_send, 2 * z.tiles, jnp.concatenate([grt, gn2], axis=0))
    for pair in range(z.pairs):
        for block in range(z.blocks):
            attend_back(z, r, block, pair, pump)
        wide = pair_back(z, r, pair)
        send = getattr(r, f"st{pair}_send")
        fill_tiles(z, send, 0, wide)
        if pair > 0:
            fill_rest(z, send, z.tiles, None)
        if pair < z.pairs - 1:
            pump.add(stage(pair), EARLY)
    late = stage(z.pairs - 1)
    next(late)
    for step, col in peers + [(0, me)]:
        for m in range(seg // unit):
            rows = aligned(col * seg + m * unit, unit, 128)
            gfirst = functools.reduce(
                lambda a, b: a + b,
                [nt(r.graws[p][rows, :], r.w_qkv[:, pl.ds(p * 3 * PAIR, 3 * PAIR)]) for p in range(z.pairs)],
            )
            part, _ = norm_back(r.x[rows, :].astype(f32), r.norm_one[...][None, :], gfirst)
            r.gtok[rows, :] = (r.gres[rows, :] + part).astype(bf16)
            pump(0.8)
        if step == 1:
            next(late)
    for step, col in peers:
        copy = pltpu.make_async_remote_copy(
            src_ref=r.gtok.at[aligned(col * seg, seg, 16), :], dst_ref=r.grad_tokens.at[me],
            send_sem=r.gt_send.at[step], recv_sem=r.gt_recv.at[step], device_id=on(col), device_id_type=MESH)
        copy.start()
        grads_sent.append(copy)
    pump.tasks.append([late, LATE, LATE])
    own_store = local_copy(r.gtok.at[own_seg, :], r.grad_tokens.at[me], 4)
    own_store.start()
    pump.drain()
    for copy in ring_stores + [own_store]:
        copy.wait()
    for copy in keep_outs + outs_sent:
        copy.wait()
    for copy in grads_sent:
        copy.wait()
    for copy in seconds_out + list(cots_out.values()):
        copy.wait_send()
    for n in range(3):
        cut = pl.ds(n * PAIR, PAIR)
        r.grad_out[:, cut] = r.st0_out[pl.ds(z.tiles + n * z.width, z.width), :]
        extra = r.st0_out[pl.ds(2 * z.tiles + n * z.extra, z.extra), :].astype(f32)
        r.grad_router[:, cut] = extra[: z.experts]
        r.grad_norm_two[:, cut] = extra[z.experts : z.experts + 1]
    total = jnp.zeros((z.width, PAIR), f32)
    for pair in range(z.pairs):
        cut = pl.ds(pair * PAIR, PAIR)
        ref = getattr(r, f"st{pair}_out")
        for n, (grad, w) in enumerate(((r.grad_query, r.w_query), (r.grad_key, r.w_key), (r.grad_value, r.w_value))):
            tile = ref[pl.ds(n * z.width, z.width), :]
            grad[:, cut] = tile
            total = total + tile.astype(f32) * w[:, cut].astype(f32)
    r.grad_norm_one[...] = jnp.sum(total.T, axis=0, keepdims=True) / r.norm_one[...][None, :]


def rope_tables(length):
    half = HEAD_DIM // 2
    inverse = np.exp(np.arange(half) * (-2.0 * math.log(10000.0) / HEAD_DIM))
    angle = np.tile(np.arange(length)[:, None] * inverse[None, :], (1, 4))
    return np.cos(angle).astype(np.float32), np.sin(angle).astype(np.float32)


def body(tokens, lengths, routes, cotangent, norm_one, w_query, w_key, w_value, w_out, norm_two, w_router, w_gate, w_up, w_down):
    z = Sizes(lax.axis_size("dp"), tokens.shape, w_router.shape, w_gate.shape)
    assert z.ways == lax.axis_size("expert") and z.local % 2 == 0
    L, D, W, H = z.length, z.width, z.ways, z.hid
    half = z.local // 2
    cp, sp = rope_tables(L)
    hbm, near = pl.BlockSpec(memory_space=pl.ANY), pl.BlockSpec(memory_space=pltpu.VMEM)
    ins = [
        ("tokens", hbm, tokens), ("cotangent", hbm, cotangent), ("routes_t", hbm, routes.transpose(0, 2, 1)),
        ("lengths", pl.BlockSpec(memory_space=pltpu.SMEM), lengths), ("cp", hbm, jnp.asarray(cp)), ("sp", hbm, jnp.asarray(sp)),
        ("norm_one", near, norm_one), ("norm_two", near, norm_two),
        ("w_query", near, w_query), ("w_key", near, w_key), ("w_value", near, w_value), ("w_out", near, w_out),
        ("w_router", near, w_router.T), ("w_gate", hbm, w_gate), ("w_up", hbm, w_up), ("w_down", hbm, w_down),
    ]
    outs = [
        ("out_in", (W, W, z.seg, D), bf16), ("mix_out", (W, L, D), bf16), ("grad_tokens", (W, z.seg, D), bf16),
        ("grad_gate", (2, half * D, H), bf16), ("grad_up", (2, half * D, H), bf16), ("grad_down", (2, half * H, D), bf16),
        ("grad_query", (D, D), bf16), ("grad_key", (D, D), bf16), ("grad_value", (D, D), bf16), ("grad_out", (D, D), bf16),
        ("grad_norm_one", (1, D), f32), ("grad_norm_two", (1, D), f32), ("grad_router", (z.experts, D), f32),
    ]
    n = z.chips
    pieces = [(half * D // n, H // 2), (half * D // n, H // 2), (half * H // (2 * n), D)]
    halves = [(half * D, H), (half * D, H), (half * H, D)]
    scratch = [
        ("x", (L, D), bf16), ("cot", (W, L, D), bf16), ("routes", (W, 2, L), i32),
        ("cos", (L, PAIR), f32), ("sin", (L, PAIR), f32), ("opening", (1, L), i32), ("starts", (PAIR, 2 * PAIR), f32),
        ("w_qkv", (D, 3 * D), bf16),
        ("first", (L, D), bf16), ("q", (L, D), bf16), ("k", (L, D), bf16), ("v", (L, D), bf16), ("vt", (D, L), bf16),
        ("bias", (bias_total(z), z.size), f32), ("p", (2, L, z.size), bf16),
        ("lse", (8, L), f32), ("mixed", (L, D), bf16), ("res", (L, D), f32), ("second", (W, L, D), bf16),


        ("gsec", (min(W, 3), L, D), bf16), ("mix", (L, D), bf16),
        ("gg_out", (W, 8, L), f32), ("gg_in", (W, 8, L), f32),

    ]
    if W > 2:
        outs.append(("gsec_in", (W - 1, L, D), bf16))
        scratch.append(("gsec_block", (W - 1, z.size, D), bf16))
    else:
        scratch.append(("gsec_in", (1, L, D), bf16))
    scratch += [("sum_gate", (2,) + halves[0], bf16), ("sum_up", (2,) + halves[1], bf16), ("sum_down", (2,) + halves[2], bf16)]
    tall = max(z.local * z.per, L)
    scratch += [
        ("upper", (z.seg, z.seg), bf16), ("slot", (z.experts, z.seg), i32), ("gate", (z.experts, z.seg), f32),
        ("wg", (z.local, D, H), bf16), ("wu", (z.local, D, H), bf16), ("wd", (z.local, H, D), bf16),
        ("table", (W, z.slots, z.seg), bf16), ("gslot", (W, z.slots, 2), f32),
        ("y", (max(W * z.slots, z.seg), 2 * D), bf16), ("delta", (8, L), f32), ("dk", (L, PAIR), f32), ("dv", (L, PAIR), f32),
        ("sent", (tall, D), bf16), ("cots", (tall, D), bf16), ("gmade", (tall, D), bf16),
        ("hidden", (tall, H), bf16), ("dgate", (tall, H), bf16), ("dup", (tall, H), bf16),
    ]
    for m in range(3):
        scratch.append((f"fm{m}", halves[m], bf16))
        scratch.append((f"ar{m}", (2, n - 1) + pieces[m], bf16))
    levels = z.depth.bit_length() - 1
    for m, rows in enumerate(z.stages):
        wide = rows // W
        piece = wide // (z.chips if m == z.pairs - 1 else 2)
        deeps = (z.chips, piece, PAIR) if m == z.pairs - 1 else (levels, 2, piece, PAIR)
        scratch += [(f"st{m}_send", (2 * rows, PAIR), bf16), (f"st{m}_out", (2 * rows, PAIR), bf16), (f"st{m}_mate", (rows, PAIR), bf16),
                    (f"st{m}_shares", (W, wide, PAIR), bf16), (f"st{m}_near", (wide + piece, PAIR), bf16), (f"st{m}_deeps", deeps, bf16)]
        for kind, count in zip(STEPS, (1, W, z.chips, levels, z.chips, W, 1), strict=True):
            scratch += [(f"st{m}_{kind}s", (count,), None), (f"st{m}_{kind}r", (count,), None)]
    for name, dims in (("x", (W,)), ("rt", (W,)), ("cot", (W, W)), ("sec", (z.blocks, W)), ("back", (W + 1, W)), ("out", (W, W, 4)), ("gt", (W,))):
        scratch += [(f"{name}_send", dims, None), (f"{name}_recv", dims, None)]
    for name, dims in (("rc", (3,)), ("rs", (3, 2, n - 1)), ("rg", (3, 2, n - 1)), ("rm", (3, 2, n))):
        scratch += [(f"{name}_s", dims, None), (f"{name}_r", dims, None)]
    scratch.append(("ring_free", (), "regular"))
    scratch.append(("local_sems", (8 + W,), None))
    results = pl.pallas_call(
        functools.partial(layer_kernel, z, ins, outs, scratch),
        out_shape=[jax.ShapeDtypeStruct(dims, kind) for _, dims, kind in outs],
        in_specs=[spec for _, spec, _ in ins],
        out_specs=[near if name in SMALL else hbm for name, *_ in outs],
        scratch_shapes=[
            pltpu.SemaphoreType.REGULAR if t == "regular" else pltpu.SemaphoreType.DMA(d) if t is None else pltpu.VMEM(d, t)
            for _, d, t in scratch
        ],
        compiler_params=pltpu.CompilerParams(vmem_limit_bytes=LIMIT, collective_id=0, has_side_effects=True),
        name="layer",
    )(*[item for _, _, item in ins])
    parts, _, gtok, *rest = results[:13]
    return finish(z, parts.reshape(W, W * z.seg, D), gtok.reshape(W * z.seg, D), *rest)


def finish_kernel(ways, steps, *refs):
    count = len(refs) // 2
    ins, outs = refs[:count], refs[count:]
    total = functools.reduce(lambda a, b: a + b, [ins[0][n].astype(f32) for n in range(ways)])
    outs[0][...] = total.astype(bf16)
    for src, dst in zip(ins[1:9], outs[1:9], strict=True):
        dst[...] = src[...].astype(f32)

    @pl.when(pl.program_id(0) == steps - 1)
    def _():
        for src, dst in zip(ins[9:11], outs[9:11], strict=True):
            dst[...] = src[0, :]
        outs[11][...] = ins[11][...]


def finish(z, parts, gtok, gate, up, down, gq, gk, gv, gout, gn1, gn2, grt):
    D, W, H = z.width, z.ways, z.hid
    steps = 4
    wide, deep = z.local * D, z.local * H
    args = [parts, gtok, gate.reshape(wide, H), up.reshape(wide, H), down.reshape(deep, D), gq, gk, gv, gout, gn1, gn2, grt]

    def rows(count, cols):
        return pl.BlockSpec((count // steps, cols), lambda i: (i, 0))

    sliced = [rows(W * z.seg, D), rows(wide, H), rows(wide, H), rows(deep, D)] + [rows(D, D)] * 4
    one = pl.BlockSpec((1, D), lambda i: (0, 0))
    flat = pl.BlockSpec((D,), lambda i: (0,))
    router = pl.BlockSpec(grt.shape, lambda i: (0, 0))
    shapes = [((W * z.seg, D), bf16), ((W * z.seg, D), f32), ((wide, H), f32), ((wide, H), f32), ((deep, D), f32)]
    shapes += [((D, D), f32)] * 4 + [((D,), f32)] * 2 + [(grt.shape, f32)]
    out, gtok, gate, up, down, gq, gk, gv, gout, gn1, gn2, grt = pl.pallas_call(
        functools.partial(finish_kernel, W, steps),
        grid=(steps,),
        out_shape=[jax.ShapeDtypeStruct(*s) for s in shapes],
        in_specs=[pl.BlockSpec((W, W * z.seg // steps, D), lambda i: (0, i, 0))] + sliced + [one, one, router],
        out_specs=[rows(W * z.seg, D)] + sliced + [flat, flat, router],
        compiler_params=pltpu.CompilerParams(vmem_limit_bytes=LIMIT),
        name="finish",
    )(*args)
    places = (W, z.seg, D)
    return (out.reshape(places), gtok.reshape(places), gn1, gq, gk, gv, gout, gn2, grt.T,
            gate.reshape(z.local, D, H), up.reshape(z.local, D, H), down.reshape(z.local, H, D))


def solution(mesh):
    split, copied = P("dp", "expert", None), P()
    per_expert = P("expert", None, None)
    return jax.shard_map(
        body,
        mesh=mesh,
        in_specs=(split, P("dp", None), split, split) + (copied,) * 7 + (per_expert,) * 3,
        out_specs=(split, split) + (copied,) * 7 + (per_expert,) * 3,
        check_vma=False,
    )
```

```python
import functools
import math

import jax
import jax.numpy as jnp
import numpy as np
from jax import lax
from jax.experimental import pallas as pl
from jax.experimental.pallas import tpu as pltpu
from jax.sharding import PartitionSpec as P

HEAD_DIM = 64
PAIR = 128
epsilon = 1e-06
masked_out = -1e30
f32 = jnp.float32
bf16 = jnp.bfloat16
i32 = jnp.int32
MESH = pl.DeviceIdType.MESH
LIMIT = 63 * 1024 * 1024
EARLY, LATE = 3.3, 3.3
STEPS = ("c", "w", "n", "d", "nb", "wb", "cb")
SMALL = ("grad_query", "grad_key", "grad_value", "grad_out", "grad_norm_one", "grad_norm_two", "grad_router")


def nn(a, b):
    return lax.dot_general(a, b, (((1,), (0,)), ((), ())), preferred_element_type=f32)


def nt(a, b):
    return lax.dot_general(a, b, (((1,), (1,)), ((), ())), preferred_element_type=f32)


def tn(a, b):
    return lax.dot_general(a, b, (((0,), (0,)), ((), ())), preferred_element_type=f32)


def iota(shape, dim):
    return lax.broadcasted_iota(i32, shape, dim)


def aligned(start, size, unit):
    return pl.ds(pl.multiple_of(start, unit), size)


def rms_factor(values):
    return lax.rsqrt(jnp.mean(values * values, axis=-1, keepdims=True) + epsilon)


def norm_back(values, gain, grads):
    factor = rms_factor(values)
    unit = values * factor
    weighted = grads * gain
    inner = jnp.mean(weighted * unit, axis=-1, keepdims=True)
    return factor * (weighted - unit * inner), jnp.sum(grads * unit, axis=0, keepdims=True)


def swap_halves(values):
    half = HEAD_DIM // 2
    lane = iota(values.shape, 1) % HEAD_DIM
    return jnp.where(lane < half, pltpu.roll(values, PAIR - half, 1), pltpu.roll(values, half, 1))


def rope(values, cosine, sine):
    return values * cosine + swap_halves(values) * sine


def rope_back(values, cosine, sine):
    return values * cosine - swap_halves(values) * sine


def one_head(values, which):
    return jnp.where(iota(values.shape, 1) // HEAD_DIM == which, values, jnp.zeros_like(values))


class Place:
    def __init__(self, dp_size, ways):
        self.dp, self.col = lax.axis_index("dp"), lax.axis_index("expert")
        self.ways, self.chips = ways, dp_size // 2
        self.core, self.chip = self.dp % 2, self.dp // 2
        self.side, self.deep = self.chip % 2, self.chip // 2
        self.depth = self.chips // 2
        self.ring = self.deep + self.side * (self.chips - 1 - 2 * self.deep)
        self.group = self.ways * 2
        self.member = self.col * 2 + self.side

    def at(self, chip, core, col):
        return {"dp": chip * 2 + core, "expert": col}

    def mate(self):
        return self.at(self.chip, 1 - self.core, self.col)

    def on_ring(self, step):
        place = (self.ring + step + self.chips) % self.chips
        turn = place // (self.chips // 2)
        deep = place + turn * (self.chips - 1 - 2 * place)
        return self.at(2 * deep + turn, self.core, self.col)

    def in_column(self, step):
        return self.at(self.chip, self.core, (self.col + step) % self.ways)

    def across(self):
        return self.at(self.deep * 2 + 1 - self.side, self.core, self.col)

    def other_chip(self, step):
        return self.at((self.chip + step) % self.chips, self.core, self.col)

    def deeper(self, level):
        unit = 1 << level
        return self.at((self.deep + unit * (1 - 2 * (self.deep // unit % 2))) * 2 + self.side, self.core, self.col)

    def everyone(self):
        return (
            [self.mate()]
            + [self.in_column(s) for s in range(1, self.ways)]
            + [self.other_chip(s) for s in range(1, self.chips)]
        )


class Pump:
    def __init__(self):
        self.tasks = []

    def add(self, task, every):
        next(task)
        self.tasks.append([task, every, 0.0])

    def __call__(self, work):
        for item in list(self.tasks):
            item[2] += work
            while item[2] >= item[1] and item in self.tasks:
                item[2] -= item[1]
                if next(item[0], "end") == "end":
                    self.tasks.remove(item)

    def drain(self):
        while self.tasks:
            self(1.1)


def greet(others):
    barrier = pltpu.get_barrier_semaphore()
    for other in others:
        pl.semaphore_signal(barrier, inc=1, device_id=other, device_id_type=MESH)
    pl.semaphore_wait(barrier, len(others))


def push(src, dst, sends, recvs, index, device):
    copy = pltpu.make_async_remote_copy(
        src_ref=src, dst_ref=dst, send_sem=sends.at[index], recv_sem=recvs.at[index], device_id=device, device_id_type=MESH
    )
    copy.start()
    return copy


def ring_sums(place, sums, from_mate, arrived, sems):
    n = place.chips
    core_sems, ring_sems, gather_sems, mate_sems, free_sem = sems
    parts = range(len(sums))
    by_rows = [arrived[p].shape[3] == sums[p].shape[2] for p in parts]
    copies = []
    firsts = [push(sums[p].at[1 - place.core], from_mate[p], *core_sems, p, place.mate()) for p in parts]
    yield

    def cut(p, way, index):
        rows, cols = arrived[p].shape[2:]
        if by_rows[p]:
            return aligned((way * n + index) * rows, rows, 16), pl.ds(0, cols)
        return aligned(index * rows, rows, 16), pl.ds(way * cols, cols)

    def own(p, way, index):
        rows, cols = cut(p, way, index)
        return sums[p][place.core, rows, cols].astype(f32) + from_mate[p][rows, cols].astype(f32)

    inbound, sent = {}, {}
    for step in range(n - 1):
        for p in parts:
            if step == 0:
                firsts[p].wait()
            for way in range(2):
                sign = 1 - 2 * way
                if step > 0:
                    sent[p, way].wait_send()
                index = (place.ring - sign * (1 + step) + 2 * n) % n
                total = own(p, way, index)
                if step > 0:
                    inbound[p, way].wait_recv()
                    total = total + arrived[p][way, step - 1].astype(f32)
                rows, cols = cut(p, way, index)
                sums[p][place.core, rows, cols] = total.astype(bf16)
                here = sums[p].at[place.core, rows, cols]
                copy = push(here, arrived[p].at[way, step], *ring_sems, (p, way, step), place.on_ring(sign))
                inbound[p, way] = sent[p, way] = copy
            if step == 0 and p == parts[-1]:
                pl.semaphore_signal(free_sem, inc=1, device_id=place.mate(), device_id_type=MESH)
            yield
    pl.semaphore_wait(free_sem, 1)
    to_mate = []
    for step in range(n):
        for p in parts:
            for way in range(2):
                sign = 1 - 2 * way
                index = (place.ring - sign * step + 2 * n) % n
                rows, cols = cut(p, way, index)
                inbound[p, way].wait_recv()
                if step == 0:
                    sent[p, way].wait_send()
                    total = own(p, way, index) + arrived[p][way, n - 2].astype(f32)
                    sums[p][place.core, rows, cols] = total.astype(bf16)
                here = sums[p].at[place.core, rows, cols]
                if step < n - 1:
                    copy = push(here, here, *gather_sems, (p, way, step), place.on_ring(sign))
                    inbound[p, way] = copy
                    copies.append(copy)
                to_mate.append(push(here, here, *mate_sems, (p, way, step), place.mate()))
            yield
    for copy in copies:
        copy.wait_send()
    for copy in to_mate:
        copy.wait()
    yield


def spread_sums(place, rows, flat, mine, out, from_mate, shares, near, deeps, sems):
    core_sems, share_sems, near_sems, deep_sems, near_back, share_back, core_back = sems
    ways, chips = place.ways, place.chips
    wide = rows // ways
    piece = wide // (chips if flat else 2)
    half, away = aligned(place.core * rows, rows, 16), aligned((1 - place.core) * rows, rows, 16)

    def part(ref, index, size, base=0):
        return ref.at[aligned(base + index * size, size, 16), :]

    first = push(mine.at[away, :], from_mate, *core_sems, 0, place.mate())
    yield
    first.wait()
    mine[half, :] = (mine[half, :].astype(f32) + from_mate[...].astype(f32)).astype(bf16)
    base = place.core * rows
    copies = [
        push(part(mine, (place.col + s) % ways, wide, base), shares.at[place.col], *share_sems, s, place.in_column(s))
        for s in range(1, ways)
    ]
    yield
    shares[place.col] = part(mine, place.col, wide, base)[...]
    for copy in copies:
        copy.wait_recv()
    total = shares[0].astype(f32)
    for n in range(1, ways):
        total = total + shares[n].astype(f32)
    near[0:wide, :] = total.astype(bf16)
    if flat:
        copies += [
            push(part(near, (place.chip + s) % chips, piece), deeps.at[place.chip], *near_sems, s, place.other_chip(s))
            for s in range(1, chips)
        ]
        yield
        deeps[place.chip] = part(near, place.chip, piece)[...]
        for copy in copies[ways - 1 :]:
            copy.wait_recv()
        total = deeps[0].astype(f32)
        for n in range(1, chips):
            total = total + deeps[n].astype(f32)
        own = part(out, place.chip, piece, base + place.col * wide)
        own[...] = total.astype(bf16)
        backs = [push(own, own, *near_back, s, place.other_chip(s)) for s in range(1, chips)]
        copies += backs
        yield
        for copy in backs:
            copy.wait_recv()
    else:
        yield from halving(place, near, deeps, out, part, base, wide, piece, copies, near_sems, deep_sems, near_back)
    own = part(out, place.col, wide, base)
    gathers = [push(own, own, *share_back, s, place.in_column(s)) for s in range(1, ways)]
    yield
    for copy in gathers:
        copy.wait_recv()
    last = push(out.at[half, :], out.at[half, :], *core_back, 0, place.mate())
    yield
    for copy in copies + gathers:
        copy.wait_send()
    last.wait()
    yield


def halving(place, near, deeps, out, part, base, wide, piece, copies, near_sems, deep_sems, near_back):
    copies.append(push(part(near, 1 - place.side, piece), near.at[wide : wide + piece, :], *near_sems, 0, place.across()))
    yield
    copies[-1].wait_recv()
    total = part(near, place.side, piece)[...].astype(f32) + near[wide : wide + piece, :].astype(f32)
    deeps[0, 0] = total.astype(bf16)
    levels = place.depth.bit_length() - 1
    for n in range(levels):
        copies.append(push(deeps.at[n, 0], deeps.at[n, 1], *deep_sems, n, place.deeper(n)))
        yield
        copies[-1].wait_recv()
        total = deeps[n, 0].astype(f32) + deeps[n, 1].astype(f32)
        if n < levels - 1:
            deeps[n + 1, 0] = total.astype(bf16)
    own = part(out, place.member, piece, base)
    own[...] = total.astype(bf16)
    copies.append(push(own, own, *near_back, 0, place.across()))
    yield
    copies[-1].wait_recv()


class Sizes:
    def __init__(self, dp_size, tokens, w_router, w_gate):
        self.dp, self.ways = dp_size, tokens[0]
        self.seg, self.width = tokens[1], tokens[2]
        self.length = self.seg * self.ways
        self.experts = w_router[1]
        self.local, self.hid = w_gate[0], w_gate[2]
        self.cap = -(-max(2, 3 * self.seg // self.experts) // 16) * 16
        self.slots = self.local * self.cap
        self.per = self.ways * self.cap
        self.size = 256
        self.blocks = self.length // self.size
        self.heads = self.width // HEAD_DIM
        self.pairs = self.width // PAIR
        self.chips = dp_size // 2
        self.depth = self.chips // 2
        self.group = self.ways * 2
        self.extra = -(-(self.experts + 1) // 16) * 16
        self.tiles = 3 * self.width
        sizes = [2 * self.tiles + 3 * self.extra] + [self.tiles] * (self.pairs - 1)
        units = [32 * self.group] * (self.pairs - 1) + [32 * self.ways * self.chips]
        self.stages = [-(-size // unit) * unit // 2 for size, unit in zip(sizes, units, strict=True)]

    def plain(self, block):
        return (block + 1) * self.size <= self.length - self.seg


def series_tables(z, place, lengths_ref, cos_ref, sin_ref, opening_ref, table_ref):
    count = lengths_ref.shape[1]
    start = 0
    starts = [start]
    for n in range(count):
        start = start + lengths_ref[place.col, n]
        starts.append(start)
    pos = iota((1, z.length), 1)
    opening = jnp.zeros((1, z.length), i32)
    lane = iota((1, PAIR), 1)
    low = jnp.full((1, PAIR), 2 * z.length, i32)
    high = jnp.full((1, PAIR), 2 * z.length, i32)
    table_ref[...] = jnp.zeros_like(table_ref)
    for n, at in enumerate(starts):
        opening = jnp.maximum(opening, jnp.where(pos >= at, at, 0))
        low = jnp.where(lane == n, at, low)
        if n > 0:
            high = jnp.where(lane == n - 1, at, high)
        row = jnp.minimum(at, z.length - 1)
        table_ref[n : n + 1, :PAIR] = cos_ref[pl.ds(row, 1), :]
        table_ref[n : n + 1, PAIR:] = sin_ref[pl.ds(row, 1), :]
    opening_ref[...] = opening
    table = table_ref[...]
    parts = []
    for n in range(3):
        parts.append(table.astype(bf16))
        table = table - parts[-1].astype(f32)
    sign = jnp.where(iota((1, PAIR), 1) % HEAD_DIM < HEAD_DIM // 2, -1.0, 1.0)
    for block in range(z.blocks):
        rows = pl.ds(block * z.size, z.size)
        at = iota((z.size, PAIR), 0) + block * z.size
        picks = jnp.where((at >= low) & (at < high), 1.0, 0.0).astype(bf16)
        base = nn(picks, parts[0]) + (nn(picks, parts[1]) + nn(picks, parts[2]))
        cs, ss = base[:, :PAIR], base[:, PAIR:]
        cp, sp = cos_ref[rows, :], sin_ref[rows, :]
        cos_ref[rows, :] = cp * cs + sp * ss
        sin_ref[rows, :] = (sp * cs - cp * ss) * sign


def project(z, r, rows):
    x = r.x[rows, :].astype(f32)
    first = (x * rms_factor(x) * r.norm_one[...][None, :]).astype(bf16)
    r.first[rows, :] = first
    cosine, sine = r.cos[rows, :], r.sin[rows, :]
    raw = nn(first, r.w_qkv[...])
    for pair in range(z.pairs):
        cut = pl.ds(pair * PAIR, PAIR)
        at = pair * 3 * PAIR
        r.q[rows, cut] = rope(raw[:, at : at + PAIR], cosine, sine).astype(bf16) * HEAD_DIM ** (-0.5)
        r.k[rows, cut] = rope(raw[:, at + PAIR : at + 2 * PAIR], cosine, sine).astype(bf16)
        value = raw[:, at + 2 * PAIR : at + 3 * PAIR].astype(bf16)
        r.v[rows, cut] = value
        r.vt[cut, rows] = value.T


def bias_rows(z, r, block):
    plain = [b for b in range(z.blocks) if z.plain(b)]
    if block in plain:
        return 0, block * z.size
    row = z.size if plain else 0
    for b in range(block):
        if b not in plain:
            row += (b + 1) * z.size
    return row, 0


def bias_total(z):
    plain = [b for b in range(z.blocks) if z.plain(b)]
    return (z.size if plain else 0) + sum((b + 1) * z.size for b in range(z.blocks) if b not in plain)


def make_bias(z, r, block):
    row, low = bias_rows(z, r, block)
    count = (block + 1) * z.size - low
    keys = iota((count, z.size), 0) + low
    queries = iota((count, z.size), 1) + block * z.size
    allowed = keys <= queries
    if not z.plain(block):
        allowed = allowed & (keys >= r.opening[:, block * z.size : (block + 1) * z.size])
    r.bias[pl.ds(row, count), :] = jnp.where(allowed, 0.0, masked_out)


def scores(z, r, block, at, cut, q_head):
    row, low = bias_rows(z, r, block)
    s = nt(r.k[pl.ds(at, z.size), cut], q_head)
    if at >= low:
        s = s + r.bias[pl.ds(row + at - low, z.size), :]
    return s


def attend(z, r, block):
    keys = (block + 1) * z.size
    rows = pl.ds(block * z.size, z.size)
    for pair in range(z.pairs):
        cut = pl.ds(pair * PAIR, PAIR)
        q = r.q[rows, cut]
        outs = []
        for half in range(2):
            q_head = one_head(q, half)
            parts = [scores(z, r, block, at, cut, q_head) for at in range(0, keys, z.size)]
            peak = functools.reduce(jnp.maximum, [jnp.max(s, axis=0, keepdims=True) for s in parts])
            total = jnp.zeros((1, z.size), f32)
            for n, s in enumerate(parts):
                e = jnp.exp(s - peak)
                total = total + jnp.sum(e, axis=0, keepdims=True)
                r.p[half, n * z.size : (n + 1) * z.size, :] = e.astype(bf16)
            head = pair * 2 + half
            r.lse[pl.ds(head, 1), rows] = peak + jnp.log(total)
            o = nn(r.vt[pl.ds(head * HEAD_DIM, HEAD_DIM), :keys], r.p[half, :keys, :])
            outs.append(o * (1.0 / total))
        r.mixed[rows, cut] = jnp.concatenate(outs, axis=0).T.astype(bf16)


def routing(z, routes, second, w_router_t):
    logits = nt(w_router_t, second)
    expert = iota(logits.shape, 0)
    hits = expert == routes[0:1, :], expert == routes[1:2, :]
    l0, l1 = (jnp.sum(jnp.where(hit, logits, 0.0), axis=0, keepdims=True) for hit in hits)
    peak = jnp.maximum(l0, l1)
    e0, e1 = jnp.exp(l0 - peak), jnp.exp(l1 - peak)
    scale = 1.0 / (e0 + e1)
    return hits, (e0 * scale, e1 * scale)


def expert_group(z, r, place, owner, segs, first, last, step, slot, own):
    places = [(n, aligned(segs[n] * z.seg, z.seg, 128)) for n in range(first, last)]
    for n, rows in places:
        send_tokens(z, r, place, owner, n, rows)
    run_experts(z, r, first, last)
    for n, rows in places:
        bring_back(z, r, n, rows, step, slot, own)


def send_tokens(z, r, place, owner, n, rows):
    width, cap = z.width, z.cap
    base = place.col * z.local
    second = r.second[owner, rows, :]
    hits, gates = routing(z, r.routes[owner, :, rows], second, r.wrt[...])
    hit = hits[0] | hits[1]
    rank = nn(hit.astype(bf16), r.upper[...])
    r.slot[...] = jnp.where(hit, rank, -1.0).astype(i32)
    r.gate[...] = jnp.where(hits[0], gates[0], 0.0) + jnp.where(hits[1], gates[1], 0.0)

    def fill_table(e, carry):
        cut = aligned(e * cap, cap, 16)
        mine = iota((cap, z.seg), 0) == r.slot[pl.ds(base + e, 1), :]
        r.table[n, cut, :] = jnp.where(mine, 1.0, 0.0).astype(bf16)
        r.gslot[n, cut, 0:1] = jnp.sum(jnp.where(mine, r.gate[pl.ds(base + e, 1), :], 0.0), axis=1, keepdims=True)
        return carry

    lax.fori_loop(0, z.local, fill_table, 0, unroll=4)
    r.y[: z.seg, :width] = second
    r.y[: z.seg, width:] = r.cot[owner, rows, :]
    taken = nn(r.table[n], r.y[: z.seg, :]).astype(bf16)
    for e in range(z.local):
        to = pl.ds(e * z.per + n * cap, cap)
        r.sent[to, :] = taken[e * cap : (e + 1) * cap, :width]
        r.cots[to, :] = taken[e * cap : (e + 1) * cap, width:]


def run_experts(z, r, first, last):
    width, hid, cap = z.width, z.hid, z.cap
    size = (last - first) * cap

    def one_expert(e, carry):
        to = aligned(e * z.per + first * cap, size, 16)
        cut = aligned(e * cap, cap, 16)
        sent = r.sent[to, :]
        cot = r.cots[to, :].astype(f32)
        gate = jnp.concatenate([r.gslot[n, cut, 0:1] for n in range(first, last)], axis=0)
        gate_pre = nn(sent, r.wg[e])
        up_pre = nn(sent, r.wu[e])
        sigma = jax.nn.sigmoid(gate_pre)
        active = gate_pre * sigma
        hidden = (active * up_pre).astype(bf16)
        made = nn(hidden, r.wd[e]).astype(bf16).astype(f32)
        gmade = (gate * cot).astype(bf16)
        ghid = nt(gmade, r.wd[e])
        slope = sigma * (1.0 + gate_pre * (1.0 - sigma))
        dgate = (ghid * up_pre * slope).astype(bf16)
        dup = (ghid * active).astype(bf16)
        gsent = (nt(dgate, r.wg[e]) + nt(dup, r.wu[e])).astype(bf16)
        r.hidden[to, :] = hidden
        r.gmade[to, :] = gmade
        r.dgate[to, :] = dgate
        r.dup[to, :] = dup
        gg = jnp.sum(made * cot, axis=1, keepdims=True)
        weighted = (gate * made).astype(bf16)
        for n in range(first, last):
            lay = aligned(n * z.slots + e * cap, cap, 16)
            part = slice((n - first) * cap, (n - first + 1) * cap)
            r.y[lay, :width] = weighted[part]
            r.y[lay, width:] = gsent[part]
            r.gslot[n, cut, 1:2] = gg[part]
        return carry

    lax.fori_loop(0, z.local, one_expert, 0, unroll=4)


def bring_back(z, r, n, rows, step, slot, own):
    width, cap = z.width, z.cap
    back = tn(r.table[n], r.y[n * z.slots : (n + 1) * z.slots, :])
    r.gsec[slot, rows, :] = back[:, width:].astype(bf16)
    r.mix[rows, :] = (r.res[rows, :] + back[:, :width] if own else back[:, :width]).astype(bf16)
    for e in range(z.local):
        cut = pl.ds(e * cap, cap)
        r.gg_out[step, e : e + 1, rows] = jnp.sum(
            r.table[n, cut, :].astype(f32) * r.gslot[n, cut, 1:2], axis=0, keepdims=True
        )
    keep = pltpu.make_async_copy(r.mix.at[rows, :], r.mix_out.at[step, rows, :], r.local_sems.at[6])
    keep.start()
    keep.wait()


def through_router(z, r, rows):
    second = r.second_own(rows)
    hits, (g0, g1) = routing(z, r.routes_own(rows), second, r.wrt[...])
    gg = jnp.concatenate([r.gg_in[p, : z.local, rows] for p in range(z.ways)], axis=0)
    gg0, gg1 = (jnp.sum(jnp.where(hit, gg, 0.0), axis=0, keepdims=True) for hit in hits)
    inner = g0 * gg0 + g1 * gg1
    glog = jnp.where(hits[0], g0 * (gg0 - inner), 0.0) + jnp.where(hits[1], g1 * (gg1 - inner), 0.0)
    glog = glog.astype(bf16)
    gsec = r.gsec[0, rows, :].astype(f32)
    if z.ways > 2:
        fetch = pltpu.make_async_copy(r.gsec_in.at[:, rows, :], r.gsec_block, r.local_sems.at[7])
        fetch.start()
        fetch.wait()
    for p in range(z.ways - 1):
        gsec = gsec + (r.gsec_block[p] if z.ways > 2 else r.gsec_in[p, rows, :]).astype(f32)
    return second, glog, gsec + tn(glog, r.wrt[...])


def before_attention(z, r, pump):
    heads = (iota((8, z.width), 1) // HEAD_DIM == iota((8, z.width), 0)).astype(bf16)
    gn2 = jnp.zeros((1, z.width), f32)
    grt = jnp.zeros((z.experts, z.width), f32)
    for block in range(z.blocks):
        rows = pl.ds(block * z.size, z.size)
        second, glog, gsec = through_router(z, r, rows)
        grt = grt + nn(glog, second)
        part, gain = norm_back(r.res[rows, :], r.norm_two[...][None, :], gsec)
        gn2 = gn2 + gain
        gres = r.cot_own(rows).astype(f32) + part
        r.gres[rows, :] = gres
        ga = gres.astype(bf16)
        r.ga[rows, :] = ga
        gm = nt(ga, r.w_out[...]).astype(bf16)
        r.gm[rows, :] = gm
        prod = gm.astype(f32) * r.mixed[rows, :].astype(f32)
        high = prod.astype(bf16)
        rest = (prod - high.astype(f32)).astype(bf16)
        r.delta[:, rows] = nt(heads, high) + nt(heads, rest)
        pump(1.0)
    return gn2, grt


def attend_back(z, r, block, pair, pump):
    keys = (block + 1) * z.size
    rows = pl.ds(block * z.size, z.size)
    cut = pl.ds(pair * PAIR, PAIR)
    q, gm = r.q[rows, cut], r.gm[rows, cut]
    q_heads = [one_head(q, half) for half in range(2)]
    gm_heads = [one_head(gm, half) for half in range(2)]
    dq = []
    for half in range(2):
        head = pair * 2 + half
        lse = r.lse[pl.ds(head, 1), rows]
        delta = r.delta[pl.ds(head, 1), rows]
        for at in range(0, keys, z.size):
            cols = pl.ds(at, z.size)
            p = jnp.exp(scores(z, r, block, at, cut, q_heads[half]) - lse)
            dp = nt(r.v[cols, cut], gm_heads[half])
            r.p[half, cols, :] = p.astype(bf16)
            r.ds[half][cols, :] = (p * (dp - delta)).astype(bf16)
        dq.append(tn(r.ds[half][:keys, :], r.k[:keys, cut]))
        pump(0.22 * (block + 1))
    dv = nn(r.p[0, :keys, :], gm_heads[0]) + nn(r.p[1, :keys, :], gm_heads[1])
    dk = nn(r.ds[0][:keys, :], q_heads[0]) + nn(r.ds[1][:keys, :], q_heads[1])
    last = keys - z.size
    if block > 0:
        r.dv[:last, :] += dv[:last]
        r.dk[:last, :] += dk[:last]
    r.dv[last:keys, :] = dv[last:]
    r.dk[last:keys, :] = dk[last:]
    dq = jnp.where(iota((z.size, PAIR), 1) < HEAD_DIM, dq[0], dq[1]) * HEAD_DIM ** (-0.5)
    pump(0.25 * (block + 1))
    r.graws[pair][rows, :PAIR] = rope_back(dq, r.cos[rows, :], r.sin[rows, :]).astype(bf16)


def pair_back(z, r, pair):
    r.graws[pair][:, PAIR : 2 * PAIR] = rope_back(r.dk[...], r.cos[...], r.sin[...]).astype(bf16)
    r.graws[pair][:, 2 * PAIR :] = r.dv[...].astype(bf16)
    return tn(r.first[...], r.graws[pair][...])


def fill_tiles(z, ref, at, wide):
    for n in range(3):
        ref[pl.ds(at + n * z.width, z.width), :] = wide[:, n * PAIR : (n + 1) * PAIR].astype(bf16)


def fill_rest(z, ref, at, extra):
    if extra is not None:
        gap = jnp.zeros((z.extra - extra.shape[0], z.width), f32)
        extra = jnp.concatenate([extra, gap], axis=0).astype(bf16)
        for n in range(3):
            ref[pl.ds(at, z.extra), :] = extra[:, n * PAIR : (n + 1) * PAIR]
            at += z.extra
    if at < ref.shape[0]:
        ref[pl.ds(at, ref.shape[0] - at), :] = jnp.zeros((ref.shape[0] - at, PAIR), bf16)


class Names:
    pass


def layer_kernel(z, ins, outs, scratch, *refs):
    r = Names()
    for (name, *_), ref in zip(ins + outs + scratch, refs, strict=True):
        setattr(r, name, ref)
    place = Place(z.dp, z.ways)
    me, ways, seg = place.col, z.ways, z.seg
    peers = [(step, (me + step) % ways) for step in range(1, ways)]

    def on(col):
        return {"expert": col}

    def local_copy(src, dst, index):
        return pltpu.make_async_copy(src, dst, r.local_sems.at[index])

    own_seg = aligned(me * seg, seg, 16)
    own_lanes = aligned(me * seg, seg, 128)
    loads = [
        local_copy(r.tokens.at[me], r.x.at[own_seg, :], 0),
        local_copy(r.w_gate, r.wg, 1),
        local_copy(r.w_up, r.wu, 2),
        local_copy(r.w_down, r.wd, 3),
        local_copy(r.cotangent, r.cot.at[:, own_seg, :], 4),
        local_copy(r.routes_t, r.routes.at[:, :, own_lanes], 5),
        local_copy(r.cp, r.cos, 6),
        local_copy(r.sp, r.sin, 7),
    ]
    for copy in loads:
        copy.start()
    greet(place.everyone())

    def token_copy(step, col):
        return pltpu.make_async_remote_copy(
            src_ref=r.tokens.at[col], dst_ref=r.x.at[own_seg, :], send_sem=r.x_send.at[step], recv_sem=r.x_recv.at[step],
            device_id=on(col), device_id_type=MESH)

    def route_copy(step, col):
        return pltpu.make_async_remote_copy(
            src_ref=r.routes_t, dst_ref=r.routes.at[:, :, own_lanes], send_sem=r.rt_send.at[step], recv_sem=r.rt_recv.at[step],
            device_id=on(col), device_id_type=MESH)

    def cot_copy(row, kind, step, col):
        return pltpu.make_async_remote_copy(
            src_ref=r.cotangent.at[row], dst_ref=r.cot.at[row, own_seg, :], send_sem=r.cot_send.at[kind, step],
            recv_sem=r.cot_recv.at[kind, step], device_id=on(col), device_id_type=MESH)

    def second_copy(block, step, col):
        rows = pl.ds(block * z.size, z.size)
        return pltpu.make_async_remote_copy(
            src_ref=r.second.at[me, rows, :], dst_ref=r.second.at[me, rows, :], send_sem=r.sec_send.at[block, step],
            recv_sem=r.sec_recv.at[block, step], device_id=on(col), device_id_type=MESH)

    tokens_out = [token_copy(step, col) for step, col in peers]
    routes_out = [route_copy(step, col) for step, col in peers]
    for copy in tokens_out + routes_out:
        copy.start()

    for pair in range(z.pairs):
        cut = pl.ds(pair * PAIR, PAIR)
        for n, w in enumerate((r.w_query, r.w_key, r.w_value)):
            r.w_qkv[:, pl.ds((pair * 3 + n) * PAIR, PAIR)] = w[:, cut]
    r.wrt = r.w_router
    r.upper[...] = jnp.where(iota((seg, seg), 0) < iota((seg, seg), 1), 1.0, 0.0).astype(bf16)
    loads[6].wait()
    loads[7].wait()
    series_tables(z, place, r.lengths, r.cos, r.sin, r.opening, r.starts)
    for block in range(z.blocks):
        if not z.plain(block) or block == 0:
            make_bias(z, r, block)
    unit = min(z.size, seg)
    loads[0].wait()
    for n in range(seg // unit):
        project(z, r, aligned(me * seg + n * unit, unit, 128))
    for copy in tokens_out:
        copy.wait()
    cots_out = {}
    for step, col in peers:
        cots_out[0, step] = cot_copy(col, 0, step, col)
        cots_out[0, step].start()
    for step, col in peers:
        for n in range(seg // unit):
            project(z, r, aligned(col * seg + n * unit, unit, 128))
    seconds_out = []
    for block in range(z.blocks):
        rows = pl.ds(block * z.size, z.size)
        attend(z, r, block)
        residual = r.x[rows, :].astype(f32) + nn(r.mixed[rows, :], r.w_out[...])
        r.res[rows, :] = residual
        r.second[me, rows, :] = (residual * rms_factor(residual) * r.norm_two[...][None, :]).astype(bf16)
        for step, col in peers:
            seconds_out.append(second_copy(block, step, col))
            seconds_out[-1].start()
    for step, col in peers:
        for kind in range(1, ways):
            cots_out[kind, step] = cot_copy((col + kind) % ways, kind, step, col)
            cots_out[kind, step].start()
    for copy in loads[1:6]:
        copy.wait()
    for copy in routes_out:
        copy.wait()

    def slot_of(step):
        return (step > 0) * (1 + (step + 1) % 2) if ways > 2 else step

    def send_back(step, owner, first=0, last=ways):
        copies = []
        for n in range(first, last):
            rows = aligned((me + n) % ways * seg, seg, 16)
            copies.append(pltpu.make_async_remote_copy(
                src_ref=r.gsec.at[slot_of(step), rows, :], dst_ref=r.gsec_in.at[step - 1, rows, :], send_sem=r.back_send.at[n, step],
                recv_sem=r.back_recv.at[n, step], device_id=on(owner), device_id_type=MESH))
        if last == ways:
            copies.append(pltpu.make_async_remote_copy(
                src_ref=r.gg_out.at[step], dst_ref=r.gg_in.at[me], send_sem=r.back_send.at[ways, step],
                recv_sem=r.back_recv.at[ways, step], device_id=on(owner), device_id_type=MESH))
        return copies

    half = z.local // 2
    sums = (r.sum_gate, r.sum_up, r.sum_down)

    def weight_grads(first):
        def one(n, carry):
            e = (n + (1 - place.core) * half) % z.local
            side = e // half
            to = aligned(e * z.per, z.per, 16)
            wide, deep = aligned(e % half * z.width, z.width, 16), aligned(e % half * z.hid, z.hid, 16)
            sent, hidden = r.sent[to, :], r.hidden[to, :]
            grads = tn(sent, r.dgate[to, :]), tn(sent, r.dup[to, :]), tn(hidden, r.gmade[to, :])
            for ref, rows, grad in zip(sums, (wide, wide, deep), grads, strict=True):
                ref[side, rows, :] = (grad if first else ref[side, rows, :].astype(f32) + grad).astype(bf16)
            return carry

        return one

    ring = ring_sums(place, sums, (r.fm0, r.fm1, r.fm2), (r.ar0, r.ar1, r.ar2),
                     ((r.rc_s, r.rc_r), (r.rs_s, r.rs_r), (r.rg_s, r.rg_r), (r.rm_s, r.rm_r), r.ring_free))

    r.gg_out[...] = jnp.zeros_like(r.gg_out)
    segs = [(me + n) % ways for n in range(ways)]
    for step, col in peers:
        cot_copy(me, 0, step, col).wait_recv()
    expert_group(z, r, place, me, segs, 0, ways, 0, 0, True)
    lax.fori_loop(0, z.local, weight_grads(True), 0, unroll=2)

    def other_row(step, carry):
        owner = (me + step) % ways
        for block in range(z.blocks):
            second_copy(block, ways - step, owner).wait_recv()

        @pl.when(step > 2)
        def _():
            for copy in send_back(step - 2, (owner + ways - 2) % ways):
                copy.wait_send()

        expert_group(z, r, place, owner, segs, 0, 1, step, slot_of(step), False)
        for copy in send_back(step, owner, 0, 1):
            copy.start()
        for other in range(1, ways):
            cot_copy(owner, step, other, owner).wait_recv()
        expert_group(z, r, place, owner, segs, 1, ways, step, slot_of(step), False)
        for copy in send_back(step, owner, 1, ways):
            copy.start()

        @pl.when(step < ways - 1)
        def _():
            lax.fori_loop(0, z.local, weight_grads(False), 0)

        return carry

    lax.fori_loop(1, ways, other_row, 0)
    last_grads = weight_grads(False)
    lax.fori_loop(0, half, last_grads, 0, unroll=2)
    next(ring)
    lax.fori_loop(half, z.local, last_grads, 0, unroll=2)
    r.gg_in[me] = r.gg_out[0]
    pump = Pump()
    ring_stores = [local_copy(sums[n], (r.grad_gate, r.grad_up, r.grad_down)[n], 1 + n) for n in range(3)]

    def ring_and_store():
        yield from ring
        for copy in ring_stores:
            copy.start()
        yield

    pump.tasks.append([ring_and_store(), 1.05, 0.0])
    pump(9.6)
    for step, owner in peers:
        for copy in send_back(step, owner):
            copy.wait_recv()
            if step > ways - 3:
                copy.wait_send()
    keep_outs = []
    for n in range(ways):
        keep_outs.append(local_copy(r.mix_out.at[n, own_seg, :], r.out_in.at[me, (me + n) % ways], 8 + n))
        keep_outs[-1].start()
    outs_sent = []

    def send_outputs():
        chunk = max(seg // 4, 16)
        for step, col in peers:
            for n in range(ways):
                for m in range(seg // chunk):
                    copy = pltpu.make_async_remote_copy(
                        src_ref=r.mix_out.at[n, aligned(col * seg + m * chunk, chunk, 16), :],
                        dst_ref=r.out_in.at[me, (me + n) % ways, pl.ds(m * chunk, chunk), :],
                        send_sem=r.out_send.at[n, step, m], recv_sem=r.out_recv.at[n, step, m], device_id=on(col), device_id_type=MESH)
                    copy.start()
                    outs_sent.append(copy)
                    yield

    pump.add(send_outputs(), 3.0 / max(1, ways - 1) ** 2)
    r.second_own = lambda rows: r.second[me, rows, :]
    r.routes_own = lambda rows: r.routes[me, :, rows]
    r.cot_own = lambda rows: r.cot[me, rows, :]

    def stage(n):
        own = [getattr(r, f"st{n}_{part}") for part in ("send", "out", "mate", "shares", "near", "deeps")]
        sems = [(getattr(r, f"st{n}_{k}s"), getattr(r, f"st{n}_{k}r")) for k in STEPS]
        return spread_sums(place, z.stages[n], n == z.pairs - 1, *own, sems)

    grads_sent = []

    r.gres, r.gtok = r.res, r.sent.at[: z.length, :]
    r.ga, r.gm = r.sent.at[: z.length, :], r.cots.at[: z.length, :]
    r.graws = [r.gmade.at[: z.length, :], r.hidden.at[: z.length, : z.width], r.dgate.at[: z.length, : z.width]]
    r.ds = [r.dup.at[: z.length, : z.size], r.dup.at[: z.length, z.size : 2 * z.size]]
    gn2, grt = before_attention(z, r, pump)
    fill_tiles(z, r.st0_send, z.tiles, tn(r.mixed[...], r.ga[...]))
    fill_rest(z, r.st0_send, 2 * z.tiles, jnp.concatenate([grt, gn2], axis=0))
    for pair in range(z.pairs):
        for block in range(z.blocks):
            attend_back(z, r, block, pair, pump)
        wide = pair_back(z, r, pair)
        send = getattr(r, f"st{pair}_send")
        fill_tiles(z, send, 0, wide)
        if pair > 0:
            fill_rest(z, send, z.tiles, None)
        if pair < z.pairs - 1:
            pump.add(stage(pair), EARLY)
    late = stage(z.pairs - 1)
    next(late)
    for step, col in peers + [(0, me)]:
        for m in range(seg // unit):
            rows = aligned(col * seg + m * unit, unit, 128)
            gfirst = functools.reduce(
                lambda a, b: a + b,
                [nt(r.graws[p][rows, :], r.w_qkv[:, pl.ds(p * 3 * PAIR, 3 * PAIR)]) for p in range(z.pairs)],
            )
            part, _ = norm_back(r.x[rows, :].astype(f32), r.norm_one[...][None, :], gfirst)
            r.gtok[rows, :] = (r.gres[rows, :] + part).astype(bf16)
            pump(0.8)
        if step == 1:
            next(late)
    for step, col in peers:
        copy = pltpu.make_async_remote_copy(
            src_ref=r.gtok.at[aligned(col * seg, seg, 16), :], dst_ref=r.grad_tokens.at[me],
            send_sem=r.gt_send.at[step], recv_sem=r.gt_recv.at[step], device_id=on(col), device_id_type=MESH)
        copy.start()
        grads_sent.append(copy)
    pump.tasks.append([late, LATE, LATE])
    own_store = local_copy(r.gtok.at[own_seg, :], r.grad_tokens.at[me], 4)
    own_store.start()
    pump.drain()
    for copy in ring_stores + [own_store]:
        copy.wait()
    for copy in keep_outs + outs_sent:
        copy.wait()
    for copy in grads_sent:
        copy.wait()
    for copy in seconds_out + list(cots_out.values()):
        copy.wait_send()
    for n in range(3):
        cut = pl.ds(n * PAIR, PAIR)
        r.grad_out[:, cut] = r.st0_out[pl.ds(z.tiles + n * z.width, z.width), :]
        extra = r.st0_out[pl.ds(2 * z.tiles + n * z.extra, z.extra), :].astype(f32)
        r.grad_router[:, cut] = extra[: z.experts]
        r.grad_norm_two[:, cut] = extra[z.experts : z.experts + 1]
    total = jnp.zeros((z.width, PAIR), f32)
    for pair in range(z.pairs):
        cut = pl.ds(pair * PAIR, PAIR)
        ref = getattr(r, f"st{pair}_out")
        for n, (grad, w) in enumerate(((r.grad_query, r.w_query), (r.grad_key, r.w_key), (r.grad_value, r.w_value))):
            tile = ref[pl.ds(n * z.width, z.width), :]
            grad[:, cut] = tile
            total = total + tile.astype(f32) * w[:, cut].astype(f32)
    r.grad_norm_one[...] = jnp.sum(total.T, axis=0, keepdims=True) / r.norm_one[...][None, :]


def rope_tables(length):
    half = HEAD_DIM // 2
    inverse = np.exp(np.arange(half) * (-2.0 * math.log(10000.0) / HEAD_DIM))
    angle = np.tile(np.arange(length)[:, None] * inverse[None, :], (1, 4))
    return np.cos(angle).astype(np.float32), np.sin(angle).astype(np.float32)


def body(tokens, lengths, routes, cotangent, norm_one, w_query, w_key, w_value, w_out, norm_two, w_router, w_gate, w_up, w_down):
    z = Sizes(lax.axis_size("dp"), tokens.shape, w_router.shape, w_gate.shape)
    assert z.ways == lax.axis_size("expert") and z.local % 2 == 0
    L, D, W, H = z.length, z.width, z.ways, z.hid
    half = z.local // 2
    cp, sp = rope_tables(L)
    hbm, near = pl.BlockSpec(memory_space=pl.ANY), pl.BlockSpec(memory_space=pltpu.VMEM)
    ins = [
        ("tokens", hbm, tokens), ("cotangent", hbm, cotangent), ("routes_t", hbm, routes.transpose(0, 2, 1)),
        ("lengths", pl.BlockSpec(memory_space=pltpu.SMEM), lengths), ("cp", hbm, jnp.asarray(cp)), ("sp", hbm, jnp.asarray(sp)),
        ("norm_one", near, norm_one), ("norm_two", near, norm_two),
        ("w_query", near, w_query), ("w_key", near, w_key), ("w_value", near, w_value), ("w_out", near, w_out),
        ("w_router", near, w_router.T), ("w_gate", hbm, w_gate), ("w_up", hbm, w_up), ("w_down", hbm, w_down),
    ]
    outs = [
        ("out_in", (W, W, z.seg, D), bf16), ("mix_out", (W, L, D), bf16), ("grad_tokens", (W, z.seg, D), bf16),
        ("grad_gate", (2, half * D, H), bf16), ("grad_up", (2, half * D, H), bf16), ("grad_down", (2, half * H, D), bf16),
        ("grad_query", (D, D), bf16), ("grad_key", (D, D), bf16), ("grad_value", (D, D), bf16), ("grad_out", (D, D), bf16),
        ("grad_norm_one", (1, D), f32), ("grad_norm_two", (1, D), f32), ("grad_router", (z.experts, D), f32),
    ]
    n = z.chips
    pieces = [(half * D // n, H // 2), (half * D // n, H // 2), (half * H // (2 * n), D)]
    halves = [(half * D, H), (half * D, H), (half * H, D)]
    scratch = [
        ("x", (L, D), bf16), ("cot", (W, L, D), bf16), ("routes", (W, 2, L), i32),
        ("cos", (L, PAIR), f32), ("sin", (L, PAIR), f32), ("opening", (1, L), i32), ("starts", (PAIR, 2 * PAIR), f32),
        ("w_qkv", (D, 3 * D), bf16),
        ("first", (L, D), bf16), ("q", (L, D), bf16), ("k", (L, D), bf16), ("v", (L, D), bf16), ("vt", (D, L), bf16),
        ("bias", (bias_total(z), z.size), f32), ("p", (2, L, z.size), bf16),
        ("lse", (8, L), f32), ("mixed", (L, D), bf16), ("res", (L, D), f32), ("second", (W, L, D), bf16),


        ("gsec", (min(W, 3), L, D), bf16), ("mix", (L, D), bf16),
        ("gg_out", (W, 8, L), f32), ("gg_in", (W, 8, L), f32),

    ]
    if W > 2:
        outs.append(("gsec_in", (W - 1, L, D), bf16))
        scratch.append(("gsec_block", (W - 1, z.size, D), bf16))
    else:
        scratch.append(("gsec_in", (1, L, D), bf16))
    scratch += [("sum_gate", (2,) + halves[0], bf16), ("sum_up", (2,) + halves[1], bf16), ("sum_down", (2,) + halves[2], bf16)]
    tall = max(z.local * z.per, L)
    scratch += [
        ("upper", (z.seg, z.seg), bf16), ("slot", (z.experts, z.seg), i32), ("gate", (z.experts, z.seg), f32),
        ("wg", (z.local, D, H), bf16), ("wu", (z.local, D, H), bf16), ("wd", (z.local, H, D), bf16),
        ("table", (W, z.slots, z.seg), bf16), ("gslot", (W, z.slots, 2), f32),
        ("y", (max(W * z.slots, z.seg), 2 * D), bf16), ("delta", (8, L), f32), ("dk", (L, PAIR), f32), ("dv", (L, PAIR), f32),
        ("sent", (tall, D), bf16), ("cots", (tall, D), bf16), ("gmade", (tall, D), bf16),
        ("hidden", (tall, H), bf16), ("dgate", (tall, H), bf16), ("dup", (tall, H), bf16),
    ]
    for m in range(3):
        scratch.append((f"fm{m}", halves[m], bf16))
        scratch.append((f"ar{m}", (2, n - 1) + pieces[m], bf16))
    levels = z.depth.bit_length() - 1
    for m, rows in enumerate(z.stages):
        wide = rows // W
        piece = wide // (z.chips if m == z.pairs - 1 else 2)
        deeps = (z.chips, piece, PAIR) if m == z.pairs - 1 else (levels, 2, piece, PAIR)
        scratch += [(f"st{m}_send", (2 * rows, PAIR), bf16), (f"st{m}_out", (2 * rows, PAIR), bf16), (f"st{m}_mate", (rows, PAIR), bf16),
                    (f"st{m}_shares", (W, wide, PAIR), bf16), (f"st{m}_near", (wide + piece, PAIR), bf16), (f"st{m}_deeps", deeps, bf16)]
        for kind, count in zip(STEPS, (1, W, z.chips, levels, z.chips, W, 1), strict=True):
            scratch += [(f"st{m}_{kind}s", (count,), None), (f"st{m}_{kind}r", (count,), None)]
    for name, dims in (("x", (W,)), ("rt", (W,)), ("cot", (W, W)), ("sec", (z.blocks, W)), ("back", (W + 1, W)), ("out", (W, W, 4)), ("gt", (W,))):
        scratch += [(f"{name}_send", dims, None), (f"{name}_recv", dims, None)]
    for name, dims in (("rc", (3,)), ("rs", (3, 2, n - 1)), ("rg", (3, 2, n - 1)), ("rm", (3, 2, n))):
        scratch += [(f"{name}_s", dims, None), (f"{name}_r", dims, None)]
    scratch.append(("ring_free", (), "regular"))
    scratch.append(("local_sems", (8 + W,), None))
    results = pl.pallas_call(
        functools.partial(layer_kernel, z, ins, outs, scratch),
        out_shape=[jax.ShapeDtypeStruct(dims, kind) for _, dims, kind in outs],
        in_specs=[spec for _, spec, _ in ins],
        out_specs=[near if name in SMALL else hbm for name, *_ in outs],
        scratch_shapes=[
            pltpu.SemaphoreType.REGULAR if t == "regular" else pltpu.SemaphoreType.DMA(d) if t is None else pltpu.VMEM(d, t)
            for _, d, t in scratch
        ],
        compiler_params=pltpu.CompilerParams(vmem_limit_bytes=LIMIT, collective_id=0, has_side_effects=True),
        name="layer",
    )(*[item for _, _, item in ins])
    parts, _, gtok, *rest = results[:13]
    return finish(z, parts.reshape(W, W * z.seg, D), gtok.reshape(W * z.seg, D), *rest)


def finish_kernel(ways, steps, *refs):
    count = len(refs) // 2
    ins, outs = refs[:count], refs[count:]
    total = functools.reduce(lambda a, b: a + b, [ins[0][n].astype(f32) for n in range(ways)])
    outs[0][...] = total.astype(bf16)
    for src, dst in zip(ins[1:9], outs[1:9], strict=True):
        dst[...] = src[...].astype(f32)

    @pl.when(pl.program_id(0) == steps - 1)
    def _():
        for src, dst in zip(ins[9:11], outs[9:11], strict=True):
            dst[...] = src[0, :]
        outs[11][...] = ins[11][...]


def finish(z, parts, gtok, gate, up, down, gq, gk, gv, gout, gn1, gn2, grt):
    D, W, H = z.width, z.ways, z.hid
    steps = 4
    wide, deep = z.local * D, z.local * H
    args = [parts, gtok, gate.reshape(wide, H), up.reshape(wide, H), down.reshape(deep, D), gq, gk, gv, gout, gn1, gn2, grt]

    def rows(count, cols):
        return pl.BlockSpec((count // steps, cols), lambda i: (i, 0))

    sliced = [rows(W * z.seg, D), rows(wide, H), rows(wide, H), rows(deep, D)] + [rows(D, D)] * 4
    one = pl.BlockSpec((1, D), lambda i: (0, 0))
    flat = pl.BlockSpec((D,), lambda i: (0,))
    router = pl.BlockSpec(grt.shape, lambda i: (0, 0))
    shapes = [((W * z.seg, D), bf16), ((W * z.seg, D), f32), ((wide, H), f32), ((wide, H), f32), ((deep, D), f32)]
    shapes += [((D, D), f32)] * 4 + [((D,), f32)] * 2 + [(grt.shape, f32)]
    out, gtok, gate, up, down, gq, gk, gv, gout, gn1, gn2, grt = pl.pallas_call(
        functools.partial(finish_kernel, W, steps),
        grid=(steps,),
        out_shape=[jax.ShapeDtypeStruct(*s) for s in shapes],
        in_specs=[pl.BlockSpec((W, W * z.seg // steps, D), lambda i: (0, i, 0))] + sliced + [one, one, router],
        out_specs=[rows(W * z.seg, D)] + sliced + [flat, flat, router],
        compiler_params=pltpu.CompilerParams(vmem_limit_bytes=LIMIT),
        name="finish",
    )(*args)
    places = (W, z.seg, D)
    return (out.reshape(places), gtok.reshape(places), gn1, gq, gk, gv, gout, gn2, grt.T,
            gate.reshape(z.local, D, H), up.reshape(z.local, D, H), down.reshape(z.local, H, D))


def solution(mesh):
    split, copied = P("dp", "expert", None), P()
    per_expert = P("expert", None, None)
    return jax.shard_map(
        body,
        mesh=mesh,
        in_specs=(split, P("dp", None), split, split) + (copied,) * 7 + (per_expert,) * 3,
        out_specs=(split, split) + (copied,) * 7 + (per_expert,) * 3,
        check_vma=False,
    )
```
